32 devices in a mesh: src: 4 (over z), shard: 4 (over y, core), slab: 2 (over x).
Axes of the slice: x: 2, y: 2, z: 4, core: 2. Of those that a mesh axis runs over, the one named last changes fastest.
Arguments:
- src_feat: bfloat16 [4, 64, 64, 256], P('src', 'slab', 'shard'), may hold values from -6 to 6
- coords: int32 [4, 2], P('src'), may hold values from 0 to 6
- offsets: int32 [2], P('slab'), may hold values from 0 to 2128
- weights: bfloat16 [4, 2, 9, 512, 128], P('src'), may hold values from -0.09375 to 0.09375
Outputs:
- target_feat: bfloat16 [4, 64, 64, 256], P('src', 'slab', 'shard')
The draws below stay inside these ranges and needn't reach their ends.
All inputs are finite; a program needn't handle non-finite values.
Results may differ from the reference program's by a relative error of at most 0.0047.
Values may be sent and summed in bfloat16 or wider, within the bound.
No kernel may reach another device: no remote copies, remote signals or barrier semaphores. Data moves between devices by JAX's collectives and lax.ppermute only.
A program may use at most 64 MiB of HBM per device.

```python
import math
import jax
import jax.numpy as jnp
from jax import lax

VIEWS = 4
C = 256
GROUPS = 2
ROWS = 32
IMAGE_H = 2160
SLABS = 2
H = 64
W = 64
TARGETS = 4


def touch_ends(array, stream_key, low, high):
    longest = array.shape.index(max(array.shape))
    spots = []
    for shift in (0, 1):
        where = [jax.random.randint(jax.random.fold_in(stream_key, axis), (), 0, length) for axis, length in enumerate(array.shape)]
        where[longest] = (where[longest] + shift) % array.shape[longest]
        spots.append(tuple(where))
    return array.at[spots[0]].set(low).at[spots[1]].set(high)


def steps_of(key, extent, shards, low, top_value):
    def one(dim, blocks):
        draws = jax.random.uniform(jax.random.fold_in(jax.random.fold_in(key, 6), dim), (blocks,), jnp.float32, low / len(shards), top_value / len(shards))
        return jnp.repeat(jnp.exp(draws), extent[dim] // blocks).reshape((-1,) + (1,) * (len(extent) - dim - 1))

    gain = one(*shards[0])
    for cut in shards[1:]:
        gain = gain * one(*cut)
    return gain


def noise(rng, shape, spread, bound, shards=(), kind=jnp.bfloat16):
    entries = spread * jax.random.normal(rng, shape, jnp.float32)
    if shards:
        entries = entries * steps_of(rng, shape, shards, -0.22, 0.18)
    return jnp.clip(entries, -bound, bound).astype(kind)


def setup_inputs(seed: int = 0) -> dict:
    arg_keys = jax.random.split(jax.random.key(seed), 5)
    src_feat = noise(arg_keys[0], (VIEWS, H, W, C), 1.0, 6.0, ((0, 4), (1, 2), (2, 4)))
    coords = touch_ends(jax.random.randint(arg_keys[1], (TARGETS, 2), 0, 7), jax.random.fold_in(arg_keys[1], 1), 0, 6).astype(jnp.int32)
    offsets = jax.random.randint(arg_keys[2], (SLABS,), 0, IMAGE_H - ROWS + 1).astype(jnp.int32)
    weights = noise(arg_keys[3], (TARGETS, GROUPS, 9, VIEWS * C // GROUPS, C // GROUPS), (9 * VIEWS * C // GROUPS) ** -0.5, 0.09375, ((0, 4),))
    return dict(src_feat=src_feat, coords=coords, offsets=offsets, weights=weights)


def encoding(rowpos, chan_count):
    channel_idx = jnp.arange(chan_count, dtype=jnp.int32)
    halves = (channel_idx // 2).astype(jnp.float32)
    frequency = jnp.exp(-math.log(1000.0) * halves / (chan_count / 2))
    phases = (channel_idx % 2).astype(jnp.float32) * (math.pi / 2)
    return jnp.sin(rowpos.astype(jnp.float32)[:, None] * frequency[None, :] + phases[None, :])


def blend_weights(coords):
    vertical = coords[:, 0].astype(jnp.float32) / 6.0
    across = coords[:, 1].astype(jnp.float32) / 6.0
    return jnp.stack([(1.0 - vertical) * (1.0 - across), (1.0 - vertical) * across,
                      vertical * (1.0 - across), vertical * across], axis=1)


def reference(src_feat, coords, offsets, weights):
    rowpos = (offsets[:, None] + jnp.arange(ROWS, dtype=jnp.int32)[None, :]).reshape(-1)
    encoded = encoding(rowpos, C)
    posed = (src_feat.astype(jnp.float32) + encoded[None, :, None, :]).astype(jnp.bfloat16)
    padded = jnp.pad(posed, ((0, 0), (1, 1), (1, 1), (0, 0)))
    height = posed.shape[1]
    img_width = posed.shape[2]
    per_group = VIEWS // GROUPS
    grouped = padded.reshape(GROUPS, per_group, height + 2, img_width + 2, C)
    grouped = grouped.transpose(0, 2, 3, 1, 4).reshape(GROUPS, height + 2, img_width + 2, per_group * C)
    mixing = blend_weights(coords)
    posed_wide = posed.astype(jnp.float32)

    def one_target(packed):
        kernel, mixture = packed
        group_parts = []
        for group_idx in range(GROUPS):
            running = jnp.zeros((height * img_width, C // GROUPS), jnp.float32)
            for tap_index in range(9):
                tap_row = tap_index // 3
                tap_col = tap_index % 3
                window = grouped[group_idx, tap_row:tap_row + height, tap_col:tap_col + img_width, :]
                window = window.reshape(height * img_width, per_group * C)
                running = running + jnp.dot(window, kernel[group_idx, tap_index], preferred_element_type=jnp.float32)
            group_parts.append(running.reshape(height, img_width, C // GROUPS))
        convolved = jnp.concatenate(group_parts, axis=-1)
        blended = jnp.einsum("v,vhwc->hwc", mixture, posed_wide)
        return (blended + jax.nn.silu(convolved)).astype(jnp.bfloat16)

    return lax.map(one_target, (weights, mixing))
```

```python
import functools
import math

import jax
import jax.numpy as jnp
from jax import lax
from jax.experimental import pallas as pl
from jax.experimental.pallas import tpu as pltpu
from jax.sharding import PartitionSpec as P

BF16, F32 = jnp.bfloat16, jnp.float32
VMEM_SPEC = pl.BlockSpec(memory_space=pltpu.VMEM)
SMEM_SPEC = pl.BlockSpec(memory_space=pltpu.SMEM)
LANES = 128
PITCH = 24


def encoding(rowpos, chan_count):
    channel_idx = jnp.arange(chan_count, dtype=jnp.int32)
    halves = (channel_idx // 2).astype(F32)
    frequency = jnp.exp(-math.log(1000.0) * halves / (chan_count / 2))
    phases = (channel_idx % 2).astype(F32) * (math.pi / 2)
    return jnp.sin(rowpos.astype(F32)[:, None] * frequency[None, :] + phases[None, :])


def blend_weights(coords):
    vertical = coords[:, 0].astype(F32) / 6.0
    across = coords[:, 1].astype(F32) / 6.0
    return jnp.stack(
        [
            (1.0 - vertical) * (1.0 - across),
            (1.0 - vertical) * across,
            vertical * (1.0 - across),
            vertical * across,
        ],
        axis=1,
    )


def tiles(chan):
    return [(c, slice(c * LANES, (c + 1) * LANES)) for c in range(chan // LANES)]


def borders_kernel(rows, cols, view, enc, first_col, last_col, edge_rows, wide):
    for h in range(rows):
        block = view[h * cols : (h + 1) * cols, :].astype(F32) + enc[h : h + 1, :]
        for c, lanes in tiles(view.shape[1]):
            wide[c, h * cols : (h + 1) * cols, :] = block[:, lanes]
        if h == 0:
            edge_rows[0:cols, :] = block.astype(BF16)
        if h == rows - 1:
            edge_rows[cols : 2 * cols, :] = block.astype(BF16)
    for c, lanes in tiles(view.shape[1]):
        first_col[:, lanes] = wide[c, pl.ds(0, rows, stride=cols), :].astype(BF16)
        last_col[:, lanes] = wide[c, pl.ds(cols - 1, rows, stride=cols), :].astype(BF16)


def corners(left, right, at):
    picked = [left[at : at + 1, :].astype(F32), right[at : at + 1, :].astype(F32)]
    fill = jnp.zeros((14, left.shape[1]), F32)
    return jnp.concatenate(picked + [fill], axis=0).astype(BF16)


def edges_kernel(rows, cols, pick, edge_rows, left, right, *outs):
    if pick:
        first = lax.axis_index(pick) == 0
        out = outs[0]
        out[0:cols, :] = jnp.where(first, edge_rows[cols : 2 * cols, :], edge_rows[0:cols, :])
        out[cols : cols + 16, :] = jnp.where(
            first, corners(left, right, rows - 1), corners(left, right, 0)
        )
    else:
        top, bottom = outs
        top[0:cols, :] = edge_rows[0:cols, :]
        top[cols : cols + 16, :] = corners(left, right, 0)
        bottom[0:cols, :] = edge_rows[cols : 2 * cols, :]
        bottom[cols : cols + 16, :] = corners(left, right, rows - 1)


def strip_kernel(*refs):
    out, at = refs[-1], 0
    for ref in refs[:-1]:
        out[at : at + ref.shape[0], :] = ref[...]
        at += ref.shape[0]


def unfold(rows, cols, pick, view, enc, strip, wide, windows, base, weight, start):
    chan = view.shape[1]
    extra = cols + 16
    before = strip[2 * rows : 2 * rows + extra, :].astype(F32)
    if pick:
        first = lax.axis_index(pick) == 0
        zero = jnp.zeros_like(before)
        before, after = jnp.where(first, zero, before), jnp.where(first, before, zero)
    else:
        after = strip[2 * rows + extra : 2 * rows + 2 * extra, :].astype(F32)
    for c, lanes in tiles(chan):
        for h, edge in ((0, before), (rows + 1, after)):
            at = h * PITCH + 8
            wide[c, at : at + cols, :] = edge[0:cols, lanes]
            wide[c, at - 1 : at, :] = edge[cols : cols + 1, lanes]
            wide[c, at + cols : at + cols + 1, :] = edge[cols + 1 : cols + 2, lanes]
        left, right = strip[0:rows, lanes].astype(F32), strip[rows : 2 * rows, lanes].astype(F32)
        wide[c, pl.ds(PITCH + 7, rows, stride=PITCH), :] = left
        wide[c, pl.ds(PITCH + 8 + cols, rows, stride=PITCH), :] = right
    for h in range(rows):
        here = slice(h * cols, (h + 1) * cols)
        posed = (view[here, :].astype(F32) + enc[h : h + 1, :]).astype(BF16).astype(F32)
        at = (h + 1) * PITCH + 8
        for c, lanes in tiles(chan):
            wide[c, at : at + cols, :] = posed[:, lanes]
        part = weight * posed
        base[here, :] = part if start else base[here, :] + part
    for h in range(rows + 2):
        at = h * PITCH + 7
        here = slice(h * cols, (h + 1) * cols)
        for b in range(3):
            for c in range(chan // LANES):
                to = b * chan + c * LANES
                windows[here, to : to + LANES] = wide[c, at + b : at + b + cols, :].astype(BF16)


def convolve(pixels, cols, windows, weights, view_index):
    chan = windows.shape[1] // 3
    group = lax.div(view_index, 2)
    at = pl.multiple_of(lax.rem(view_index, 2) * chan, chan)
    total = None
    for a in range(3):
        kernel = jnp.concatenate(
            [weights[group, 3 * a + b, pl.ds(at, chan), :] for b in range(3)], axis=0
        )
        part = jnp.dot(
            windows[a * cols : a * cols + pixels, :], kernel, preferred_element_type=F32
        )
        total = part if total is None else total + part
    return total


def silu(x):
    return x / (1.0 + jnp.exp(-x))


def early_kernel(rows, cols, pick, mixing, own, near, far, enc, strip0, strip1, strip2, weights,
                 base, joined, wide, windows):
    me = lax.axis_index("src")
    pixels = rows * cols
    width = joined.shape[1]
    index = [me, jnp.bitwise_xor(me, 1), jnp.bitwise_xor(me, 2)]
    sums = []
    for i, (view, strip) in enumerate(((own, strip0), (near, strip1), (far, strip2))):
        unfold(rows, cols, pick, view, enc, strip, wide, windows, base, mixing[index[i]], i == 0)
        sums.append(convolve(pixels, cols, windows, weights, index[i]))
    joined[...] = sums[2]
    here = pl.ds(pl.multiple_of(lax.div(me, 2) * width, width), width)
    base[:, here] = base[:, here] + silu(sums[0] + sums[1])


def late_kernel(rows, cols, pick, mixing, last, enc, strip, weights, base_in, joined, out,
                wide, windows, base):
    me = lax.axis_index("src")
    pixels = rows * cols
    width = joined.shape[1]
    index = jnp.bitwise_xor(me, 3)
    base[...] = base_in[...]
    unfold(rows, cols, pick, last, enc, strip, wide, windows, base, mixing[index], False)
    total = joined[...] + convolve(pixels, cols, windows, weights, index)
    here = pl.ds(pl.multiple_of(lax.div(index, 2) * width, width), width)
    base[:, here] = base[:, here] + silu(total)
    out[...] = base[...].astype(BF16)


def shape(rows, chan, dtype=BF16):
    return jax.ShapeDtypeStruct((rows, chan), dtype)


def call(kernel, ins, outs, scratch=(), smem=0, cost=None):
    return pl.pallas_call(
        kernel,
        out_shape=outs,
        in_specs=[SMEM_SPEC] * smem + [VMEM_SPEC] * (len(ins) - smem),
        out_specs=jax.tree.map(lambda _: VMEM_SPEC, outs),
        scratch_shapes=list(scratch),
        compiler_params=pltpu.CompilerParams(vmem_limit_bytes=32 * 1024 * 1024),
        cost_estimate=cost,
    )(*ins)


def local(src_feat, coords, offsets, weights):
    _, rows, cols, chan = src_feat.shape
    pixels = rows * cols
    width = weights.shape[4]
    own = src_feat.reshape(pixels, chan)

    def across(array, k):
        return lax.ppermute(array, "src", [(i, i ^ k) for i in range(4)])

    far = across(own, 2)
    near = across(own, 1)
    rowpos = offsets[0] + jnp.arange(rows, dtype=jnp.int32)
    enc = encoding(rowpos, chan)
    mixing = blend_weights(coords).reshape(4)

    first_col, last_col, edge_rows = call(
        functools.partial(borders_kernel, rows, cols),
        [own, enc],
        [shape(rows, chan), shape(rows, chan), shape(2 * cols, chan)],
        [pltpu.VMEM((chan // LANES, pixels, LANES), F32)],
    )
    shards, slabs = lax.axis_size("shard"), lax.axis_size("slab")
    up = [(i, i + 1) for i in range(shards - 1)]
    left = lax.ppermute(last_col, "shard", up)
    right = lax.ppermute(first_col, "shard", [(j, i) for i, j in up])
    pick = "slab" if slabs == 2 else None
    edge = shape(cols + 16, chan)
    edges = call(
        functools.partial(edges_kernel, rows, cols, pick),
        [edge_rows, left, right],
        [edge] if pick else [edge, edge],
    )
    if pick:
        beyond = [lax.ppermute(edges[0], "slab", [(0, 1), (1, 0)])]
    else:
        up = [(i, i + 1) for i in range(slabs - 1)]
        beyond = [
            lax.ppermute(edges[1], "slab", up),
            lax.ppermute(edges[0], "slab", [(j, i) for i, j in up]),
        ]
    strip_rows = 2 * rows + len(beyond) * (cols + 16)
    strip = call(strip_kernel, [left, right, *beyond], [shape(strip_rows, chan)])[0]
    strips = [strip] + [across(strip, k) for k in (1, 2, 3)]
    last = across(far, 1)

    scratch = [
        pltpu.VMEM((chan // LANES, (rows + 2) * PITCH + 8, LANES), F32),
        pltpu.VMEM(((rows + 2) * cols, 3 * chan), BF16),
    ]
    base, joined = call(
        functools.partial(early_kernel, rows, cols, pick),
        [mixing, own, near, far, enc, *strips[:3], weights[0]],
        [shape(pixels, chan, F32), shape(pixels, width, F32)],
        scratch,
        smem=1,
    )
    out = call(
        functools.partial(late_kernel, rows, cols, pick),
        [mixing, last, enc, strips[3], weights[0], base, joined],
        [shape(pixels, chan)],
        scratch + [pltpu.VMEM((pixels, chan), F32)],
        smem=1,
    )[0]
    return out.reshape(1, rows, cols, chan)


def solution(mesh):
    in_specs = (
        P("src", "slab", "shard", None),
        P("src", None),
        P("slab"),
        P("src", None, None, None, None),
    )
    out_specs = P("src", "slab", "shard", None)
    return jax.shard_map(local, mesh=mesh, in_specs=in_specs, out_specs=out_specs, check_vma=False)
```

```python
import functools
import math

import jax
import jax.numpy as jnp
from jax import lax
from jax.experimental import pallas as pl
from jax.experimental.pallas import tpu as pltpu
from jax.sharding import PartitionSpec as P

BF16, F32 = jnp.bfloat16, jnp.float32
VMEM_SPEC = pl.BlockSpec(memory_space=pltpu.VMEM)
SMEM_SPEC = pl.BlockSpec(memory_space=pltpu.SMEM)
LANES = 128
PITCH = 24


def encoding(rowpos, chan_count):
    channel_idx = jnp.arange(chan_count, dtype=jnp.int32)
    halves = (channel_idx // 2).astype(F32)
    frequency = jnp.exp(-math.log(1000.0) * halves / (chan_count / 2))
    phases = (channel_idx % 2).astype(F32) * (math.pi / 2)
    return jnp.sin(rowpos.astype(F32)[:, None] * frequency[None, :] + phases[None, :])


def blend_weight(coords, view_index):
    vertical = coords[0, 0].astype(F32) / 6.0
    across = coords[0, 1].astype(F32) / 6.0
    low, left = lax.div(view_index, 2) == 0, lax.rem(view_index, 2) == 0
    return jnp.where(low, 1.0 - vertical, vertical) * jnp.where(left, 1.0 - across, across)


def tiles(chan):
    return [(c, slice(c * LANES, (c + 1) * LANES)) for c in range(chan // LANES)]


def borders_kernel(rows, cols, view, enc, col_a, col_b, edge_rows, wide):
    even = lax.rem(lax.axis_index("shard"), 2) == 0
    for h in range(rows):
        block = view[h * cols : (h + 1) * cols, :].astype(F32) + enc[h : h + 1, :]
        for c, lanes in tiles(view.shape[1]):
            wide[c, h * cols : (h + 1) * cols, :] = block[:, lanes]
        if h == 0:
            edge_rows[0:cols, :] = block.astype(BF16)
        if h == rows - 1:
            edge_rows[cols : 2 * cols, :] = block.astype(BF16)
    for c, lanes in tiles(view.shape[1]):
        first = wide[c, pl.ds(0, rows, stride=cols), :]
        last = wide[c, pl.ds(cols - 1, rows, stride=cols), :]
        col_a[:, lanes] = jnp.where(even, last, first).astype(BF16)
        col_b[:, lanes] = jnp.where(even, first, last).astype(BF16)


def sides(got_a, got_b):
    even = lax.rem(lax.axis_index("shard"), 2) == 0
    a, b = got_a[...].astype(F32), got_b[...].astype(F32)
    return jnp.where(even, b, a), jnp.where(even, a, b)


def corners(left, right, at):
    fill = jnp.zeros((14, left.shape[1]), F32)
    return jnp.concatenate([left[at : at + 1], right[at : at + 1], fill], axis=0)


def edges_kernel(rows, cols, pick, edge_rows, got_a, got_b, *outs):
    left, right = sides(got_a, got_b)
    top = jnp.concatenate([edge_rows[0:cols, :].astype(F32), corners(left, right, 0)], axis=0)
    bottom = jnp.concatenate(
        [edge_rows[cols : 2 * cols, :].astype(F32), corners(left, right, rows - 1)], axis=0
    )
    if pick:
        outs[0][...] = jnp.where(lax.axis_index(pick) == 0, bottom, top).astype(BF16)
    else:
        outs[0][...] = top.astype(BF16)
        outs[1][...] = bottom.astype(BF16)


def strip_kernel(rows, got_a, got_b, *refs):
    out = refs[-1]
    left, right = sides(got_a, got_b)
    out[0:rows, :] = left.astype(BF16)
    out[rows : 2 * rows, :] = right.astype(BF16)
    at = 2 * rows
    for ref in refs[:-1]:
        out[at : at + ref.shape[0], :] = ref[...]
        at += ref.shape[0]


def join_kernel(panel, strip, out):
    out[0 : panel.shape[0], :] = panel[...]
    out[panel.shape[0] :, :] = strip[...]


def unfold(rows, cols, pick, view, enc, strip, wide, windows, base, weight, start):
    chan = view.shape[1]
    extra = cols + 16
    before = strip[2 * rows : 2 * rows + extra, :].astype(F32)
    if pick:
        first = lax.axis_index(pick) == 0
        zero = jnp.zeros_like(before)
        before, after = jnp.where(first, zero, before), jnp.where(first, before, zero)
    else:
        after = strip[2 * rows + extra : 2 * rows + 2 * extra, :].astype(F32)
    for c, lanes in tiles(chan):
        for h, edge in ((0, before), (rows + 1, after)):
            at = h * PITCH + 8
            wide[c, at : at + cols, :] = edge[0:cols, lanes]
            wide[c, at - 1 : at, :] = edge[cols : cols + 1, lanes]
            wide[c, at + cols : at + cols + 1, :] = edge[cols + 1 : cols + 2, lanes]
        left, right = strip[0:rows, lanes].astype(F32), strip[rows : 2 * rows, lanes].astype(F32)
        wide[c, pl.ds(PITCH + 7, rows, stride=PITCH), :] = left
        wide[c, pl.ds(PITCH + 8 + cols, rows, stride=PITCH), :] = right
    for h in range(rows):
        here = slice(h * cols, (h + 1) * cols)
        posed = (view[here, :].astype(F32) + enc[h : h + 1, :]).astype(BF16).astype(F32)
        at = (h + 1) * PITCH + 8
        for c, lanes in tiles(chan):
            wide[c, at : at + cols, :] = posed[:, lanes]
        part = weight * posed
        base[here, :] = part if start else base[here, :] + part
    for h in range(rows + 2):
        at = h * PITCH + 7
        here = slice(h * cols, (h + 1) * cols)
        for b in range(3):
            for c in range(chan // LANES):
                to = b * chan + c * LANES
                windows[here, to : to + LANES] = wide[c, at + b : at + b + cols, :].astype(BF16)


def convolve(pixels, cols, windows, weights, view_index):
    chan = windows.shape[1] // 3
    group = lax.div(view_index, 2)
    at = pl.multiple_of(lax.rem(view_index, 2) * chan, chan)
    total = None
    for a in range(3):
        kernel = jnp.concatenate(
            [weights[group, 3 * a + b, pl.ds(at, chan), :] for b in range(3)], axis=0
        )
        part = jnp.dot(
            windows[a * cols : a * cols + pixels, :], kernel, preferred_element_type=F32
        )
        total = part if total is None else total + part
    return total


def silu(x):
    return x / (1.0 + jnp.exp(-x))


def early_kernel(rows, cols, pick, coords, own, near, far, enc, strip0, strip1, strip2, weights,
                 base, joined, last_weight, wide, windows):
    me = lax.axis_index("src")
    pixels = rows * cols
    width = joined.shape[1]
    index = [me, jnp.bitwise_xor(me, 1), jnp.bitwise_xor(me, 2)]
    sums = []
    for i, (view, strip) in enumerate(((own, strip0), (near, strip1), (far, strip2))):
        weight = blend_weight(coords, index[i])
        unfold(rows, cols, pick, view, enc, strip, wide, windows, base, weight, i == 0)
        sums.append(convolve(pixels, cols, windows, weights, index[i]))
    joined[...] = sums[2]
    here = pl.ds(pl.multiple_of(lax.div(me, 2) * width, width), width)
    base[:, here] = base[:, here] + silu(sums[0] + sums[1])
    weight = blend_weight(coords, jnp.bitwise_xor(me, 3))
    last_weight[...] = jnp.full(last_weight.shape, weight, F32)


def late_kernel(rows, cols, pick, last, enc, weights, base_in, joined, last_weight, out,
                wide, windows, base):
    me = lax.axis_index("src")
    pixels = rows * cols
    width = joined.shape[1]
    index = jnp.bitwise_xor(me, 3)
    base[...] = base_in[...]
    unfold(rows, cols, pick, last.at[0:pixels], enc, last.at[pixels:], wide, windows, base,
           last_weight[0:1, :], False)
    total = joined[...] + convolve(pixels, cols, windows, weights, index)
    here = pl.ds(pl.multiple_of(lax.div(index, 2) * width, width), width)
    base[:, here] = base[:, here] + silu(total)
    out[...] = base[...].astype(BF16)


def shape(rows, chan, dtype=BF16):
    return jax.ShapeDtypeStruct((rows, chan), dtype)


def call(kernel, ins, outs, scratch=(), smem=0, cost=None):
    return pl.pallas_call(
        kernel,
        out_shape=outs,
        in_specs=[SMEM_SPEC] * smem + [VMEM_SPEC] * (len(ins) - smem),
        out_specs=jax.tree.map(lambda _: VMEM_SPEC, outs),
        scratch_shapes=list(scratch),
        compiler_params=pltpu.CompilerParams(vmem_limit_bytes=32 * 1024 * 1024),
        cost_estimate=cost,
    )(*ins)


def local(src_feat, coords, offsets, weights):
    _, rows, cols, chan = src_feat.shape
    pixels = rows * cols
    width = weights.shape[4]
    own = src_feat.reshape(pixels, chan)

    def across(array, k):
        return lax.ppermute(array, "src", [(i, i ^ k) for i in range(4)])

    far = across(own, 2)
    near = across(own, 1)
    rowpos = offsets[0] + jnp.arange(rows, dtype=jnp.int32)
    enc = encoding(rowpos, chan)

    column = shape(rows, chan)
    col_a, col_b, edge_rows = call(
        functools.partial(borders_kernel, rows, cols),
        [own, enc],
        [column, column, shape(2 * cols, chan)],
        [pltpu.VMEM((chan // LANES, pixels, LANES), F32)],
    )
    shards, slabs = lax.axis_size("shard"), lax.axis_size("slab")

    def swap(array, first):
        pairs = [(i, i + 1) for i in range(first, shards - 1, 2)]
        return lax.ppermute(array, "shard", pairs + [(j, i) for i, j in pairs])

    got_b, got_a = swap(col_b, 1), swap(col_a, 0)
    pick = "slab" if slabs == 2 else None
    edge = shape(cols + 16, chan)
    edges = call(
        functools.partial(edges_kernel, rows, cols, pick),
        [edge_rows, got_a, got_b],
        [edge] if pick else [edge, edge],
    )
    if pick:
        beyond = [lax.ppermute(edges[0], "slab", [(0, 1), (1, 0)])]
    else:
        up = [(i, i + 1) for i in range(slabs - 1)]
        beyond = [
            lax.ppermute(edges[1], "slab", up),
            lax.ppermute(edges[0], "slab", [(j, i) for i, j in up]),
        ]
    strip_rows = 2 * rows + len(beyond) * (cols + 16)
    strip = call(
        functools.partial(strip_kernel, rows), [got_a, got_b, *beyond], [shape(strip_rows, chan)]
    )[0]
    strip_far, strip_near = across(strip, 2), across(strip, 1)
    far, near, strip_far, strip_near = lax.optimization_barrier((far, near, strip_far, strip_near))
    last = across(call(join_kernel, [far, strip_far], [shape(pixels + strip_rows, chan)])[0], 1)

    scratch = [
        pltpu.VMEM((chan // LANES, (rows + 2) * PITCH + 8, LANES), F32),
        pltpu.VMEM(((rows + 2) * cols, 3 * chan), BF16),
    ]
    base, joined, last_weight = call(
        functools.partial(early_kernel, rows, cols, pick),
        [coords, own, near, far, enc, strip, strip_near, strip_far, weights[0]],
        [shape(pixels, chan, F32), shape(pixels, width, F32), shape(8, chan, F32)],
        scratch,
        smem=1,
    )
    out = call(
        functools.partial(late_kernel, rows, cols, pick),
        [last, enc, weights[0], base, joined, last_weight],
        [shape(pixels, chan)],
        scratch + [pltpu.VMEM((pixels, chan), F32)],
    )[0]
    return out.reshape(1, rows, cols, chan)


def solution(mesh):
    in_specs = (
        P("src", "slab", "shard", None),
        P("src", None),
        P("slab"),
        P("src", None, None, None, None),
    )
    out_specs = P("src", "slab", "shard", None)
    return jax.shard_map(local, mesh=mesh, in_specs=in_specs, out_specs=out_specs, check_vma=False)
```

```python
import functools
import math

import jax
import jax.numpy as jnp
from jax import lax
from jax.experimental import pallas as pl
from jax.experimental.pallas import tpu as pltpu
from jax.sharding import PartitionSpec as P

BF16, F32 = jnp.bfloat16, jnp.float32
VMEM_SPEC = pl.BlockSpec(memory_space=pltpu.VMEM)
LANES = 128
PITCH = 24


def encoding(rowpos, chan_count):
    channel_idx = jnp.arange(chan_count, dtype=jnp.int32)
    halves = (channel_idx // 2).astype(F32)
    frequency = jnp.exp(-math.log(1000.0) * halves / (chan_count / 2))
    phases = (channel_idx % 2).astype(F32) * (math.pi / 2)
    return jnp.sin(rowpos.astype(F32)[:, None] * frequency[None, :] + phases[None, :])


def blend_weight(coords, view_index):
    vertical, across = coords[0:1, :] / 6.0, coords[1:2, :] / 6.0
    low, left = lax.div(view_index, 2) == 0, lax.rem(view_index, 2) == 0
    return jnp.where(low, 1.0 - vertical, vertical) * jnp.where(left, 1.0 - across, across)


def tiles(chan):
    return [(c, slice(c * LANES, (c + 1) * LANES)) for c in range(chan // LANES)]


def columns_kernel(rows, cols, view, col_a, col_b, edge_rows, panel, wide):
    even = lax.rem(lax.axis_index("shard"), 2) == 0
    for c, lanes in tiles(view.shape[1]):
        wide[c] = view[:, lanes].astype(F32)
        first = wide[c, pl.ds(0, rows, stride=cols), :]
        last = wide[c, pl.ds(cols - 1, rows, stride=cols), :]
        col_a[:, lanes] = jnp.where(even, last, first).astype(BF16)
        col_b[:, lanes] = jnp.where(even, first, last).astype(BF16)
    edge_rows[0:cols, :] = view[0:cols, :]
    edge_rows[cols : 2 * cols, :] = view[(rows - 1) * cols :, :]
    panel[...] = view[...]


def sides(shards, got_a, got_b, enc):
    me = lax.axis_index("shard")
    even = lax.rem(me, 2) == 0
    a, b = got_a[...].astype(F32) + enc[...], got_b[...].astype(F32) + enc[...]
    left = jnp.where(me > 0, jnp.where(even, b, a), 0.0)
    right = jnp.where(me < shards - 1, jnp.where(even, a, b), 0.0)
    return left, right


def corners(left, right, at):
    fill = jnp.zeros((14, left.shape[1]), F32)
    return jnp.concatenate([left[at : at + 1], right[at : at + 1], fill], axis=0)


def edges_kernel(rows, cols, shards, pick, edge_rows, got_a, got_b, enc, *outs):
    left, right = sides(shards, got_a, got_b, enc)
    lines = []
    for i, h in ((0, 0), (1, rows - 1)):
        row = edge_rows[i * cols : (i + 1) * cols, :].astype(F32) + enc[h : h + 1, :]
        lines.append(jnp.concatenate([row, corners(left, right, h)], axis=0))
    if pick:
        outs[0][...] = jnp.where(lax.axis_index(pick) == 0, lines[1], lines[0]).astype(BF16)
    else:
        outs[0][...] = lines[0].astype(BF16)
        outs[1][...] = lines[1].astype(BF16)


def strip_kernel(rows, shards, got_a, got_b, enc, *refs):
    out = refs[-1]
    left, right = sides(shards, got_a, got_b, enc)
    out[0:rows, :] = left.astype(BF16)
    out[rows : 2 * rows, :] = right.astype(BF16)
    at = 2 * rows
    for ref in refs[:-1]:
        out[at : at + ref.shape[0], :] = ref[...]
        at += ref.shape[0]


def unfold(rows, cols, pick, view, enc, strip, wide, windows, base, weight, start):
    chan = view.shape[1]
    extra = cols + 16
    before = strip[2 * rows : 2 * rows + extra, :].astype(F32)
    if pick:
        first = lax.axis_index(pick) == 0
        zero = jnp.zeros_like(before)
        before, after = jnp.where(first, zero, before), jnp.where(first, before, zero)
    else:
        after = strip[2 * rows + extra : 2 * rows + 2 * extra, :].astype(F32)
    for c, lanes in tiles(chan):
        for h, edge in ((0, before), (rows + 1, after)):
            at = h * PITCH + 8
            wide[c, at : at + cols, :] = edge[0:cols, lanes]
            wide[c, at - 1 : at, :] = edge[cols : cols + 1, lanes]
            wide[c, at + cols : at + cols + 1, :] = edge[cols + 1 : cols + 2, lanes]
        left, right = strip[0:rows, lanes].astype(F32), strip[rows : 2 * rows, lanes].astype(F32)
        wide[c, pl.ds(PITCH + 7, rows, stride=PITCH), :] = left
        wide[c, pl.ds(PITCH + 8 + cols, rows, stride=PITCH), :] = right
    for h in range(rows):
        here = slice(h * cols, (h + 1) * cols)
        posed = (view[here, :].astype(F32) + enc[h : h + 1, :]).astype(BF16).astype(F32)
        at = (h + 1) * PITCH + 8
        for c, lanes in tiles(chan):
            wide[c, at : at + cols, :] = posed[:, lanes]
        part = weight * posed
        base[here, :] = part if start else base[here, :] + part
    for h in range(rows + 2):
        at = h * PITCH + 7
        here = slice(h * cols, (h + 1) * cols)
        for b in range(3):
            for c in range(chan // LANES):
                to = b * chan + c * LANES
                windows[here, to : to + LANES] = wide[c, at + b : at + b + cols, :].astype(BF16)


def convolve(pixels, cols, windows, weights, view_index):
    chan = windows.shape[1] // 3
    group = lax.div(view_index, 2)
    at = pl.multiple_of(lax.rem(view_index, 2) * chan, chan)
    total = None
    for a in range(3):
        kernel = jnp.concatenate(
            [weights[group, 3 * a + b, pl.ds(at, chan), :] for b in range(3)], axis=0
        )
        part = jnp.dot(
            windows[a * cols : a * cols + pixels, :], kernel, preferred_element_type=F32
        )
        total = part if total is None else total + part
    return total


def silu(x):
    return x / (1.0 + jnp.exp(-x))


def own_kernel(rows, cols, pick, coords, own, enc, strip, weights, base, joined, wide, windows):
    me = lax.axis_index("src")
    unfold(rows, cols, pick, own, enc, strip, wide, windows, base, blend_weight(coords, me), True)
    joined[...] = convolve(rows * cols, cols, windows, weights, me)


def middle_kernel(rows, cols, pick, coords, near, far, enc, strip1, strip2, weights, base_in,
                  joined_in, base, joined, wide, windows):
    me = lax.axis_index("src")
    pixels = rows * cols
    width = joined.shape[1]
    base[...] = base_in[...]
    sums = []
    for k, view, strip in ((1, near, strip1), (2, far, strip2)):
        index = jnp.bitwise_xor(me, k)
        weight = blend_weight(coords, index)
        unfold(rows, cols, pick, view, enc, strip, wide, windows, base, weight, False)
        sums.append(convolve(pixels, cols, windows, weights, index))
    joined[...] = sums[1]
    here = pl.ds(pl.multiple_of(lax.div(me, 2) * width, width), width)
    base[:, here] = base[:, here] + silu(joined_in[...] + sums[0])


def late_kernel(rows, cols, pick, coords, last, enc, strip, weights, base_in, joined, out,
                wide, windows, base):
    me = lax.axis_index("src")
    pixels = rows * cols
    width = joined.shape[1]
    index = jnp.bitwise_xor(me, 3)
    base[...] = base_in[...]
    weight = blend_weight(coords, index)
    unfold(rows, cols, pick, last, enc, strip, wide, windows, base, weight, False)
    total = joined[...] + convolve(pixels, cols, windows, weights, index)
    here = pl.ds(pl.multiple_of(lax.div(index, 2) * width, width), width)
    base[:, here] = base[:, here] + silu(total)
    out[...] = base[...].astype(BF16)


def shape(rows, chan, dtype=BF16):
    return jax.ShapeDtypeStruct((rows, chan), dtype)


def call(kernel, ins, outs, scratch=(), cost=None):
    return pl.pallas_call(
        kernel,
        out_shape=outs,
        in_specs=[VMEM_SPEC] * len(ins),
        out_specs=jax.tree.map(lambda _: VMEM_SPEC, outs),
        scratch_shapes=list(scratch),
        compiler_params=pltpu.CompilerParams(vmem_limit_bytes=32 * 1024 * 1024),
        cost_estimate=cost,
    )(*ins)


def local(src_feat, coords, offsets, weights):
    _, rows, cols, chan = src_feat.shape
    pixels = rows * cols
    width = weights.shape[4]
    own = src_feat.reshape(pixels, chan)

    def across(array, k):
        return lax.ppermute(array, "src", [(i, i ^ k) for i in range(4)])

    far = across(own, 2)
    near = across(own, 1)
    rowpos = offsets[0] + jnp.arange(rows, dtype=jnp.int32)
    enc = encoding(rowpos, chan)

    column = shape(rows, chan)
    col_a, col_b, edge_rows, panel = call(
        functools.partial(columns_kernel, rows, cols),
        [own],
        [column, column, shape(2 * cols, chan), shape(pixels, chan)],
        [pltpu.VMEM((chan // LANES, pixels, LANES), F32)],
    )
    place = jnp.broadcast_to(coords.astype(F32).reshape(2, 1), (2, chan))
    shards, slabs = lax.axis_size("shard"), lax.axis_size("slab")

    def swap(array, first):
        pairs = [(i, i + 1) for i in range(first, shards - 1, 2)]
        return lax.ppermute(array, "shard", pairs + [(j, i) for i, j in pairs])

    got_b, got_a = swap(col_b, 1), swap(col_a, 0)
    pick = "slab" if slabs == 2 else None
    edge = shape(cols + 16, chan)
    edges = call(
        functools.partial(edges_kernel, rows, cols, shards, pick),
        [edge_rows, got_a, got_b, enc],
        [edge] if pick else [edge, edge],
    )
    if pick:
        beyond = [lax.ppermute(edges[0], "slab", [(0, 1), (1, 0)])]
    else:
        up = [(i, i + 1) for i in range(slabs - 1)]
        beyond = [
            lax.ppermute(edges[1], "slab", up),
            lax.ppermute(edges[0], "slab", [(j, i) for i, j in up]),
        ]
    strip_rows = 2 * rows + len(beyond) * (cols + 16)
    strip = call(
        functools.partial(strip_kernel, rows, shards),
        [got_a, got_b, enc, *beyond],
        [shape(strip_rows, chan)],
    )[0]
    strip_near, strip_far = across(strip, 1), across(strip, 2)
    far, panel = lax.optimization_barrier((far, panel))
    last = across(far, 1)

    scratch = [
        pltpu.VMEM((chan // LANES, (rows + 2) * PITCH + 8, LANES), F32),
        pltpu.VMEM(((rows + 2) * cols, 3 * chan), BF16),
    ]
    sums = [shape(pixels, chan, F32), shape(pixels, width, F32)]
    cost = pl.CostEstimate(flops=5_000_000_000, bytes_accessed=4_000_000, transcendentals=0)
    base, joined = call(
        functools.partial(own_kernel, rows, cols, pick),
        [place, panel, enc, strip, weights[0]],
        sums,
        scratch,
        cost=cost,
    )
    strip_far, base = lax.optimization_barrier((strip_far, base))
    strip_last = across(strip_far, 1)
    base, joined = call(
        functools.partial(middle_kernel, rows, cols, pick),
        [place, near, far, enc, strip_near, strip_far, weights[0], base, joined],
        sums,
        scratch,
        cost=pl.CostEstimate(flops=0, bytes_accessed=0, transcendentals=0),
    )
    out = call(
        functools.partial(late_kernel, rows, cols, pick),
        [place, last, enc, strip_last, weights[0], base, joined],
        [shape(pixels, chan)],
        scratch + [pltpu.VMEM((pixels, chan), F32)],
    )[0]
    return out.reshape(1, rows, cols, chan)


def solution(mesh):
    in_specs = (
        P("src", "slab", "shard", None),
        P("src", None),
        P("slab"),
        P("src", None, None, None, None),
    )
    out_specs = P("src", "slab", "shard", None)
    return jax.shard_map(local, mesh=mesh, in_specs=in_specs, out_specs=out_specs, check_vma=False)
```

```python
import functools
import math

import jax
import jax.numpy as jnp
from jax import lax
from jax.experimental import pallas as pl
from jax.experimental.pallas import tpu as pltpu
from jax.sharding import PartitionSpec as P

BF16, F32 = jnp.bfloat16, jnp.float32
VMEM_SPEC = pl.BlockSpec(memory_space=pltpu.VMEM)
LANES = 128
PITCH = 24


def encoding(rowpos, chan_count):
    channel_idx = jnp.arange(chan_count, dtype=jnp.int32)
    halves = (channel_idx // 2).astype(F32)
    frequency = jnp.exp(-math.log(1000.0) * halves / (chan_count / 2))
    phases = (channel_idx % 2).astype(F32) * (math.pi / 2)
    return jnp.sin(rowpos.astype(F32)[:, None] * frequency[None, :] + phases[None, :])


def blend_weight(coords, view_index):
    vertical, across = coords[0:1, :] / 6.0, coords[1:2, :] / 6.0
    low, left = lax.div(view_index, 2) == 0, lax.rem(view_index, 2) == 0
    return jnp.where(low, 1.0 - vertical, vertical) * jnp.where(left, 1.0 - across, across)


def tiles(chan):
    return [(c, slice(c * LANES, (c + 1) * LANES)) for c in range(chan // LANES)]


def column(rows, cols, view, wide, pick_last):
    for c, lanes in tiles(view.shape[1]):
        wide[c] = view[:, lanes].astype(F32)
        first = wide[c, pl.ds(0, rows, stride=cols), :]
        last = wide[c, pl.ds(cols - 1, rows, stride=cols), :]
        yield lanes, jnp.where(pick_last, last, first), jnp.where(pick_last, first, last)


def columns_kernel(rows, cols, view, col_a, col_b, edge_rows, panel, wide):
    even = lax.rem(lax.axis_index("shard"), 2) == 0
    for lanes, a, b in column(rows, cols, view, wide, even):
        col_a[:, lanes] = a.astype(BF16)
        col_b[:, lanes] = b.astype(BF16)
    edge_rows[0:cols, :] = view[0:cols, :]
    edge_rows[cols : 2 * cols, :] = view[(rows - 1) * cols :, :]
    panel[...] = view[...]


def inner_kernel(rows, cols, near, far, cols_a, wide):
    even = lax.rem(lax.axis_index("shard"), 2) == 0
    for i, view in enumerate((near, far)):
        for lanes, a, _ in column(rows, cols, view, wide, even):
            cols_a[i * rows : (i + 1) * rows, lanes] = a.astype(BF16)


def pose(shards, raw, enc, is_a):
    me = lax.axis_index("shard")
    is_left = (lax.rem(me, 2) == 0) != is_a
    inside = jnp.where(is_left, me > 0, me < shards - 1)
    return jnp.where(inside, raw[...].astype(F32) + enc[...], 0.0)


def sides(a, b):
    even = lax.rem(lax.axis_index("shard"), 2) == 0
    return jnp.where(even, b, a), jnp.where(even, a, b)


def corners(left, right, at):
    fill = jnp.zeros((14, left.shape[1]), F32)
    return jnp.concatenate([left[at : at + 1], right[at : at + 1], fill], axis=0)


def edges_kernel(rows, cols, shards, pick, edge_rows, got_a, got_b, enc, *outs):
    left, right = sides(pose(shards, got_a, enc, True), pose(shards, got_b, enc, False))
    lines = []
    for i, h in ((0, 0), (1, rows - 1)):
        row = edge_rows[i * cols : (i + 1) * cols, :].astype(F32) + enc[h : h + 1, :]
        lines.append(jnp.concatenate([row, corners(left, right, h)], axis=0))
    if pick:
        outs[0][...] = jnp.where(lax.axis_index(pick) == 0, lines[1], lines[0]).astype(BF16)
    else:
        outs[0][...] = lines[0].astype(BF16)
        outs[1][...] = lines[1].astype(BF16)


def strip_kernel(rows, shards, got_a, got_b, enc, *refs):
    out, at = refs[-1], rows
    out[0:rows, :] = pose(shards, got_b, enc, False).astype(BF16)
    for ref in refs[:-1]:
        out[at : at + ref.shape[0], :] = ref[...]
        at += ref.shape[0]


def relay_kernel(rows, strip, cols_a, out):
    size = strip.shape[0]
    out[0:size, :] = strip[...]
    out[size:, :] = cols_a[rows:, :]


def unfold(rows, cols, shards, pick, view, enc, strip, raw_a, wide, windows, base, weight, start):
    chan = view.shape[1]
    extra = cols + 16
    size = extra if pick else 2 * extra
    lines = strip[rows : rows + size, :].astype(F32)
    if pick:
        first = lax.axis_index(pick) == 0
        zero = jnp.zeros_like(lines)
        before, after = jnp.where(first, zero, lines), jnp.where(first, lines, zero)
    else:
        before, after = lines[0:extra], lines[extra:]
    posed_a = pose(shards, raw_a, enc, True).astype(BF16).astype(F32)
    left_col, right_col = sides(posed_a, strip[0:rows, :].astype(F32))
    for c, lanes in tiles(chan):
        for h, edge in ((0, before), (rows + 1, after)):
            at = h * PITCH + 8
            wide[c, at : at + cols, :] = edge[0:cols, lanes]
            wide[c, at - 1 : at, :] = edge[cols : cols + 1, lanes]
            wide[c, at + cols : at + cols + 1, :] = edge[cols + 1 : cols + 2, lanes]
        wide[c, pl.ds(PITCH + 7, rows, stride=PITCH), :] = left_col[:, lanes]
        wide[c, pl.ds(PITCH + 8 + cols, rows, stride=PITCH), :] = right_col[:, lanes]
    for h in range(rows):
        here = slice(h * cols, (h + 1) * cols)
        posed = (view[here, :].astype(F32) + enc[h : h + 1, :]).astype(BF16).astype(F32)
        at = (h + 1) * PITCH + 8
        for c, lanes in tiles(chan):
            wide[c, at : at + cols, :] = posed[:, lanes]
        part = weight * posed
        base[here, :] = part if start else base[here, :] + part
    for h in range(rows + 2):
        at = h * PITCH + 7
        here = slice(h * cols, (h + 1) * cols)
        for b in range(3):
            for c in range(chan // LANES):
                to = b * chan + c * LANES
                windows[here, to : to + LANES] = wide[c, at + b : at + b + cols, :].astype(BF16)


def convolve(pixels, cols, windows, weights, view_index):
    chan = windows.shape[1] // 3
    group = lax.div(view_index, 2)
    at = pl.multiple_of(lax.rem(view_index, 2) * chan, chan)
    width = weights.shape[3]
    kernel = jnp.concatenate(
        [
            jnp.concatenate(
                [weights[group, 3 * a + b, pl.ds(at, chan), :] for b in range(3)], axis=0
            )
            for a in range(3)
        ],
        axis=1,
    )
    taps = jnp.dot(windows[...], kernel, preferred_element_type=F32)
    return (
        taps[0:pixels, 0:width]
        + taps[cols : cols + pixels, width : 2 * width]
        + taps[2 * cols : 2 * cols + pixels, 2 * width :]
    )


def silu(x):
    return x / (1.0 + jnp.exp(-x))


def own_kernel(rows, cols, shards, pick, coords, own, enc, strip, got_a, weights, base, joined, wide,
               windows):
    me = lax.axis_index("src")
    weight = blend_weight(coords, me)
    unfold(rows, cols, shards, pick, own, enc, strip, got_a, wide, windows, base, weight, True)
    joined[...] = convolve(rows * cols, cols, windows, weights, me)


def middle_kernel(rows, cols, shards, pick, coords, near, far, enc, near_strip, far_strip, cols_a,
                  weights, base_in, joined_in, base, joined, wide, windows):
    me = lax.axis_index("src")
    pixels = rows * cols
    width = joined.shape[1]
    base[...] = base_in[...]
    sums = []
    views = (
        (1, near, near_strip, cols_a.at[0:rows]),
        (2, far, far_strip, cols_a.at[rows : 2 * rows]),
    )
    for k, view, strip, raw_a in views:
        index = jnp.bitwise_xor(me, k)
        weight = blend_weight(coords, index)
        unfold(rows, cols, shards, pick, view, enc, strip, raw_a, wide, windows, base, weight, False)
        sums.append(convolve(pixels, cols, windows, weights, index))
    joined[...] = sums[1]
    here = pl.ds(pl.multiple_of(lax.div(me, 2) * width, width), width)
    base[:, here] = base[:, here] + silu(joined_in[...] + sums[0])


def late_kernel(rows, cols, shards, pick, coords, last, enc, strip, weights, base_in, joined, out, wide,
                windows, base):
    me = lax.axis_index("src")
    pixels = rows * cols
    width = joined.shape[1]
    index = jnp.bitwise_xor(me, 3)
    base[...] = base_in[...]
    weight = blend_weight(coords, index)
    size = strip.shape[0] - rows
    raw_a = strip.at[size:]
    unfold(rows, cols, shards, pick, last, enc, strip.at[0:size], raw_a, wide, windows, base, weight, False)
    total = joined[...] + convolve(pixels, cols, windows, weights, index)
    here = pl.ds(pl.multiple_of(lax.div(index, 2) * width, width), width)
    base[:, here] = base[:, here] + silu(total)
    out[...] = base[...].astype(BF16)


def shape(rows, chan, dtype=BF16):
    return jax.ShapeDtypeStruct((rows, chan), dtype)


def call(kernel, ins, outs, scratch=(), cost=None):
    return pl.pallas_call(
        kernel,
        out_shape=outs,
        in_specs=[VMEM_SPEC] * len(ins),
        out_specs=jax.tree.map(lambda _: VMEM_SPEC, outs),
        scratch_shapes=list(scratch),
        compiler_params=pltpu.CompilerParams(vmem_limit_bytes=32 * 1024 * 1024),
        cost_estimate=cost,
    )(*ins)


def local(src_feat, coords, offsets, weights):
    _, rows, cols, chan = src_feat.shape
    pixels = rows * cols
    width = weights.shape[4]
    own = src_feat.reshape(pixels, chan)

    def across(array, k):
        return lax.ppermute(array, "src", [(i, i ^ k) for i in range(4)])

    far = across(own, 2)
    near = across(own, 1)
    rowpos = offsets[0] + jnp.arange(rows, dtype=jnp.int32)
    enc = encoding(rowpos, chan)

    line = shape(rows, chan)
    col_a, col_b, edge_rows, panel = call(
        functools.partial(columns_kernel, rows, cols),
        [own],
        [line, line, shape(2 * cols, chan), shape(pixels, chan)],
        [pltpu.VMEM((chan // LANES, pixels, LANES), F32)],
    )
    place = jnp.broadcast_to(coords.astype(F32).reshape(2, 1), (2, chan))
    shards, slabs = lax.axis_size("shard"), lax.axis_size("slab")

    def swap(array, first):
        pairs = [(i, i + 1) for i in range(first, shards - 1, 2)]
        return lax.ppermute(array, "shard", pairs + [(j, i) for i, j in pairs])

    got_b, got_a = swap(col_b, 1), swap(col_a, 0)
    pick = "slab" if slabs == 2 else None
    edge = shape(cols + 16, chan)
    edges = call(
        functools.partial(edges_kernel, rows, cols, shards, pick),
        [edge_rows, got_a, got_b, enc],
        [edge] if pick else [edge, edge],
    )
    if pick:
        beyond = [lax.ppermute(edges[0], "slab", [(0, 1), (1, 0)])]
    else:
        up = [(i, i + 1) for i in range(slabs - 1)]
        beyond = [
            lax.ppermute(edges[1], "slab", up),
            lax.ppermute(edges[0], "slab", [(j, i) for i, j in up]),
        ]
    strip = call(
        functools.partial(strip_kernel, rows, shards),
        [got_a, got_b, enc, *beyond],
        [shape(rows + len(beyond) * (cols + 16), chan)],
    )[0]
    near_strip, far_strip = across(strip, 1), across(strip, 2)
    far, panel = lax.optimization_barrier((far, panel))
    last = across(far, 1)

    scratch = [
        pltpu.VMEM((chan // LANES, (rows + 2) * PITCH + 8, LANES), F32),
        pltpu.VMEM(((rows + 2) * cols, 3 * chan), BF16),
    ]
    sums = [shape(pixels, chan, F32), shape(pixels, width, F32)]
    cost = pl.CostEstimate(flops=5_000_000_000, bytes_accessed=4_000_000, transcendentals=0)
    base, joined = call(
        functools.partial(own_kernel, rows, cols, shards, pick),
        [place, panel, enc, strip, got_a, weights[0]],
        sums,
        scratch,
        cost=cost,
    )
    near, far, base, near_strip = lax.optimization_barrier((near, far, base, near_strip))
    cols_a = call(
        functools.partial(inner_kernel, rows, cols),
        [near, far],
        [shape(2 * rows, chan)],
        [pltpu.VMEM((chan // LANES, pixels, LANES), F32)],
    )[0]
    cols_a = swap(cols_a, 0)
    relayed = call(
        functools.partial(relay_kernel, rows),
        [far_strip, cols_a],
        [shape(strip.shape[0] + rows, chan)],
    )[0]
    last_strip = across(relayed, 1)
    base, joined = call(
        functools.partial(middle_kernel, rows, cols, shards, pick),
        [place, near, far, enc, near_strip, far_strip, cols_a, weights[0], base, joined],
        sums,
        scratch,
        cost=pl.CostEstimate(flops=0, bytes_accessed=0, transcendentals=0),
    )
    out = call(
        functools.partial(late_kernel, rows, cols, shards, pick),
        [place, last, enc, last_strip, weights[0], base, joined],
        [shape(pixels, chan)],
        scratch + [pltpu.VMEM((pixels, chan), F32)],
    )[0]
    return out.reshape(1, rows, cols, chan)


def solution(mesh):
    in_specs = (
        P("src", "slab", "shard", None),
        P("src", None),
        P("slab"),
        P("src", None, None, None, None),
    )
    out_specs = P("src", "slab", "shard", None)
    return jax.shard_map(local, mesh=mesh, in_specs=in_specs, out_specs=out_specs, check_vma=False)
```

```python
import functools
import math

import jax
import jax.numpy as jnp
from jax import lax
from jax.experimental import pallas as pl
from jax.experimental.pallas import tpu as pltpu
from jax.sharding import PartitionSpec as P

BF16, F32 = jnp.bfloat16, jnp.float32
VMEM_SPEC = pl.BlockSpec(memory_space=pltpu.VMEM)
LANES = 128
PITCH = 24


def encoding(rowpos, chan_count):
    channel_idx = jnp.arange(chan_count, dtype=jnp.int32)
    halves = (channel_idx // 2).astype(F32)
    frequency = jnp.exp(-math.log(1000.0) * halves / (chan_count / 2))
    phases = (channel_idx % 2).astype(F32) * (math.pi / 2)
    return jnp.sin(rowpos.astype(F32)[:, None] * frequency[None, :] + phases[None, :])


def blend_weight(coords, view_index):
    vertical, across = coords[0:1, :] / 6.0, coords[1:2, :] / 6.0
    low, left = lax.div(view_index, 2) == 0, lax.rem(view_index, 2) == 0
    return jnp.where(low, 1.0 - vertical, vertical) * jnp.where(left, 1.0 - across, across)


def tiles(chan):
    return [(c, slice(c * LANES, (c + 1) * LANES)) for c in range(chan // LANES)]


def column(rows, cols, view, wide, pick_last):
    for c, lanes in tiles(view.shape[1]):
        wide[c] = view[:, lanes].astype(F32)
        first = wide[c, pl.ds(0, rows, stride=cols), :]
        last = wide[c, pl.ds(cols - 1, rows, stride=cols), :]
        yield lanes, jnp.where(pick_last, last, first), jnp.where(pick_last, first, last)


def columns_kernel(rows, cols, view, col_a, col_b, edge_rows, panel, wide):
    even = lax.rem(lax.axis_index("shard"), 2) == 0
    for lanes, a, b in column(rows, cols, view, wide, even):
        col_a[:, lanes] = a.astype(BF16)
        col_b[:, lanes] = b.astype(BF16)
    edge_rows[0:cols, :] = view[0:cols, :]
    edge_rows[cols : 2 * cols, :] = view[(rows - 1) * cols :, :]
    panel[...] = view[...]


def inner_kernel(rows, cols, near, far, cols_a, wide):
    even = lax.rem(lax.axis_index("shard"), 2) == 0
    for i, view in enumerate((near, far)):
        for lanes, a, _ in column(rows, cols, view, wide, even):
            cols_a[i * rows : (i + 1) * rows, lanes] = a.astype(BF16)


def pose(shards, raw, enc, is_a):
    me = lax.axis_index("shard")
    is_left = (lax.rem(me, 2) == 0) != is_a
    inside = jnp.where(is_left, me > 0, me < shards - 1)
    return jnp.where(inside, raw[...].astype(F32) + enc[...], 0.0)


def sides(a, b):
    even = lax.rem(lax.axis_index("shard"), 2) == 0
    return jnp.where(even, b, a), jnp.where(even, a, b)


def corners(left, right, at):
    fill = jnp.zeros((14, left.shape[1]), F32)
    return jnp.concatenate([left[at : at + 1], right[at : at + 1], fill], axis=0)


def edges_kernel(rows, cols, shards, pick, edge_rows, got_a, got_b, enc, *outs):
    left, right = sides(pose(shards, got_a, enc, True), pose(shards, got_b, enc, False))
    lines = []
    for i, h in ((0, 0), (1, rows - 1)):
        row = edge_rows[i * cols : (i + 1) * cols, :].astype(F32) + enc[h : h + 1, :]
        lines.append(jnp.concatenate([row, corners(left, right, h)], axis=0))
    if pick:
        outs[0][...] = jnp.where(lax.axis_index(pick) == 0, lines[1], lines[0]).astype(BF16)
    else:
        outs[0][...] = lines[0].astype(BF16)
        outs[1][...] = lines[1].astype(BF16)


def strip_kernel(rows, shards, got_a, got_b, enc, *refs):
    out, at = refs[-1], rows
    out[0:rows, :] = pose(shards, got_b, enc, False).astype(BF16)
    for ref in refs[:-1]:
        out[at : at + ref.shape[0], :] = ref[...]
        at += ref.shape[0]


def relay_kernel(rows, strip, cols_a, out):
    size = strip.shape[0]
    out[0:size, :] = strip[...]
    out[size:, :] = cols_a[rows:, :]


def halo(rows, cols, shards, pick, enc, strip, raw_a):
    extra = cols + 16
    size = extra if pick else 2 * extra
    lines = strip[rows : rows + size, :].astype(F32)
    if pick:
        first = lax.axis_index(pick) == 0
        zero = jnp.zeros_like(lines)
        before, after = jnp.where(first, zero, lines), jnp.where(first, lines, zero)
    else:
        before, after = lines[0:extra], lines[extra:]
    posed_a = pose(shards, raw_a, enc, True).astype(BF16).astype(F32)
    left, right = sides(posed_a, strip[0:rows, :].astype(F32))
    return left, right, before, after


def unfold(rows, cols, view, enc, edges, wide, windows, base, weight, start):
    chan = view.shape[1]
    left, right, before, after = edges
    for c, lanes in tiles(chan):
        for h, edge in ((0, before), (rows + 1, after)):
            at = h * PITCH + 8
            wide[c, at : at + cols, :] = edge[0:cols, lanes]
            wide[c, at - 1 : at, :] = edge[cols : cols + 1, lanes]
            wide[c, at + cols : at + cols + 1, :] = edge[cols + 1 : cols + 2, lanes]
        wide[c, pl.ds(PITCH + 7, rows, stride=PITCH), :] = left[:, lanes]
        wide[c, pl.ds(PITCH + 8 + cols, rows, stride=PITCH), :] = right[:, lanes]
    for h in range(rows):
        here = slice(h * cols, (h + 1) * cols)
        posed = (view[here, :].astype(F32) + enc[h : h + 1, :]).astype(BF16).astype(F32)
        at = (h + 1) * PITCH + 8
        for c, lanes in tiles(chan):
            wide[c, at : at + cols, :] = posed[:, lanes]
        part = weight * posed
        base[here, :] = part if start is True else (base if start is None else start)[here, :] + part
    for h in range(rows + 2):
        at = h * PITCH + 7
        here = slice(h * cols, (h + 1) * cols)
        for b in range(3):
            for c in range(chan // LANES):
                to = b * chan + c * LANES
                windows[here, to : to + LANES] = wide[c, at + b : at + b + cols, :].astype(BF16)


def kernel_of(weights, group, at, chan):
    return jnp.concatenate(
        [
            jnp.concatenate(
                [weights[group, 3 * a + b, pl.ds(at, chan), :] for b in range(3)], axis=0
            )
            for a in range(3)
        ],
        axis=1,
    )


def convolve(pixels, cols, windows, weights, view_index):
    chan = windows.shape[1] // 3
    group = lax.div(view_index, 2)
    at = pl.multiple_of(lax.rem(view_index, 2) * chan, chan)
    width = weights.shape[3]
    taps = jnp.dot(
        windows[...], kernel_of(weights, group, at, chan), preferred_element_type=F32
    )
    return (
        taps[0:pixels, 0:width]
        + taps[cols : cols + pixels, width : 2 * width]
        + taps[2 * cols : 2 * cols + pixels, 2 * width :]
    )


def silu(x):
    return x / (1.0 + jnp.exp(-x))


def own_kernel(rows, cols, shards, pick, coords, own, enc, strip, got_a, weights, base, joined, wide,
               windows):
    me = lax.axis_index("src")
    edges = halo(rows, cols, shards, pick, enc, strip, got_a)
    unfold(rows, cols, own, enc, edges, wide, windows, base, blend_weight(coords, me), True)
    joined[...] = convolve(rows * cols, cols, windows, weights, me)


def middle_kernel(rows, cols, shards, pick, coords, near, far, enc, near_strip, far_strip, cols_a,
                  weights, base_in, joined_in, base, joined, wide, windows):
    me = lax.axis_index("src")
    width = joined.shape[1]
    sums = []
    views = (
        (1, near, near_strip, cols_a.at[0:rows], base_in),
        (2, far, far_strip, cols_a.at[rows : 2 * rows], None),
    )
    for k, view, strip, raw_a, start in views:
        index = jnp.bitwise_xor(me, k)
        edges = halo(rows, cols, shards, pick, enc, strip, raw_a)
        weight = blend_weight(coords, index)
        unfold(rows, cols, view, enc, edges, wide, windows, base, weight, start)
        sums.append(convolve(rows * cols, cols, windows, weights, index))
    joined[...] = sums[1]
    here = pl.ds(pl.multiple_of(lax.div(me, 2) * width, width), width)
    base[:, here] = base[:, here] + silu(joined_in[...] + sums[0])


def inside_kernel(rows, cols, top, coords, part, enc, weights, base_in, joined_in, base, joined, wide,
                  windows):
    index = jnp.bitwise_xor(lax.axis_index("src"), 3)
    weight = blend_weight(coords, index)
    chan, width = base.shape[1], joined.shape[1]
    count = part.shape[0] // cols
    column = jnp.zeros((count, LANES), F32)
    for c in range(chan // LANES):
        wide[c, pl.ds(PITCH + 7, count, stride=PITCH), :] = column
        wide[c, pl.ds(PITCH + 8 + cols, count, stride=PITCH), :] = column
    for h in range(count):
        here = slice(h * cols, (h + 1) * cols)
        line = enc[top + h : top + h + 1, :]
        posed = (part[here, :].astype(F32) + line).astype(BF16).astype(F32)
        at = (h + 1) * PITCH + 8
        for c, lanes in tiles(chan):
            wide[c, at : at + cols, :] = posed[:, lanes]
        base[here, :] = base_in[(top + h) * cols : (top + h + 1) * cols, :] + weight * posed
        for b in range(3):
            for c in range(chan // LANES):
                to = b * chan + c * LANES
                windows[here, to : to + LANES] = wide[c, at - 1 + b : at - 1 + b + cols, :].astype(BF16)
    group = lax.div(index, 2)
    at = pl.multiple_of(lax.rem(index, 2) * chan, chan)
    taps = jnp.dot(
        windows[0 : count * cols, :], kernel_of(weights, group, at, chan), preferred_element_type=F32
    )
    joined[...] = joined_in[...]
    for a in range(3):
        first, last = max(top + 1 - a, 0), min(top + 1 - a + count, rows)
        skip = (first - (top + 1 - a)) * cols
        size = (last - first) * cols
        joined[first * cols : last * cols, :] += taps[
            skip : skip + size, a * width : (a + 1) * width
        ]


def rim_kernel(rows, cols, shards, pick, enc, strip, weights, joined_in, *refs):
    index = jnp.bitwise_xor(lax.axis_index("src"), 3)
    *bases, out, joined = refs
    chan, width = out.shape[1], joined.shape[1]
    group = lax.div(index, 2)
    at = pl.multiple_of(lax.rem(index, 2) * chan, chan)

    def taps(pairs):
        return jnp.concatenate([weights[group, 3 * a + b, pl.ds(at, chan), :] for a, b in pairs], axis=0)

    joined[...] = joined_in[...]
    size = strip.shape[0] - rows
    left, right, before, after = halo(
        rows, cols, shards, pick, enc, strip.at[0:size], strip.at[size:]
    )
    for column, corner, b in ((left, 0, 0), (right, 1, 2)):
        above, below = (line[cols + corner : cols + corner + 1] for line in (before, after))
        tall = jnp.concatenate([above, column, below], axis=0)
        wide = jnp.concatenate([tall[a : a + rows] for a in range(3)], axis=1).astype(BF16)
        kernel = taps([(a, b) for a in range(3)])
        where = pl.ds(b // 2 * (cols - 1), rows, stride=cols)
        joined[where, :] += jnp.dot(wide, kernel, preferred_element_type=F32)
    if pick:
        first = lax.axis_index(pick) == 0
        lines = [(before + after, jnp.where(first, rows - 1, 0), jnp.where(first, 2, 0))]
    else:
        lines = [(before, 0, 0), (after, rows - 1, 2)]
    for line, h, a in lines:
        zero = jnp.zeros((1, chan), F32)
        tall = jnp.concatenate([zero, line[0:cols], zero], axis=0)
        wide = jnp.concatenate([tall[b : b + cols] for b in range(3)], axis=1).astype(BF16)
        where = pl.ds(pl.multiple_of(h * cols, cols), cols)
        kernel = taps([(a, b) for b in range(3)])
        joined[where, :] += jnp.dot(wide, kernel, preferred_element_type=F32)
    added, at = silu(joined[...]), 0
    for base in bases:
        size = base.shape[0]
        for c, lanes in tiles(chan):
            here = group == c * LANES // width
            more = jnp.where(here, added[at : at + size], 0.0)
            out[at : at + size, lanes] = (base[:, lanes] + more).astype(BF16)
        at += size


def shape(rows, chan, dtype=BF16):
    return jax.ShapeDtypeStruct((rows, chan), dtype)


def call(kernel, ins, outs, scratch=(), cost=None):
    return pl.pallas_call(
        kernel,
        out_shape=outs,
        in_specs=[VMEM_SPEC] * len(ins),
        out_specs=jax.tree.map(lambda _: VMEM_SPEC, outs),
        scratch_shapes=list(scratch),
        compiler_params=pltpu.CompilerParams(vmem_limit_bytes=32 * 1024 * 1024),
        cost_estimate=cost,
    )(*ins)


def local(src_feat, coords, offsets, weights):
    _, rows, cols, chan = src_feat.shape
    pixels = rows * cols
    width = weights.shape[4]
    own = src_feat.reshape(pixels, chan)

    def across(array, k):
        return lax.ppermute(array, "src", [(i, i ^ k) for i in range(4)])

    far = across(own, 2)
    near = across(own, 1)
    rowpos = offsets[0] + jnp.arange(rows, dtype=jnp.int32)
    enc = encoding(rowpos, chan)

    line = shape(rows, chan)
    col_a, col_b, edge_rows, panel = call(
        functools.partial(columns_kernel, rows, cols),
        [own],
        [line, line, shape(2 * cols, chan), shape(pixels, chan)],
        [pltpu.VMEM((chan // LANES, pixels, LANES), F32)],
    )
    place = jnp.broadcast_to(coords.astype(F32).reshape(2, 1), (2, chan))
    shards, slabs = lax.axis_size("shard"), lax.axis_size("slab")

    def swap(array, first):
        pairs = [(i, i + 1) for i in range(first, shards - 1, 2)]
        return lax.ppermute(array, "shard", pairs + [(j, i) for i, j in pairs])

    got_b, got_a = swap(col_b, 1), swap(col_a, 0)
    pick = "slab" if slabs == 2 else None
    edge = shape(cols + 16, chan)
    edges = call(
        functools.partial(edges_kernel, rows, cols, shards, pick),
        [edge_rows, got_a, got_b, enc],
        [edge] if pick else [edge, edge],
    )
    if pick:
        beyond = [lax.ppermute(edges[0], "slab", [(0, 1), (1, 0)])]
    else:
        up = [(i, i + 1) for i in range(slabs - 1)]
        beyond = [
            lax.ppermute(edges[1], "slab", up),
            lax.ppermute(edges[0], "slab", [(j, i) for i, j in up]),
        ]
    strip = call(
        functools.partial(strip_kernel, rows, shards),
        [got_a, got_b, enc, *beyond],
        [shape(rows + len(beyond) * (cols + 16), chan)],
    )[0]
    near_strip, far_strip = across(strip, 1), across(strip, 2)
    far, panel = lax.optimization_barrier((far, panel))
    parts = [(0, across(far, 1))]

    scratch = [
        pltpu.VMEM((chan // LANES, (rows + 2) * PITCH + 8, LANES), F32),
        pltpu.VMEM(((rows + 2) * cols, 3 * chan), BF16),
    ]
    sums = [shape(pixels, chan, F32), shape(pixels, width, F32)]
    cost = pl.CostEstimate(flops=5_000_000_000, bytes_accessed=4_000_000, transcendentals=0)
    base, joined = call(
        functools.partial(own_kernel, rows, cols, shards, pick),
        [place, panel, enc, strip, got_a, weights[0]],
        sums,
        scratch,
        cost=cost,
    )
    near, far, base, near_strip = lax.optimization_barrier((near, far, base, near_strip))
    cols_a = call(
        functools.partial(inner_kernel, rows, cols),
        [near, far],
        [shape(2 * rows, chan)],
        [pltpu.VMEM((chan // LANES, pixels, LANES), F32)],
    )[0]
    cols_a = swap(cols_a, 0)
    relayed = call(
        functools.partial(relay_kernel, rows),
        [far_strip, cols_a],
        [shape(strip.shape[0] + rows, chan)],
    )[0]
    last_strip = across(relayed, 1)
    base, joined = call(
        functools.partial(middle_kernel, rows, cols, shards, pick),
        [place, near, far, enc, near_strip, far_strip, cols_a, weights[0], base, joined],
        sums,
        scratch,
        cost=pl.CostEstimate(flops=0, bytes_accessed=0, transcendentals=0),
    )
    bases = []
    for top, part in parts:
        done, joined = call(
            functools.partial(inside_kernel, rows, cols, top),
            [place, part, enc, weights[0], base, joined],
            [shape(part.shape[0], chan, F32), shape(pixels, width, F32)],
            scratch,
            cost=pl.CostEstimate(flops=0, bytes_accessed=0, transcendentals=0),
        )
        bases.append(done)
    out = call(
        functools.partial(rim_kernel, rows, cols, shards, pick),
        [enc, last_strip, weights[0], joined, *bases],
        [shape(pixels, chan)],
        [pltpu.VMEM((pixels, width), F32)],
    )[0]
    return out.reshape(1, rows, cols, chan)


def solution(mesh):
    in_specs = (
        P("src", "slab", "shard", None),
        P("src", None),
        P("slab"),
        P("src", None, None, None, None),
    )
    out_specs = P("src", "slab", "shard", None)
    return jax.shard_map(local, mesh=mesh, in_specs=in_specs, out_specs=out_specs, check_vma=False)
```

```python
import functools
import math

import jax
import jax.numpy as jnp
from jax import lax
from jax.experimental import pallas as pl
from jax.experimental.pallas import tpu as pltpu
from jax.sharding import PartitionSpec as P

BF16, F32 = jnp.bfloat16, jnp.float32
VMEM_SPEC = pl.BlockSpec(memory_space=pltpu.VMEM)
LANES = 128
PITCH = 24


def encoding(rowpos, chan_count):
    channel_idx = jnp.arange(chan_count, dtype=jnp.int32)
    halves = (channel_idx // 2).astype(F32)
    frequency = jnp.exp(-math.log(1000.0) * halves / (chan_count / 2))
    phases = (channel_idx % 2).astype(F32) * (math.pi / 2)
    return jnp.sin(rowpos.astype(F32)[:, None] * frequency[None, :] + phases[None, :])


def blend_weight(coords, view_index):
    vertical, across = coords[0:1, :] / 6.0, coords[1:2, :] / 6.0
    low, left = lax.div(view_index, 2) == 0, lax.rem(view_index, 2) == 0
    return jnp.where(low, 1.0 - vertical, vertical) * jnp.where(left, 1.0 - across, across)


def tiles(chan):
    return [(c, slice(c * LANES, (c + 1) * LANES)) for c in range(chan // LANES)]


def column(rows, cols, view, wide, pick_last):
    for c, lanes in tiles(view.shape[1]):
        wide[c] = view[:, lanes].astype(F32)
        first = wide[c, pl.ds(0, rows, stride=cols), :]
        last = wide[c, pl.ds(cols - 1, rows, stride=cols), :]
        yield lanes, jnp.where(pick_last, last, first), jnp.where(pick_last, first, last)


def columns_kernel(rows, cols, view, col_a, col_b, edge_rows, panel, wide):
    even = lax.rem(lax.axis_index("shard"), 2) == 0
    for lanes, a, b in column(rows, cols, view, wide, even):
        col_a[:, lanes] = a.astype(BF16)
        col_b[:, lanes] = b.astype(BF16)
    edge_rows[0:cols, :] = view[0:cols, :]
    edge_rows[cols : 2 * cols, :] = view[(rows - 1) * cols :, :]
    panel[...] = view[...]


def inner_kernel(rows, cols, near, far, cols_a, wide):
    even = lax.rem(lax.axis_index("shard"), 2) == 0
    for i, view in enumerate((near, far)):
        for lanes, a, _ in column(rows, cols, view, wide, even):
            cols_a[i * rows : (i + 1) * rows, lanes] = a.astype(BF16)


def pose(shards, raw, enc, is_a):
    me = lax.axis_index("shard")
    is_left = (lax.rem(me, 2) == 0) != is_a
    inside = jnp.where(is_left, me > 0, me < shards - 1)
    return jnp.where(inside, raw[...].astype(F32) + enc[...], 0.0)


def sides(a, b):
    even = lax.rem(lax.axis_index("shard"), 2) == 0
    return jnp.where(even, b, a), jnp.where(even, a, b)


def corners(left, right, at):
    fill = jnp.zeros((14, left.shape[1]), F32)
    return jnp.concatenate([left[at : at + 1], right[at : at + 1], fill], axis=0)


def edges_kernel(rows, cols, shards, pick, edge_rows, got_a, got_b, enc, *outs):
    left, right = sides(pose(shards, got_a, enc, True), pose(shards, got_b, enc, False))
    lines = []
    for i, h in ((0, 0), (1, rows - 1)):
        row = edge_rows[i * cols : (i + 1) * cols, :].astype(F32) + enc[h : h + 1, :]
        lines.append(jnp.concatenate([row, corners(left, right, h)], axis=0))
    if pick:
        outs[0][...] = jnp.where(lax.axis_index(pick) == 0, lines[1], lines[0]).astype(BF16)
    else:
        outs[0][...] = lines[0].astype(BF16)
        outs[1][...] = lines[1].astype(BF16)


def strip_kernel(rows, shards, got_a, got_b, enc, *refs):
    out, at = refs[-1], rows
    out[0:rows, :] = pose(shards, got_b, enc, False).astype(BF16)
    for ref in refs[:-1]:
        out[at : at + ref.shape[0], :] = ref[...]
        at += ref.shape[0]


def relay_kernel(rows, strip, cols_a, out):
    size = strip.shape[0]
    out[0:size, :] = strip[...]
    out[size:, :] = cols_a[rows:, :]


def halo(rows, cols, shards, pick, enc, strip, raw_a):
    extra = cols + 16
    size = extra if pick else 2 * extra
    lines = strip[rows : rows + size, :].astype(F32)
    if pick:
        first = lax.axis_index(pick) == 0
        zero = jnp.zeros_like(lines)
        before, after = jnp.where(first, zero, lines), jnp.where(first, lines, zero)
    else:
        before, after = lines[0:extra], lines[extra:]
    posed_a = pose(shards, raw_a, enc, True).astype(BF16).astype(F32)
    left, right = sides(posed_a, strip[0:rows, :].astype(F32))
    return left, right, before, after


def unfold(rows, cols, view, enc, edges, wide, windows, base, weight, start):
    chan = view.shape[1]
    left, right, before, after = edges
    for c, lanes in tiles(chan):
        for h, edge in ((0, before), (rows + 1, after)):
            at = h * PITCH + 8
            wide[c, at : at + cols, :] = edge[0:cols, lanes]
            wide[c, at - 1 : at, :] = edge[cols : cols + 1, lanes]
            wide[c, at + cols : at + cols + 1, :] = edge[cols + 1 : cols + 2, lanes]
        wide[c, pl.ds(PITCH + 7, rows, stride=PITCH), :] = left[:, lanes]
        wide[c, pl.ds(PITCH + 8 + cols, rows, stride=PITCH), :] = right[:, lanes]
    for h in range(rows):
        here = slice(h * cols, (h + 1) * cols)
        posed = (view[here, :].astype(F32) + enc[h : h + 1, :]).astype(BF16).astype(F32)
        at = (h + 1) * PITCH + 8
        for c, lanes in tiles(chan):
            wide[c, at : at + cols, :] = posed[:, lanes]
        part = weight * posed
        base[here, :] = part if start is True else (base if start is None else start)[here, :] + part
    for h in range(rows + 2):
        at = h * PITCH + 7
        here = slice(h * cols, (h + 1) * cols)
        for b in range(3):
            for c in range(chan // LANES):
                to = b * chan + c * LANES
                windows[here, to : to + LANES] = wide[c, at + b : at + b + cols, :].astype(BF16)


def kernel_of(weights, group, at, chan):
    return jnp.concatenate(
        [
            jnp.concatenate(
                [weights[group, 3 * a + b, pl.ds(at, chan), :] for b in range(3)], axis=0
            )
            for a in range(3)
        ],
        axis=1,
    )


def convolve(pixels, cols, windows, weights, view_index):
    chan = windows.shape[1] // 3
    group = lax.div(view_index, 2)
    at = pl.multiple_of(lax.rem(view_index, 2) * chan, chan)
    width = weights.shape[3]
    taps = jnp.dot(
        windows[...], kernel_of(weights, group, at, chan), preferred_element_type=F32
    )
    return (
        taps[0:pixels, 0:width]
        + taps[cols : cols + pixels, width : 2 * width]
        + taps[2 * cols : 2 * cols + pixels, 2 * width :]
    )


def silu(x):
    return x / (1.0 + jnp.exp(-x))


def own_kernel(rows, cols, shards, pick, coords, own, enc, strip, got_a, weights, base, joined, wide,
               windows):
    me = lax.axis_index("src")
    edges = halo(rows, cols, shards, pick, enc, strip, got_a)
    unfold(rows, cols, own, enc, edges, wide, windows, base, blend_weight(coords, me), True)
    joined[...] = convolve(rows * cols, cols, windows, weights, me)


def middle_kernel(rows, cols, shards, pick, coords, near, far, enc, near_strip, cols_a, weights,
                  base_in, joined_in, base, joined, wide, windows):
    me = lax.axis_index("src")
    width = joined.shape[1]
    index = jnp.bitwise_xor(me, 1)
    edges = halo(rows, cols, shards, pick, enc, near_strip, cols_a.at[0:rows])
    weight = blend_weight(coords, index)
    unfold(rows, cols, near, enc, edges, wide, windows, base, weight, base_in)
    done = joined_in[...] + convolve(rows * cols, cols, windows, weights, index)
    here = pl.ds(pl.multiple_of(lax.div(me, 2) * width, width), width)
    base[:, here] = base[:, here] + silu(done)
    joined[...] = jnp.zeros_like(joined)
    inside(rows, cols, 3, coords, far, enc, weights, base, base, joined, wide, windows)


def inside(rows, cols, k, coords, view, enc, weights, base_in, base, joined, wide, windows):
    index = jnp.bitwise_xor(lax.axis_index("src"), k)
    weight = blend_weight(coords, index)
    chan, width = base.shape[1], joined.shape[1]
    column = jnp.zeros((rows, LANES), F32)
    for c in range(chan // LANES):
        wide[c, pl.ds(PITCH + 7, rows, stride=PITCH), :] = column
        wide[c, pl.ds(PITCH + 8 + cols, rows, stride=PITCH), :] = column
    for h in range(rows):
        here = slice(h * cols, (h + 1) * cols)
        posed = (view[here, :].astype(F32) + enc[h : h + 1, :]).astype(BF16).astype(F32)
        at = (h + 1) * PITCH + 8
        for c, lanes in tiles(chan):
            wide[c, at : at + cols, :] = posed[:, lanes]
        base[here, :] = base_in[here, :] + weight * posed
        for b in range(3):
            for c in range(chan // LANES):
                to = b * chan + c * LANES
                windows[here, to : to + LANES] = wide[c, at - 1 + b : at - 1 + b + cols, :].astype(BF16)
    group = lax.div(index, 2)
    at = pl.multiple_of(lax.rem(index, 2) * chan, chan)
    taps = jnp.dot(
        windows[0 : rows * cols, :], kernel_of(weights, group, at, chan), preferred_element_type=F32
    )
    for a in range(3):
        first, last = max(1 - a, 0), min(1 - a + rows, rows)
        skip, size = (first - (1 - a)) * cols, (last - first) * cols
        joined[first * cols : last * cols, :] += taps[
            skip : skip + size, a * width : (a + 1) * width
        ]


def last_kernel(rows, cols, coords, last, enc, weights, base_in, joined_in, base, joined, wide,
                windows):
    joined[...] = joined_in[...]
    inside(rows, cols, 2, coords, last, enc, weights, base_in, base, joined, wide, windows)


def rim_kernel(rows, cols, shards, pick, enc, last_strip, relayed, cols_a, weights, base, joined_in,
               out, joined):
    me = lax.axis_index("src")
    chan, width = out.shape[1], joined.shape[1]
    group = lax.div(jnp.bitwise_xor(me, 2), 2)
    size = last_strip.shape[0]
    edges = [
        (3, halo(rows, cols, shards, pick, enc, relayed.at[0:size], cols_a.at[rows : 2 * rows])),
        (2, halo(rows, cols, shards, pick, enc, last_strip, relayed.at[size : size + rows])),
    ]

    def add(where, lines, pairs):
        wide, kernel = [], []
        for k, line in lines:
            at = pl.multiple_of(lax.rem(jnp.bitwise_xor(me, k), 2) * chan, chan)
            count = line.shape[0] - 2
            wide += [line[i : i + count] for i in range(3)]
            kernel += [weights[group, 3 * a + b, pl.ds(at, chan), :] for a, b in pairs]
        joined[where, :] += jnp.dot(
            jnp.concatenate(wide, axis=1).astype(BF16),
            jnp.concatenate(kernel, axis=0),
            preferred_element_type=F32,
        )

    joined[...] = joined_in[...]
    for side, b in ((0, 0), (1, 2)):
        tall = []
        for k, view in edges:
            above, below = (line[cols + side : cols + side + 1] for line in view[2:])
            tall.append((k, jnp.concatenate([above, view[side], below], axis=0)))
        where = pl.ds(side * (cols - 1), rows, stride=cols)
        add(where, tall, [(a, b) for a in range(3)])
    zero = jnp.zeros((1, chan), F32)
    if pick:
        first = lax.axis_index(pick) == 0
        places = [(jnp.where(first, rows - 1, 0), jnp.where(first, 2, 0), lambda view: view[2] + view[3])]
    else:
        places = [(0, 0, lambda view: view[2]), (rows - 1, 2, lambda view: view[3])]
    for h, a, line in places:
        tall = [(k, jnp.concatenate([zero, line(view)[0:cols], zero], axis=0)) for k, view in edges]
        where = pl.ds(pl.multiple_of(h * cols, cols), cols)
        add(where, tall, [(a, b) for b in range(3)])
    added = silu(joined[...])
    for c, lanes in tiles(chan):
        here = group == c * LANES // width
        out[:, lanes] = (base[:, lanes] + jnp.where(here, added, 0.0)).astype(BF16)


def shape(rows, chan, dtype=BF16):
    return jax.ShapeDtypeStruct((rows, chan), dtype)


def call(kernel, ins, outs, scratch=(), cost=None):
    return pl.pallas_call(
        kernel,
        out_shape=outs,
        in_specs=[VMEM_SPEC] * len(ins),
        out_specs=jax.tree.map(lambda _: VMEM_SPEC, outs),
        scratch_shapes=list(scratch),
        compiler_params=pltpu.CompilerParams(vmem_limit_bytes=32 * 1024 * 1024),
        cost_estimate=cost,
    )(*ins)


def local(src_feat, coords, offsets, weights):
    _, rows, cols, chan = src_feat.shape
    pixels = rows * cols
    width = weights.shape[4]
    own = src_feat.reshape(pixels, chan)

    def across(array, k):
        return lax.ppermute(array, "src", [(i, i ^ k) for i in range(4)])

    far = across(own, 3)
    near = across(own, 1)
    rowpos = offsets[0] + jnp.arange(rows, dtype=jnp.int32)
    enc = encoding(rowpos, chan)

    line = shape(rows, chan)
    col_a, col_b, edge_rows, panel = call(
        functools.partial(columns_kernel, rows, cols),
        [own],
        [line, line, shape(2 * cols, chan), shape(pixels, chan)],
        [pltpu.VMEM((chan // LANES, pixels, LANES), F32)],
    )
    place = jnp.broadcast_to(coords.astype(F32).reshape(2, 1), (2, chan))
    shards, slabs = lax.axis_size("shard"), lax.axis_size("slab")

    def swap(array, first):
        pairs = [(i, i + 1) for i in range(first, shards - 1, 2)]
        return lax.ppermute(array, "shard", pairs + [(j, i) for i, j in pairs])

    got_b, got_a = swap(col_b, 1), swap(col_a, 0)
    pick = "slab" if slabs == 2 else None
    edge = shape(cols + 16, chan)
    edges = call(
        functools.partial(edges_kernel, rows, cols, shards, pick),
        [edge_rows, got_a, got_b, enc],
        [edge] if pick else [edge, edge],
    )
    if pick:
        beyond = [lax.ppermute(edges[0], "slab", [(0, 1), (1, 0)])]
    else:
        up = [(i, i + 1) for i in range(slabs - 1)]
        beyond = [
            lax.ppermute(edges[1], "slab", up),
            lax.ppermute(edges[0], "slab", [(j, i) for i, j in up]),
        ]
    strip = call(
        functools.partial(strip_kernel, rows, shards),
        [got_a, got_b, enc, *beyond],
        [shape(rows + len(beyond) * (cols + 16), chan)],
    )[0]
    near_strip, last_strip = across(strip, 1), across(strip, 2)
    far, panel = lax.optimization_barrier((far, panel))
    last = across(far, 1)

    scratch = [
        pltpu.VMEM((chan // LANES, (rows + 2) * PITCH + 8, LANES), F32),
        pltpu.VMEM(((rows + 2) * cols, 3 * chan), BF16),
    ]
    sums = [shape(pixels, chan, F32), shape(pixels, width, F32)]
    cost = pl.CostEstimate(flops=5_000_000_000, bytes_accessed=4_000_000, transcendentals=0)
    base, joined = call(
        functools.partial(own_kernel, rows, cols, shards, pick),
        [place, panel, enc, strip, got_a, weights[0]],
        sums,
        scratch,
        cost=cost,
    )
    near, far, base, near_strip = lax.optimization_barrier((near, far, base, near_strip))
    cols_a = call(
        functools.partial(inner_kernel, rows, cols),
        [near, far],
        [shape(2 * rows, chan)],
        [pltpu.VMEM((chan // LANES, pixels, LANES), F32)],
    )[0]
    cols_a = swap(cols_a, 0)
    relayed = call(
        functools.partial(relay_kernel, rows),
        [last_strip, cols_a],
        [shape(strip.shape[0] + rows, chan)],
    )[0]
    relayed = across(relayed, 1)
    base, joined = call(
        functools.partial(middle_kernel, rows, cols, shards, pick),
        [place, near, far, enc, near_strip, cols_a, weights[0], base, joined],
        sums,
        scratch,
        cost=pl.CostEstimate(flops=0, bytes_accessed=0, transcendentals=0),
    )
    base, joined = call(
        functools.partial(last_kernel, rows, cols),
        [place, last, enc, weights[0], base, joined],
        sums,
        scratch,
        cost=pl.CostEstimate(flops=0, bytes_accessed=0, transcendentals=0),
    )
    out = call(
        functools.partial(rim_kernel, rows, cols, shards, pick),
        [enc, last_strip, relayed, cols_a, weights[0], base, joined],
        [shape(pixels, chan)],
        [pltpu.VMEM((pixels, width), F32)],
    )[0]
    return out.reshape(1, rows, cols, chan)


def solution(mesh):
    in_specs = (
        P("src", "slab", "shard", None),
        P("src", None),
        P("slab"),
        P("src", None, None, None, None),
    )
    out_specs = P("src", "slab", "shard", None)
    return jax.shard_map(local, mesh=mesh, in_specs=in_specs, out_specs=out_specs, check_vma=False)
```

```python
import functools
import math

import jax
import jax.numpy as jnp
from jax import lax
from jax.experimental import pallas as pl
from jax.experimental.pallas import tpu as pltpu
from jax.sharding import PartitionSpec as P

BF16, F32 = jnp.bfloat16, jnp.float32
VMEM_SPEC = pl.BlockSpec(memory_space=pltpu.VMEM)
LANES = 128
BLOCKS = 4


def encoding(rowpos, chan_count):
    channel_idx = jnp.arange(chan_count, dtype=jnp.int32)
    halves = (channel_idx // 2).astype(F32)
    frequency = jnp.exp(-math.log(1000.0) * halves / (chan_count / 2))
    phases = (channel_idx % 2).astype(F32) * (math.pi / 2)
    return jnp.sin(rowpos.astype(F32)[:, None] * frequency[None, :] + phases[None, :])


def blend_weight(coords, view_index):
    vertical, across = coords[0:1, :] / 6.0, coords[1:2, :] / 6.0
    low, left = lax.div(view_index, 2) == 0, lax.rem(view_index, 2) == 0
    return jnp.where(low, 1.0 - vertical, vertical) * jnp.where(left, 1.0 - across, across)


def tiles(chan):
    return [(c, slice(c * LANES, (c + 1) * LANES)) for c in range(chan // LANES)]


def column(rows, cols, view, wide, pick_last):
    for c, lanes in tiles(view.shape[1]):
        wide[c] = view[:, lanes].astype(F32)
        first = wide[c, pl.ds(0, rows, stride=cols), :]
        last = wide[c, pl.ds(cols - 1, rows, stride=cols), :]
        yield lanes, jnp.where(pick_last, last, first), jnp.where(pick_last, first, last)


def columns_kernel(rows, cols, view, col_a, col_b, edge_rows, panel, wide):
    even = lax.rem(lax.axis_index("shard"), 2) == 0
    for lanes, a, b in column(rows, cols, view, wide, even):
        col_a[:, lanes] = a.astype(BF16)
        col_b[:, lanes] = b.astype(BF16)
    edge_rows[0:cols, :] = view[0:cols, :]
    edge_rows[cols : 2 * cols, :] = view[(rows - 1) * cols :, :]
    panel[...] = view[...]


def inner_kernel(rows, cols, view, out, wide):
    even = lax.rem(lax.axis_index("shard"), 2) == 0
    for lanes, a, _ in column(rows, cols, view, wide, even):
        out[:, lanes] = a.astype(BF16)


def pose(shards, raw, enc, is_a):
    me = lax.axis_index("shard")
    is_left = (lax.rem(me, 2) == 0) != is_a
    inside = jnp.where(is_left, me > 0, me < shards - 1)
    return jnp.where(inside, raw[...].astype(F32) + enc[...], 0.0)


def sides(a, b):
    even = lax.rem(lax.axis_index("shard"), 2) == 0
    return jnp.where(even, b, a), jnp.where(even, a, b)


def corners(left, right, at):
    fill = jnp.zeros((14, left.shape[1]), F32)
    return jnp.concatenate([left[at : at + 1], right[at : at + 1], fill], axis=0)


def edges_kernel(rows, cols, shards, pick, edge_rows, got_a, got_b, enc, *outs):
    left, right = sides(pose(shards, got_a, enc, True), pose(shards, got_b, enc, False))
    lines = []
    for i, h in ((0, 0), (1, rows - 1)):
        row = edge_rows[i * cols : (i + 1) * cols, :].astype(F32) + enc[h : h + 1, :]
        lines.append(jnp.concatenate([row, corners(left, right, h)], axis=0))
    if pick:
        outs[0][...] = jnp.where(lax.axis_index(pick) == 0, lines[1], lines[0]).astype(BF16)
    else:
        outs[0][...] = lines[0].astype(BF16)
        outs[1][...] = lines[1].astype(BF16)


def strip_kernel(rows, shards, got_a, got_b, enc, *refs):
    out, at = refs[-1], rows
    out[0:rows, :] = pose(shards, got_b, enc, False).astype(BF16)
    for ref in refs[:-1]:
        out[at : at + ref.shape[0], :] = ref[...]
        at += ref.shape[0]


def relay_kernel(strip, far_a, out):
    size = strip.shape[0]
    out[0:size, :] = strip[...]
    out[size:, :] = far_a[...]


def neighbours(rows, cols, shards, pick, enc, strip, raw_a):
    extra = cols + 16
    size = extra if pick else 2 * extra
    lines = strip[rows : rows + size, :].astype(F32)
    if pick:
        first = lax.axis_index(pick) == 0
        zero = jnp.zeros_like(lines)
        both = jnp.where(first, zero, lines), jnp.where(first, lines, zero)
    else:
        both = lines[0:extra], lines[extra:]
    before, after = (
        jnp.concatenate([x[cols : cols + 1], x[0:cols], x[cols + 1 : cols + 2]], axis=0) for x in both
    )
    posed_a = pose(shards, raw_a, enc, True).astype(BF16).astype(F32)
    return posed_a, strip[0:rows, :].astype(F32), before, after


def where_of(k, chan):
    index = jnp.bitwise_xor(lax.axis_index("src"), k)
    return lax.div(index, 2), pl.multiple_of(lax.rem(index, 2) * chan, chan)


def inside(rows, cols, k, coords, view, enc, weights, base_in, base, joined, panel):
    weight = blend_weight(coords, jnp.bitwise_xor(lax.axis_index("src"), k))
    chan, width = view.shape[1], joined.shape[1]
    pixels = rows * cols
    for h in range(rows):
        here = slice(h * cols, (h + 1) * cols)
        posed = (view[here, :].astype(F32) + enc[h : h + 1, :]).astype(BF16)
        part = weight * posed.astype(F32)
        base[here, :] = part if base_in is None else base_in[here, :] + part
        panel[here, :] = posed
    group, at = where_of(k, chan)
    kernel = jnp.concatenate(
        [weights[group, 3 * a + b, pl.ds(at, chan), :] for b in range(3) for a in range(3)], axis=1
    )
    size = pixels // BLOCKS
    taps = jnp.concatenate(
        [
            jnp.dot(panel[i * size : (i + 1) * size, :], kernel, preferred_element_type=F32)
            for i in range(BLOCKS)
        ],
        axis=0,
    )
    column = lax.rem(lax.broadcasted_iota(jnp.int32, (pixels, width), 0), cols)
    zero = jnp.zeros((cols, width), F32)
    total = joined[...]
    for b in (1, 0, 2):
        up, level, down = (taps[:, (3 * b + a) * width : (3 * b + a + 1) * width] for a in range(3))
        part = level + jnp.concatenate([zero, up[: pixels - cols]], axis=0)
        part = part + jnp.concatenate([down[cols:], zero], axis=0)
        if b == 0:
            part = jnp.where(column == 0, 0.0, pltpu.roll(part, 1, 0))
        if b == 2:
            part = jnp.where(column == cols - 1, 0.0, pltpu.roll(part, pixels - 1, 0))
        total = total + part
    joined[...] = total


def add_line(joined, where, line, weights, group, at, taps):
    chan, count = line.shape[1], line.shape[0] - 2
    wide = jnp.concatenate([line[i : i + count] for i in range(3)], axis=1).astype(BF16)
    kernel = jnp.concatenate([weights[group, tap, pl.ds(at, chan), :] for tap in taps], axis=0)
    joined[where, :] += jnp.dot(wide, kernel, preferred_element_type=F32)


def add_columns(rows, cols, joined, weights, a, a_view, b, b_view):
    even = lax.rem(lax.axis_index("shard"), 2) == 0
    chan = a.shape[1]
    group, at_a = where_of(a_view, chan)
    at_b = where_of(b_view, chan)[1]
    zero = jnp.zeros((1, chan), F32)
    left, right = sides(a, b)
    at_left = pl.multiple_of(jnp.where(even, at_b, at_a), chan)
    at_right = pl.multiple_of(jnp.where(even, at_a, at_b), chan)
    for side, tap, start, at in ((left, 0, 0, at_left), (right, 2, cols - 1, at_right)):
        line = jnp.concatenate([zero, side, zero], axis=0)
        where = pl.ds(start, rows, stride=cols)
        add_line(joined, where, line, weights, group, at, [3 * i + tap for i in range(3)])


def add_rows(rows, cols, pick, joined, weights, view, before, after):
    group, at = where_of(view, before.shape[1])
    if pick:
        first = lax.axis_index(pick) == 0
        places = [(before + after, jnp.where(first, rows - 1, 0), jnp.where(first, 6, 0))]
    else:
        places = [(before, 0, 0), (after, rows - 1, 6)]
    for line, h, tap in places:
        where = pl.ds(pl.multiple_of(h * cols, cols), cols)
        add_line(joined, where, line, weights, group, at, [tap + i for i in range(3)])


def silu(x):
    return x / (1.0 + jnp.exp(-x))


def own_kernel(rows, cols, shards, pick, coords, own, enc, strip, got_a, weights, base, joined, panel):
    a, b, before, after = neighbours(rows, cols, shards, pick, enc, strip, got_a)
    joined[...] = jnp.zeros_like(joined)
    inside(rows, cols, 0, coords, own, enc, weights, None, base, joined, panel)
    add_columns(rows, cols, joined, weights, a, 0, b, 0)
    add_rows(rows, cols, pick, joined, weights, 0, before, after)


def middle_kernel(rows, cols, shards, pick, coords, near, far, enc, near_strip, last_strip, near_a,
                  far_a, weights, base_in, joined_in, base, joined, panel):
    me = lax.axis_index("src")
    width = joined.shape[1]
    a, b, before, after = neighbours(rows, cols, shards, pick, enc, near_strip, near_a)
    joined[...] = joined_in[...]
    inside(rows, cols, 1, coords, near, enc, weights, base_in, base, joined, panel)
    add_columns(rows, cols, joined, weights, a, 1, b, 1)
    add_rows(rows, cols, pick, joined, weights, 1, before, after)
    here = pl.ds(pl.multiple_of(lax.div(me, 2) * width, width), width)
    base[:, here] = base[:, here] + silu(joined[...])
    a, b, before, after = neighbours(rows, cols, shards, pick, enc, last_strip, far_a)
    joined[...] = jnp.zeros_like(joined)
    inside(rows, cols, 3, coords, far, enc, weights, base, base, joined, panel)
    add_columns(rows, cols, joined, weights, a, 3, b, 2)
    add_rows(rows, cols, pick, joined, weights, 2, before, after)


def last_kernel(rows, cols, coords, last, enc, weights, base_in, joined_in, base, joined, panel):
    joined[...] = joined_in[...]
    inside(rows, cols, 2, coords, last, enc, weights, base_in, base, joined, panel)


def rim_kernel(rows, cols, shards, pick, enc, relayed, weights, base, joined_in, out, joined):
    chan, width = out.shape[1], joined.shape[1]
    size = relayed.shape[0] - rows
    last_a, b, before, after = neighbours(
        rows, cols, shards, pick, enc, relayed.at[0:size], relayed.at[size : size + rows]
    )
    joined[...] = joined_in[...]
    add_columns(rows, cols, joined, weights, last_a, 2, b, 3)
    add_rows(rows, cols, pick, joined, weights, 3, before, after)
    group = where_of(2, chan)[0]
    added = silu(joined[...])
    for c, lanes in tiles(chan):
        here = group == c * LANES // width
        out[:, lanes] = (base[:, lanes] + jnp.where(here, added, 0.0)).astype(BF16)


def shape(rows, chan, dtype=BF16):
    return jax.ShapeDtypeStruct((rows, chan), dtype)


def call(kernel, ins, outs, scratch=(), cost=None):
    return pl.pallas_call(
        kernel,
        out_shape=outs,
        in_specs=[VMEM_SPEC] * len(ins),
        out_specs=jax.tree.map(lambda _: VMEM_SPEC, outs),
        scratch_shapes=list(scratch),
        compiler_params=pltpu.CompilerParams(vmem_limit_bytes=32 * 1024 * 1024),
        cost_estimate=cost,
    )(*ins)


def local(src_feat, coords, offsets, weights):
    _, rows, cols, chan = src_feat.shape
    pixels = rows * cols
    width = weights.shape[4]
    own = src_feat.reshape(pixels, chan)

    def across(array, k):
        return lax.ppermute(array, "src", [(i, i ^ k) for i in range(4)])

    far = across(own, 3)
    near = across(own, 1)
    rowpos = offsets[0] + jnp.arange(rows, dtype=jnp.int32)
    enc = encoding(rowpos, chan)

    line = shape(rows, chan)
    col_a, col_b, edge_rows, panel = call(
        functools.partial(columns_kernel, rows, cols),
        [own],
        [line, line, shape(2 * cols, chan), shape(pixels, chan)],
        [pltpu.VMEM((chan // LANES, pixels, LANES), F32)],
    )
    place = jnp.broadcast_to(coords.astype(F32).reshape(2, 1), (2, chan))
    shards, slabs = lax.axis_size("shard"), lax.axis_size("slab")

    def swap(array, first):
        pairs = [(i, i + 1) for i in range(first, shards - 1, 2)]
        return lax.ppermute(array, "shard", pairs + [(j, i) for i, j in pairs])

    got_b, got_a = swap(col_b, 1), swap(col_a, 0)
    pick = "slab" if slabs == 2 else None
    edge = shape(cols + 16, chan)
    edges = call(
        functools.partial(edges_kernel, rows, cols, shards, pick),
        [edge_rows, got_a, got_b, enc],
        [edge] if pick else [edge, edge],
    )
    if pick:
        beyond = [lax.ppermute(edges[0], "slab", [(0, 1), (1, 0)])]
    else:
        up = [(i, i + 1) for i in range(slabs - 1)]
        beyond = [
            lax.ppermute(edges[1], "slab", up),
            lax.ppermute(edges[0], "slab", [(j, i) for i, j in up]),
        ]
    strip = call(
        functools.partial(strip_kernel, rows, shards),
        [got_a, got_b, enc, *beyond],
        [shape(rows + len(beyond) * (cols + 16), chan)],
    )[0]
    near_strip, last_strip = across(strip, 1), across(strip, 2)
    far, panel = lax.optimization_barrier((far, panel))
    last = across(far, 1)

    def beside(view):
        out = call(
            functools.partial(inner_kernel, rows, cols),
            [view],
            [line],
            [pltpu.VMEM((chan // LANES, pixels, LANES), F32)],
        )[0]
        return swap(out, 0)

    far_a = beside(far)

    scratch = [pltpu.VMEM((pixels, chan), BF16)]
    sums = [shape(pixels, chan, F32), shape(pixels, width, F32)]
    cost = pl.CostEstimate(flops=5_000_000_000, bytes_accessed=4_000_000, transcendentals=0)
    base, joined = call(
        functools.partial(own_kernel, rows, cols, shards, pick),
        [place, panel, enc, strip, got_a, weights[0]],
        sums,
        scratch,
        cost=cost,
    )
    last_strip, base = lax.optimization_barrier((last_strip, base))
    near, base, near_strip, far_a = lax.optimization_barrier((near, base, near_strip, far_a))
    relayed = call(
        relay_kernel, [last_strip, far_a], [shape(strip.shape[0] + rows, chan)]
    )[0]
    relayed = across(relayed, 1)
    near_a = beside(near)
    base, joined = call(
        functools.partial(middle_kernel, rows, cols, shards, pick),
        [place, near, far, enc, near_strip, last_strip, near_a, far_a, weights[0], base, joined],
        sums,
        scratch,
        cost=pl.CostEstimate(flops=0, bytes_accessed=0, transcendentals=0),
    )
    base, joined = call(
        functools.partial(last_kernel, rows, cols),
        [place, last, enc, weights[0], base, joined],
        sums,
        scratch,
        cost=pl.CostEstimate(flops=0, bytes_accessed=0, transcendentals=0),
    )
    out = call(
        functools.partial(rim_kernel, rows, cols, shards, pick),
        [enc, relayed, weights[0], base, joined],
        [shape(pixels, chan)],
        [pltpu.VMEM((pixels, width), F32)],
    )[0]
    return out.reshape(1, rows, cols, chan)


def solution(mesh):
    in_specs = (
        P("src", "slab", "shard", None),
        P("src", None),
        P("slab"),
        P("src", None, None, None, None),
    )
    out_specs = P("src", "slab", "shard", None)
    return jax.shard_map(local, mesh=mesh, in_specs=in_specs, out_specs=out_specs, check_vma=False)
```

```python
import functools
import math

import jax
import jax.numpy as jnp
from jax import lax
from jax.experimental import pallas as pl
from jax.experimental.pallas import tpu as pltpu
from jax.sharding import PartitionSpec as P

BF16, F32 = jnp.bfloat16, jnp.float32
VMEM_SPEC = pl.BlockSpec(memory_space=pltpu.VMEM)
LANES = 128
BLOCKS = 4


def encoding(rowpos, chan_count):
    channel_idx = jnp.arange(chan_count, dtype=jnp.int32)
    halves = (channel_idx // 2).astype(F32)
    frequency = jnp.exp(-math.log(1000.0) * halves / (chan_count / 2))
    phases = (channel_idx % 2).astype(F32) * (math.pi / 2)
    return jnp.sin(rowpos.astype(F32)[:, None] * frequency[None, :] + phases[None, :])


def blend_weight(coords, view_index):
    vertical, across = coords[0:1, :] / 6.0, coords[1:2, :] / 6.0
    low, left = lax.div(view_index, 2) == 0, lax.rem(view_index, 2) == 0
    return jnp.where(low, 1.0 - vertical, vertical) * jnp.where(left, 1.0 - across, across)


def tiles(chan):
    return [(c, slice(c * LANES, (c + 1) * LANES)) for c in range(chan // LANES)]


def column(rows, cols, view, wide, pick_last):
    for c, lanes in tiles(view.shape[1]):
        wide[c] = view[:, lanes].astype(F32)
        first = wide[c, pl.ds(0, rows, stride=cols), :]
        last = wide[c, pl.ds(cols - 1, rows, stride=cols), :]
        yield lanes, jnp.where(pick_last, last, first), jnp.where(pick_last, first, last)


def columns_kernel(rows, cols, view, col_a, col_b, edge_rows, panel, wide):
    even = lax.rem(lax.axis_index("shard"), 2) == 0
    for lanes, a, b in column(rows, cols, view, wide, even):
        col_a[:, lanes] = a.astype(BF16)
        col_b[:, lanes] = b.astype(BF16)
    edge_rows[0:cols, :] = view[0:cols, :]
    edge_rows[cols : 2 * cols, :] = view[(rows - 1) * cols :, :]
    panel[...] = view[...]


def inner_kernel(rows, cols, view, out, wide):
    even = lax.rem(lax.axis_index("shard"), 2) == 0
    for lanes, a, _ in column(rows, cols, view, wide, even):
        out[:, lanes] = a.astype(BF16)


def pose(shards, raw, enc, is_a):
    me = lax.axis_index("shard")
    is_left = (lax.rem(me, 2) == 0) != is_a
    inside = jnp.where(is_left, me > 0, me < shards - 1)
    return jnp.where(inside, raw[...].astype(F32) + enc[...], 0.0)


def sides(a, b):
    even = lax.rem(lax.axis_index("shard"), 2) == 0
    return jnp.where(even, b, a), jnp.where(even, a, b)


def corners(left, right, at):
    fill = jnp.zeros((14, left.shape[1]), F32)
    return jnp.concatenate([left[at : at + 1], right[at : at + 1], fill], axis=0)


def edges_kernel(rows, cols, shards, pick, edge_rows, got_a, got_b, enc, *outs):
    left, right = sides(pose(shards, got_a, enc, True), pose(shards, got_b, enc, False))
    lines = []
    for i, h in ((0, 0), (1, rows - 1)):
        row = edge_rows[i * cols : (i + 1) * cols, :].astype(F32) + enc[h : h + 1, :]
        lines.append(jnp.concatenate([row, corners(left, right, h)], axis=0))
    if pick:
        outs[0][...] = jnp.where(lax.axis_index(pick) == 0, lines[1], lines[0]).astype(BF16)
    else:
        outs[0][...] = lines[0].astype(BF16)
        outs[1][...] = lines[1].astype(BF16)


def strip_kernel(rows, shards, got_a, got_b, enc, *refs):
    out, at = refs[-1], rows
    out[0:rows, :] = pose(shards, got_b, enc, False).astype(BF16)
    for ref in refs[:-1]:
        out[at : at + ref.shape[0], :] = ref[...]
        at += ref.shape[0]


def relay_kernel(strip, far_a, out):
    size = strip.shape[0]
    out[0:size, :] = strip[...]
    out[size:, :] = far_a[...]


def neighbours(rows, cols, shards, pick, enc, strip, raw_a):
    extra = cols + 16
    size = extra if pick else 2 * extra
    lines = strip[rows : rows + size, :].astype(F32)
    if pick:
        first = lax.axis_index(pick) == 0
        zero = jnp.zeros_like(lines)
        both = jnp.where(first, zero, lines), jnp.where(first, lines, zero)
    else:
        both = lines[0:extra], lines[extra:]
    before, after = (
        jnp.concatenate([x[cols : cols + 1], x[0:cols], x[cols + 1 : cols + 2]], axis=0) for x in both
    )
    posed_a = pose(shards, raw_a, enc, True).astype(BF16).astype(F32)
    return posed_a, strip[0:rows, :].astype(F32), before, after


def where_of(k, chan):
    index = jnp.bitwise_xor(lax.axis_index("src"), k)
    return lax.div(index, 2), pl.multiple_of(lax.rem(index, 2) * chan, chan)


def inside(rows, cols, k, coords, view, enc, weights, base_in, base, joined, panel):
    weight = blend_weight(coords, jnp.bitwise_xor(lax.axis_index("src"), k))
    chan, width = view.shape[1], joined.shape[1]
    pixels = rows * cols
    for h in range(rows):
        here = slice(h * cols, (h + 1) * cols)
        posed = (view[here, :].astype(F32) + enc[h : h + 1, :]).astype(BF16)
        part = weight * posed.astype(F32)
        base[here, :] = part if base_in is None else base_in[here, :] + part
        panel[here, :] = posed
    group, at = where_of(k, chan)
    kernel = jnp.concatenate(
        [weights[group, 3 * a + b, pl.ds(at, chan), :] for b in range(3) for a in range(3)], axis=1
    )
    size = pixels // BLOCKS
    taps = jnp.concatenate(
        [
            jnp.dot(panel[i * size : (i + 1) * size, :], kernel, preferred_element_type=F32)
            for i in range(BLOCKS)
        ],
        axis=0,
    )
    column = lax.rem(lax.broadcasted_iota(jnp.int32, (pixels, width), 0), cols)
    zero = jnp.zeros((cols, width), F32)
    total = joined[...]
    for b in (1, 0, 2):
        up, level, down = (taps[:, (3 * b + a) * width : (3 * b + a + 1) * width] for a in range(3))
        part = level + jnp.concatenate([zero, up[: pixels - cols]], axis=0)
        part = part + jnp.concatenate([down[cols:], zero], axis=0)
        if b == 0:
            part = jnp.where(column == 0, 0.0, pltpu.roll(part, 1, 0))
        if b == 2:
            part = jnp.where(column == cols - 1, 0.0, pltpu.roll(part, pixels - 1, 0))
        total = total + part
    joined[...] = total


def add_line(joined, where, line, weights, group, at, taps):
    chan, count = line.shape[1], line.shape[0] - 2
    wide = jnp.concatenate([line[i : i + count] for i in range(3)], axis=1).astype(BF16)
    kernel = jnp.concatenate([weights[group, tap, pl.ds(at, chan), :] for tap in taps], axis=0)
    joined[where, :] += jnp.dot(wide, kernel, preferred_element_type=F32)


def add_columns(rows, cols, joined, weights, a, a_view, b, b_view):
    even = lax.rem(lax.axis_index("shard"), 2) == 0
    chan = a.shape[1]
    group, at_a = where_of(a_view, chan)
    at_b = where_of(b_view, chan)[1]
    zero = jnp.zeros((1, chan), F32)
    left, right = sides(a, b)
    at_left = pl.multiple_of(jnp.where(even, at_b, at_a), chan)
    at_right = pl.multiple_of(jnp.where(even, at_a, at_b), chan)
    for side, tap, start, at in ((left, 0, 0, at_left), (right, 2, cols - 1, at_right)):
        line = jnp.concatenate([zero, side, zero], axis=0)
        where = pl.ds(start, rows, stride=cols)
        add_line(joined, where, line, weights, group, at, [3 * i + tap for i in range(3)])


def add_rows(rows, cols, pick, joined, weights, view, before, after):
    group, at = where_of(view, before.shape[1])
    if pick:
        first = lax.axis_index(pick) == 0
        places = [(before + after, jnp.where(first, rows - 1, 0), jnp.where(first, 6, 0))]
    else:
        places = [(before, 0, 0), (after, rows - 1, 6)]
    for line, h, tap in places:
        where = pl.ds(pl.multiple_of(h * cols, cols), cols)
        add_line(joined, where, line, weights, group, at, [tap + i for i in range(3)])


def silu(x):
    return x / (1.0 + jnp.exp(-x))


def own_kernel(rows, cols, shards, pick, coords, own, enc, strip, got_a, weights, base, joined, panel):
    a, b, before, after = neighbours(rows, cols, shards, pick, enc, strip, got_a)
    joined[...] = jnp.zeros_like(joined)
    inside(rows, cols, 0, coords, own, enc, weights, None, base, joined, panel)
    add_columns(rows, cols, joined, weights, a, 0, b, 0)
    add_rows(rows, cols, pick, joined, weights, 0, before, after)


def middle_kernel(rows, cols, shards, pick, coords, near, far, enc, near_strip, last_strip, near_a,
                  far_a, weights, base_in, joined_in, base, joined, panel):
    me = lax.axis_index("src")
    width = joined.shape[1]
    a, b, before, after = neighbours(rows, cols, shards, pick, enc, near_strip, near_a)
    joined[...] = joined_in[...]
    inside(rows, cols, 1, coords, near, enc, weights, base_in, base, joined, panel)
    add_columns(rows, cols, joined, weights, a, 1, b, 1)
    add_rows(rows, cols, pick, joined, weights, 1, before, after)
    here = pl.ds(pl.multiple_of(lax.div(me, 2) * width, width), width)
    base[:, here] = base[:, here] + silu(joined[...])
    a, b, before, after = neighbours(rows, cols, shards, pick, enc, last_strip, far_a)
    joined[...] = jnp.zeros_like(joined)
    inside(rows, cols, 3, coords, far, enc, weights, base, base, joined, panel)
    add_columns(rows, cols, joined, weights, a, 3, b, 2)
    add_rows(rows, cols, pick, joined, weights, 2, before, after)


def last_kernel(rows, cols, coords, last, enc, weights, base_in, joined_in, base, joined, panel):
    joined[...] = joined_in[...]
    inside(rows, cols, 2, coords, last, enc, weights, base_in, base, joined, panel)


def rim_kernel(rows, cols, shards, pick, enc, relayed, weights, base, joined_in, out, joined):
    chan, width = out.shape[1], joined.shape[1]
    size = relayed.shape[0] - rows
    last_a, b, before, after = neighbours(
        rows, cols, shards, pick, enc, relayed.at[0:size], relayed.at[size : size + rows]
    )
    joined[...] = joined_in[...]
    add_columns(rows, cols, joined, weights, last_a, 2, b, 3)
    add_rows(rows, cols, pick, joined, weights, 3, before, after)
    group = where_of(2, chan)[0]
    added = silu(joined[...])
    for c, lanes in tiles(chan):
        here = group == c * LANES // width
        out[:, lanes] = (base[:, lanes] + jnp.where(here, added, 0.0)).astype(BF16)


def shape(rows, chan, dtype=BF16):
    return jax.ShapeDtypeStruct((rows, chan), dtype)


def call(kernel, ins, outs, scratch=(), cost=None):
    return pl.pallas_call(
        kernel,
        out_shape=outs,
        in_specs=[VMEM_SPEC] * len(ins),
        out_specs=jax.tree.map(lambda _: VMEM_SPEC, outs),
        scratch_shapes=list(scratch),
        compiler_params=pltpu.CompilerParams(vmem_limit_bytes=32 * 1024 * 1024),
        cost_estimate=cost,
    )(*ins)


def local(src_feat, coords, offsets, weights):
    _, rows, cols, chan = src_feat.shape
    pixels = rows * cols
    width = weights.shape[4]
    own = src_feat.reshape(pixels, chan)

    def across(array, k):
        return lax.ppermute(array, "src", [(i, i ^ k) for i in range(4)])

    far = across(own, 3)
    near = across(own, 1)
    rowpos = offsets[0] + jnp.arange(rows, dtype=jnp.int32)
    enc = encoding(rowpos, chan)

    line = shape(rows, chan)
    col_a, col_b, edge_rows, panel = call(
        functools.partial(columns_kernel, rows, cols),
        [own],
        [line, line, shape(2 * cols, chan), shape(pixels, chan)],
        [pltpu.VMEM((chan // LANES, pixels, LANES), F32)],
    )
    place = jnp.broadcast_to(coords.astype(F32).reshape(2, 1), (2, chan))
    shards, slabs = lax.axis_size("shard"), lax.axis_size("slab")

    def swap(array, first):
        pairs = [(i, i + 1) for i in range(first, shards - 1, 2)]
        return lax.ppermute(array, "shard", pairs + [(j, i) for i, j in pairs])

    got_b, got_a = swap(col_b, 1), swap(col_a, 0)
    pick = "slab" if slabs == 2 else None
    edge = shape(cols + 16, chan)
    edges = call(
        functools.partial(edges_kernel, rows, cols, shards, pick),
        [edge_rows, got_a, got_b, enc],
        [edge] if pick else [edge, edge],
    )
    if pick:
        beyond = [lax.ppermute(edges[0], "slab", [(0, 1), (1, 0)])]
    else:
        up = [(i, i + 1) for i in range(slabs - 1)]
        beyond = [
            lax.ppermute(edges[1], "slab", up),
            lax.ppermute(edges[0], "slab", [(j, i) for i, j in up]),
        ]
    strip = call(
        functools.partial(strip_kernel, rows, shards),
        [got_a, got_b, enc, *beyond],
        [shape(rows + len(beyond) * (cols + 16), chan)],
        cost=pl.CostEstimate(flops=2000000000, bytes_accessed=0, transcendentals=0),
    )[0]
    near_strip, last_strip = across(strip, 1), across(strip, 2)
    far, panel = lax.optimization_barrier((far, panel))
    last = across(far, 1)

    def beside(view):
        out = call(
            functools.partial(inner_kernel, rows, cols),
            [view],
            [line],
            [pltpu.VMEM((chan // LANES, pixels, LANES), F32)],
        )[0]
        return swap(out, 0)


    scratch = [pltpu.VMEM((pixels, chan), BF16)]
    sums = [shape(pixels, chan, F32), shape(pixels, width, F32)]
    cost = pl.CostEstimate(flops=5000000000, bytes_accessed=4_000_000, transcendentals=0)
    base, joined = call(
        functools.partial(own_kernel, rows, cols, shards, pick),
        [place, panel, enc, strip, got_a, weights[0]],
        sums,
        scratch,
        cost=cost,
    )
    near, far, base = lax.optimization_barrier((near, far, base))
    far_a, near_a = beside(far), beside(near)
    near_a, far_a, last_strip = lax.optimization_barrier((near_a, far_a, last_strip))
    near_strip, last_strip = lax.optimization_barrier((near_strip, last_strip))
    relayed = call(
        relay_kernel, [last_strip, far_a], [shape(strip.shape[0] + rows, chan)]
    )[0]
    relayed = across(relayed, 1)
    base, joined = call(
        functools.partial(middle_kernel, rows, cols, shards, pick),
        [place, near, far, enc, near_strip, last_strip, near_a, far_a, weights[0], base, joined],
        sums,
        scratch,
        cost=pl.CostEstimate(flops=0, bytes_accessed=0, transcendentals=0),
    )
    base, joined = call(
        functools.partial(last_kernel, rows, cols),
        [place, last, enc, weights[0], base, joined],
        sums,
        scratch,
        cost=pl.CostEstimate(flops=0, bytes_accessed=0, transcendentals=0),
    )
    out = call(
        functools.partial(rim_kernel, rows, cols, shards, pick),
        [enc, relayed, weights[0], base, joined],
        [shape(pixels, chan)],
        [pltpu.VMEM((pixels, width), F32)],
    )[0]
    return out.reshape(1, rows, cols, chan)


def solution(mesh):
    in_specs = (
        P("src", "slab", "shard", None),
        P("src", None),
        P("slab"),
        P("src", None, None, None, None),
    )
    out_specs = P("src", "slab", "shard", None)
    return jax.shard_map(local, mesh=mesh, in_specs=in_specs, out_specs=out_specs, check_vma=False)
```

```python
import functools
import math

import jax
import jax.numpy as jnp
from jax import lax
from jax.experimental import pallas as pl
from jax.experimental.pallas import tpu as pltpu
from jax.sharding import PartitionSpec as P

BF16, F32 = jnp.bfloat16, jnp.float32
VMEM_SPEC = pl.BlockSpec(memory_space=pltpu.VMEM)
LANES = 128
BLOCKS = 4


def encoding(rowpos, chan_count):
    channel_idx = jnp.arange(chan_count, dtype=jnp.int32)
    halves = (channel_idx // 2).astype(F32)
    frequency = jnp.exp(-math.log(1000.0) * halves / (chan_count / 2))
    phases = (channel_idx % 2).astype(F32) * (math.pi / 2)
    return jnp.sin(rowpos.astype(F32)[:, None] * frequency[None, :] + phases[None, :])


def blend_weight(coords, view_index):
    vertical, across = coords[0:1, :] / 6.0, coords[1:2, :] / 6.0
    low, left = lax.div(view_index, 2) == 0, lax.rem(view_index, 2) == 0
    return jnp.where(low, 1.0 - vertical, vertical) * jnp.where(left, 1.0 - across, across)


def tiles(chan):
    return [(c, slice(c * LANES, (c + 1) * LANES)) for c in range(chan // LANES)]


def column(rows, cols, view, wide, pick_last):
    for c, lanes in tiles(view.shape[1]):
        wide[c] = view[:, lanes].astype(F32)
        first = wide[c, pl.ds(0, rows, stride=cols), :]
        last = wide[c, pl.ds(cols - 1, rows, stride=cols), :]
        yield lanes, jnp.where(pick_last, last, first), jnp.where(pick_last, first, last)


def columns_kernel(rows, cols, view, col_a, col_b, edge_rows, panel, wide):
    even = lax.rem(lax.axis_index("shard"), 2) == 0
    for lanes, a, b in column(rows, cols, view, wide, even):
        col_a[:, lanes] = a.astype(BF16)
        col_b[:, lanes] = b.astype(BF16)
    edge_rows[0:cols, :] = view[0:cols, :]
    edge_rows[cols : 2 * cols, :] = view[(rows - 1) * cols :, :]
    panel[...] = view[...]


def inner_kernel(rows, cols, view, out, wide):
    even = lax.rem(lax.axis_index("shard"), 2) == 0
    for lanes, a, _ in column(rows, cols, view, wide, even):
        out[:, lanes] = a.astype(BF16)


def pose(shards, raw, enc, is_a):
    me = lax.axis_index("shard")
    is_left = (lax.rem(me, 2) == 0) != is_a
    inside = jnp.where(is_left, me > 0, me < shards - 1)
    return jnp.where(inside, raw[...].astype(F32) + enc[...], 0.0)


def sides(a, b):
    even = lax.rem(lax.axis_index("shard"), 2) == 0
    return jnp.where(even, b, a), jnp.where(even, a, b)


def corners(left, right, at):
    fill = jnp.zeros((6, left.shape[1]), F32)
    return jnp.concatenate([left[at : at + 1], right[at : at + 1], fill], axis=0)


def edges_kernel(rows, cols, shards, pick, edge_rows, got_a, got_b, enc, *outs):
    left, right = sides(pose(shards, got_a, enc, True), pose(shards, got_b, enc, False))
    lines = []
    for i, h in ((0, 0), (1, rows - 1)):
        row = edge_rows[i * cols : (i + 1) * cols, :].astype(F32) + enc[h : h + 1, :]
        lines.append(jnp.concatenate([row, corners(left, right, h)], axis=0))
    if pick:
        outs[0][...] = jnp.where(lax.axis_index(pick) == 0, lines[1], lines[0]).astype(BF16)
    else:
        outs[0][...] = lines[0].astype(BF16)
        outs[1][...] = lines[1].astype(BF16)


def strip_kernel(rows, shards, got_a, got_b, enc, *refs):
    out, at = refs[-1], rows
    out[0:rows, :] = pose(shards, got_b, enc, False).astype(BF16)
    for ref in refs[:-1]:
        out[at : at + ref.shape[0], :] = ref[...]
        at += ref.shape[0]


def relay_kernel(strip, far_a, out):
    rows = far_a.shape[0]
    out[0:rows, :] = far_a[...]
    out[rows:, :] = strip[0 : out.shape[0] - rows, :]


def neighbours(rows, cols, shards, pick, enc, strip, raw_a):
    extra = cols + 8
    size = extra if pick else 2 * extra
    lines = strip[rows : rows + size, :].astype(F32)
    if pick:
        first = lax.axis_index(pick) == 0
        zero = jnp.zeros_like(lines)
        both = jnp.where(first, zero, lines), jnp.where(first, lines, zero)
    else:
        both = lines[0:extra], lines[extra:]
    before, after = (
        jnp.concatenate([x[cols : cols + 1], x[0:cols], x[cols + 1 : cols + 2]], axis=0) for x in both
    )
    posed_a = pose(shards, raw_a, enc, True).astype(BF16).astype(F32)
    return posed_a, strip[0:rows, :].astype(F32), before, after


def where_of(k, chan):
    index = jnp.bitwise_xor(lax.axis_index("src"), k)
    return lax.div(index, 2), pl.multiple_of(lax.rem(index, 2) * chan, chan)


def inside(rows, cols, k, coords, view, enc, weights, base_in, base, joined, panel):
    weight = blend_weight(coords, jnp.bitwise_xor(lax.axis_index("src"), k))
    chan, width = view.shape[1], joined.shape[1]
    pixels = rows * cols
    for h in range(rows):
        here = slice(h * cols, (h + 1) * cols)
        posed = (view[here, :].astype(F32) + enc[h : h + 1, :]).astype(BF16)
        part = weight * posed.astype(F32)
        base[here, :] = part if base_in is None else base_in[here, :] + part
        panel[here, :] = posed
    group, at = where_of(k, chan)
    kernel = jnp.concatenate(
        [weights[group, 3 * a + b, pl.ds(at, chan), :] for b in range(3) for a in range(3)], axis=1
    )
    size = pixels // BLOCKS
    taps = jnp.concatenate(
        [
            jnp.dot(panel[i * size : (i + 1) * size, :], kernel, preferred_element_type=F32)
            for i in range(BLOCKS)
        ],
        axis=0,
    )
    column = lax.rem(lax.broadcasted_iota(jnp.int32, (pixels, width), 0), cols)
    zero = jnp.zeros((cols, width), F32)
    total = joined[...]
    for b in (1, 0, 2):
        up, level, down = (taps[:, (3 * b + a) * width : (3 * b + a + 1) * width] for a in range(3))
        part = level + jnp.concatenate([zero, up[: pixels - cols]], axis=0)
        part = part + jnp.concatenate([down[cols:], zero], axis=0)
        if b == 0:
            part = jnp.where(column == 0, 0.0, pltpu.roll(part, 1, 0))
        if b == 2:
            part = jnp.where(column == cols - 1, 0.0, pltpu.roll(part, pixels - 1, 0))
        total = total + part
    joined[...] = total


def add_line(joined, where, line, weights, group, at, taps):
    chan, count = line.shape[1], line.shape[0] - 2
    wide = jnp.concatenate([line[i : i + count] for i in range(3)], axis=1).astype(BF16)
    kernel = jnp.concatenate([weights[group, tap, pl.ds(at, chan), :] for tap in taps], axis=0)
    joined[where, :] += jnp.dot(wide, kernel, preferred_element_type=F32)


def add_columns(rows, cols, joined, weights, a, a_view, b, b_view):
    even = lax.rem(lax.axis_index("shard"), 2) == 0
    chan = a.shape[1]
    group, at_a = where_of(a_view, chan)
    at_b = where_of(b_view, chan)[1]
    zero = jnp.zeros((1, chan), F32)
    left, right = sides(a, b)
    at_left = pl.multiple_of(jnp.where(even, at_b, at_a), chan)
    at_right = pl.multiple_of(jnp.where(even, at_a, at_b), chan)
    for side, tap, start, at in ((left, 0, 0, at_left), (right, 2, cols - 1, at_right)):
        line = jnp.concatenate([zero, side, zero], axis=0)
        where = pl.ds(start, rows, stride=cols)
        add_line(joined, where, line, weights, group, at, [3 * i + tap for i in range(3)])


def add_rows(rows, cols, pick, joined, weights, view, before, after):
    group, at = where_of(view, before.shape[1])
    if pick:
        first = lax.axis_index(pick) == 0
        places = [(before + after, jnp.where(first, rows - 1, 0), jnp.where(first, 6, 0))]
    else:
        places = [(before, 0, 0), (after, rows - 1, 6)]
    for line, h, tap in places:
        where = pl.ds(pl.multiple_of(h * cols, cols), cols)
        add_line(joined, where, line, weights, group, at, [tap + i for i in range(3)])


def silu(x):
    return x / (1.0 + jnp.exp(-x))


def own_kernel(rows, cols, shards, pick, coords, own, enc, strip, got_a, weights, base, joined, panel):
    a, b, before, after = neighbours(rows, cols, shards, pick, enc, strip, got_a)
    joined[...] = jnp.zeros_like(joined)
    inside(rows, cols, 0, coords, own, enc, weights, None, base, joined, panel)
    add_columns(rows, cols, joined, weights, a, 0, b, 0)
    add_rows(rows, cols, pick, joined, weights, 0, before, after)


def middle_kernel(rows, cols, shards, pick, coords, near, far, enc, near_strip, last_strip, near_a,
                  far_a, weights, base_in, joined_in, base, joined, panel):
    me = lax.axis_index("src")
    width = joined.shape[1]
    a, b, before, after = neighbours(rows, cols, shards, pick, enc, near_strip, near_a)
    joined[...] = joined_in[...]
    inside(rows, cols, 1, coords, near, enc, weights, base_in, base, joined, panel)
    add_columns(rows, cols, joined, weights, a, 1, b, 1)
    add_rows(rows, cols, pick, joined, weights, 1, before, after)
    here = pl.ds(pl.multiple_of(lax.div(me, 2) * width, width), width)
    base[:, here] = base[:, here] + silu(joined[...])
    a, b, before, after = neighbours(rows, cols, shards, pick, enc, last_strip, far_a)
    joined[...] = jnp.zeros_like(joined)
    inside(rows, cols, 3, coords, far, enc, weights, base, base, joined, panel)
    add_columns(rows, cols, joined, weights, a, 3, b, 2)
    add_rows(rows, cols, pick, joined, weights, 2, before, after)


def last_kernel(rows, cols, coords, last, enc, weights, base_in, joined_in, base, joined, panel):
    joined[...] = joined_in[...]
    inside(rows, cols, 2, coords, last, enc, weights, base_in, base, joined, panel)


def rim_kernel(rows, cols, shards, pick, enc, relayed, weights, base, joined_in, out, joined):
    chan, width = out.shape[1], joined.shape[1]
    last_a, b, before, after = neighbours(
        rows, cols, shards, pick, enc, relayed[rows:, :], relayed[0:rows, :]
    )
    joined[...] = joined_in[...]
    add_columns(rows, cols, joined, weights, last_a, 2, b, 3)
    add_rows(rows, cols, pick, joined, weights, 3, before, after)
    group = where_of(2, chan)[0]
    added = silu(joined[...])
    for c, lanes in tiles(chan):
        here = group == c * LANES // width
        out[:, lanes] = (base[:, lanes] + jnp.where(here, added, 0.0)).astype(BF16)


def shape(rows, chan, dtype=BF16):
    return jax.ShapeDtypeStruct((rows, chan), dtype)


def call(kernel, ins, outs, scratch=(), cost=None):
    return pl.pallas_call(
        kernel,
        out_shape=outs,
        in_specs=[VMEM_SPEC] * len(ins),
        out_specs=jax.tree.map(lambda _: VMEM_SPEC, outs),
        scratch_shapes=list(scratch),
        compiler_params=pltpu.CompilerParams(vmem_limit_bytes=32 * 1024 * 1024),
        cost_estimate=cost,
    )(*ins)


def local(src_feat, coords, offsets, weights):
    _, rows, cols, chan = src_feat.shape
    pixels = rows * cols
    width = weights.shape[4]
    own = src_feat.reshape(pixels, chan)

    def across(array, k):
        return lax.ppermute(array, "src", [(i, i ^ k) for i in range(4)])

    far = across(own, 3)
    near = across(own, 1)
    rowpos = offsets[0] + jnp.arange(rows, dtype=jnp.int32)
    enc = encoding(rowpos, chan)

    line = shape(rows, chan)
    col_a, col_b, edge_rows, panel = call(
        functools.partial(columns_kernel, rows, cols),
        [own],
        [line, line, shape(2 * cols, chan), shape(pixels, chan)],
        [pltpu.VMEM((chan // LANES, pixels, LANES), F32)],
    )
    place = jnp.broadcast_to(coords.astype(F32).reshape(2, 1), (2, chan))
    shards, slabs = lax.axis_size("shard"), lax.axis_size("slab")

    def swap(array, first):
        pairs = [(i, i + 1) for i in range(first, shards - 1, 2)]
        return lax.ppermute(array, "shard", pairs + [(j, i) for i, j in pairs])

    got_b, got_a = swap(col_b, 1), swap(col_a, 0)
    pick = "slab" if slabs == 2 else None
    edge = shape(cols + 8, chan)
    edges = call(
        functools.partial(edges_kernel, rows, cols, shards, pick),
        [edge_rows, got_a, got_b, enc],
        [edge] if pick else [edge, edge],
    )
    if pick:
        beyond = [lax.ppermute(edges[0], "slab", [(0, 1), (1, 0)])]
    else:
        up = [(i, i + 1) for i in range(slabs - 1)]
        beyond = [
            lax.ppermute(edges[1], "slab", up),
            lax.ppermute(edges[0], "slab", [(j, i) for i, j in up]),
        ]
    strip = call(
        functools.partial(strip_kernel, rows, shards),
        [got_a, got_b, enc, *beyond],
        [shape(rows + len(beyond) * (cols + 8), chan)],
        cost=pl.CostEstimate(flops=2_000_000_000, bytes_accessed=0, transcendentals=0),
    )[0]
    near_strip, last_strip = across(strip, 1), across(strip, 2)
    far, panel = lax.optimization_barrier((far, panel))
    last = across(far, 1)

    def beside(view):
        out = call(
            functools.partial(inner_kernel, rows, cols),
            [view],
            [line],
            [pltpu.VMEM((chan // LANES, pixels, LANES), F32)],
        )[0]
        return swap(out, 0)


    scratch = [pltpu.VMEM((pixels, chan), BF16)]
    sums = [shape(pixels, chan, F32), shape(pixels, width, F32)]
    cost = pl.CostEstimate(flops=5000000000, bytes_accessed=4_000_000, transcendentals=0)
    base, joined = call(
        functools.partial(own_kernel, rows, cols, shards, pick),
        [place, panel, enc, strip, got_a, weights[0]],
        sums,
        scratch,
        cost=cost,
    )
    near, far, base = lax.optimization_barrier((near, far, base))
    far_a, near_a = beside(far), beside(near)
    near_a, far_a, last_strip = lax.optimization_barrier((near_a, far_a, last_strip))
    near_strip, last_strip = lax.optimization_barrier((near_strip, last_strip))
    relayed = call(
        relay_kernel, [last_strip, far_a], [shape(strip.shape[0] + rows, chan)]
    )[0]
    relayed = across(relayed, 1)
    base, joined = call(
        functools.partial(middle_kernel, rows, cols, shards, pick),
        [place, near, far, enc, near_strip, last_strip, near_a, far_a, weights[0], base, joined],
        sums,
        scratch,
        cost=pl.CostEstimate(flops=0, bytes_accessed=0, transcendentals=0),
    )
    base, joined = call(
        functools.partial(last_kernel, rows, cols),
        [place, last, enc, weights[0], base, joined],
        sums,
        scratch,
        cost=pl.CostEstimate(flops=0, bytes_accessed=0, transcendentals=0),
    )
    out = call(
        functools.partial(rim_kernel, rows, cols, shards, pick),
        [enc, relayed, weights[0], base, joined],
        [shape(pixels, chan)],
        [pltpu.VMEM((pixels, width), F32)],
    )[0]
    return out.reshape(1, rows, cols, chan)


def solution(mesh):
    in_specs = (
        P("src", "slab", "shard", None),
        P("src", None),
        P("slab"),
        P("src", None, None, None, None),
    )
    out_specs = P("src", "slab", "shard", None)
    return jax.shard_map(local, mesh=mesh, in_specs=in_specs, out_specs=out_specs, check_vma=False)
```

```python
import functools
import math

import jax
import jax.numpy as jnp
from jax import lax
from jax.experimental import pallas as pl
from jax.experimental.pallas import tpu as pltpu
from jax.sharding import PartitionSpec as P

BF16, F32 = jnp.bfloat16, jnp.float32
VMEM_SPEC = pl.BlockSpec(memory_space=pltpu.VMEM)
LANES = 128
BLOCKS = 4


def encoding(rowpos, chan_count):
    channel_idx = jnp.arange(chan_count, dtype=jnp.int32)
    halves = (channel_idx // 2).astype(F32)
    frequency = jnp.exp(-math.log(1000.0) * halves / (chan_count / 2))
    phases = (channel_idx % 2).astype(F32) * (math.pi / 2)
    return jnp.sin(rowpos.astype(F32)[:, None] * frequency[None, :] + phases[None, :])


def blend_weight(coords, view_index):
    vertical, across = coords[0:1, :] / 6.0, coords[1:2, :] / 6.0
    low, left = lax.div(view_index, 2) == 0, lax.rem(view_index, 2) == 0
    return jnp.where(low, 1.0 - vertical, vertical) * jnp.where(left, 1.0 - across, across)


def tiles(chan):
    return [(c, slice(c * LANES, (c + 1) * LANES)) for c in range(chan // LANES)]


def column(rows, cols, view, wide, pick_last):
    for c, lanes in tiles(view.shape[1]):
        wide[c, 0 : rows * cols, :] = view[:, lanes].astype(F32)
        first = wide[c, pl.ds(0, rows, stride=cols), :]
        last = wide[c, pl.ds(cols - 1, rows, stride=cols), :]
        yield lanes, jnp.where(pick_last, last, first), jnp.where(pick_last, first, last)


def columns_kernel(rows, cols, view, col_a, col_b, edge_rows, panel, wide):
    even = lax.rem(lax.axis_index("shard"), 2) == 0
    for lanes, a, b in column(rows, cols, view, wide, even):
        col_a[:, lanes] = a.astype(BF16)
        col_b[:, lanes] = b.astype(BF16)
    edge_rows[0:cols, :] = view[0:cols, :]
    edge_rows[cols : 2 * cols, :] = view[(rows - 1) * cols :, :]
    panel[...] = view[...]


def inner_kernel(rows, cols, view, out, wide):
    even = lax.rem(lax.axis_index("shard"), 2) == 0
    for lanes, a, _ in column(rows, cols, view, wide, even):
        out[:, lanes] = a.astype(BF16)


def pose(shards, raw, enc, is_a):
    me = lax.axis_index("shard")
    is_left = (lax.rem(me, 2) == 0) != is_a
    inside = jnp.where(is_left, me > 0, me < shards - 1)
    return jnp.where(inside, raw[...].astype(F32) + enc[...], 0.0)


def sides(a, b):
    even = lax.rem(lax.axis_index("shard"), 2) == 0
    return jnp.where(even, b, a), jnp.where(even, a, b)


def corners(left, right, at):
    fill = jnp.zeros((6, left.shape[1]), F32)
    return jnp.concatenate([left[at : at + 1], right[at : at + 1], fill], axis=0)


def edges_kernel(rows, cols, shards, pick, edge_rows, got_a, got_b, enc, *outs):
    left, right = sides(pose(shards, got_a, enc, True), pose(shards, got_b, enc, False))
    lines = []
    for i, h in ((0, 0), (1, rows - 1)):
        row = edge_rows[i * cols : (i + 1) * cols, :].astype(F32) + enc[h : h + 1, :]
        lines.append(jnp.concatenate([row, corners(left, right, h)], axis=0))
    if pick:
        outs[0][...] = jnp.where(lax.axis_index(pick) == 0, lines[1], lines[0]).astype(BF16)
    else:
        outs[0][...] = lines[0].astype(BF16)
        outs[1][...] = lines[1].astype(BF16)


def strip_kernel(rows, shards, got_a, got_b, enc, *refs):
    out, at = refs[-1], rows
    out[0:rows, :] = pose(shards, got_b, enc, False).astype(BF16)
    for ref in refs[:-1]:
        out[at : at + ref.shape[0], :] = ref[...]
        at += ref.shape[0]


def relay_kernel(strip, far_a, out):
    rows = far_a.shape[0]
    out[0:rows, :] = far_a[...]
    out[rows:, :] = strip[0 : out.shape[0] - rows, :]


def neighbours(rows, cols, shards, pick, enc, strip, raw_a):
    extra = cols + 8
    size = extra if pick else 2 * extra
    lines = strip[rows : rows + size, :].astype(F32)
    if pick:
        first = lax.axis_index(pick) == 0
        zero = jnp.zeros_like(lines)
        both = jnp.where(first, zero, lines), jnp.where(first, lines, zero)
    else:
        both = lines[0:extra], lines[extra:]
    before, after = (
        jnp.concatenate([x[cols : cols + 1], x[0:cols], x[cols + 1 : cols + 2]], axis=0) for x in both
    )
    posed_a = pose(shards, raw_a, enc, True).astype(BF16).astype(F32)
    return posed_a, strip[0:rows, :].astype(F32), before, after


def where_of(k, chan):
    index = jnp.bitwise_xor(lax.axis_index("src"), k)
    return lax.div(index, 2), pl.multiple_of(lax.rem(index, 2) * chan, chan)


def inside(rows, cols, k, coords, view, enc, weights, base_in, base, sums, panel):
    weight = blend_weight(coords, jnp.bitwise_xor(lax.axis_index("src"), k))
    chan, width = view.shape[1], sums.shape[1]
    pixels = rows * cols
    for h in range(rows):
        here = slice(h * cols, (h + 1) * cols)
        posed = (view[here, :].astype(F32) + enc[h : h + 1, :]).astype(BF16)
        part = weight * posed.astype(F32)
        base[here, :] = part if base_in is None else base_in[here, :] + part
        panel[here, :] = posed
    group, at = where_of(k, chan)
    kernel = jnp.concatenate(
        [weights[group, 3 * a + b, pl.ds(at, chan), :] for b in range(3) for a in range(3)], axis=1
    )
    size = pixels // BLOCKS
    taps = jnp.concatenate(
        [
            jnp.dot(panel[i * size : (i + 1) * size, :], kernel, preferred_element_type=F32)
            for i in range(BLOCKS)
        ],
        axis=0,
    )
    column = lax.rem(lax.broadcasted_iota(jnp.int32, (pixels, width), 0), cols)
    zero = jnp.zeros((cols, width), F32)
    total = sums[0:pixels, :]
    for b in (1, 0, 2):
        up, level, down = (taps[:, (3 * b + a) * width : (3 * b + a + 1) * width] for a in range(3))
        part = level + jnp.concatenate([zero, up[: pixels - cols]], axis=0)
        part = part + jnp.concatenate([down[cols:], zero], axis=0)
        if b == 0:
            part = jnp.where(column == 0, 0.0, pltpu.roll(part, 1, 0))
        if b == 2:
            part = jnp.where(column == cols - 1, 0.0, pltpu.roll(part, pixels - 1, 0))
        total = total + part
    sums[0:pixels, :] = total


def add_line(sums, where, line, weights, group, at, taps):
    chan, count = line.shape[1], line.shape[0] - 2
    wide = jnp.concatenate([line[i : i + count] for i in range(3)], axis=1).astype(BF16)
    kernel = jnp.concatenate([weights[group, tap, pl.ds(at, chan), :] for tap in taps], axis=0)
    sums[where, :] += jnp.dot(wide, kernel, preferred_element_type=F32)


def add_columns(rows, cols, sums, weights, a, a_view, b, b_view):
    even = lax.rem(lax.axis_index("shard"), 2) == 0
    chan = a.shape[1]
    group, at_a = where_of(a_view, chan)
    at_b = where_of(b_view, chan)[1]
    zero = jnp.zeros((1, chan), F32)
    left, right = sides(a, b)
    at_left = pl.multiple_of(jnp.where(even, at_b, at_a), chan)
    at_right = pl.multiple_of(jnp.where(even, at_a, at_b), chan)
    for side, tap, start, at in ((left, 0, 0, at_left), (right, 2, cols - 1, at_right)):
        line = jnp.concatenate([zero, side, zero], axis=0)
        where = pl.ds(start, rows, stride=cols)
        add_line(sums, where, line, weights, group, at, [3 * i + tap for i in range(3)])


def add_rows(rows, cols, pick, sums, weights, view, before, after):
    group, at = where_of(view, before.shape[1])
    if pick:
        first = lax.axis_index(pick) == 0
        places = [(before + after, jnp.where(first, rows - 1, 0), jnp.where(first, 6, 0))]
    else:
        places = [(before, 0, 0), (after, rows - 1, 6)]
    for line, h, tap in places:
        where = pl.ds(pl.multiple_of(h * cols, cols), cols)
        add_line(sums, where, line, weights, group, at, [tap + i for i in range(3)])


def silu(x):
    return x / (1.0 + jnp.exp(-x))


def own_kernel(rows, cols, shards, pick, coords, own, enc, strip, got_a, weights, base, joined, panel):
    a, b, before, after = neighbours(rows, cols, shards, pick, enc, strip, got_a)
    joined[...] = jnp.zeros_like(joined)
    inside(rows, cols, 0, coords, own, enc, weights, None, base, joined, panel)
    add_columns(rows, cols, joined, weights, a, 0, b, 0)
    add_rows(rows, cols, pick, joined, weights, 0, before, after)


def middle_kernel(rows, cols, shards, pick, coords, near, far, enc, near_strip, last_strip, near_a,
                  far_a, weights, base_in, joined_in, base, joined, panel):
    me = lax.axis_index("src")
    width = joined.shape[1]
    a, b, before, after = neighbours(rows, cols, shards, pick, enc, near_strip, near_a)
    joined[...] = joined_in[...]
    inside(rows, cols, 1, coords, near, enc, weights, base_in, base, joined, panel)
    add_columns(rows, cols, joined, weights, a, 1, b, 1)
    add_rows(rows, cols, pick, joined, weights, 1, before, after)
    here = pl.ds(pl.multiple_of(lax.div(me, 2) * width, width), width)
    base[:, here] = base[:, here] + silu(joined[0 : rows * cols, :])
    a, b, before, after = neighbours(rows, cols, shards, pick, enc, last_strip, far_a)
    joined[...] = jnp.zeros_like(joined)
    inside(rows, cols, 3, coords, far, enc, weights, base, base, joined, panel)
    add_columns(rows, cols, joined, weights, a, 3, b, 2)
    add_rows(rows, cols, pick, joined, weights, 2, before, after)


def last_kernel(rows, cols, coords, last, enc, weights, base_in, joined_in, base, joined, panel):
    joined[...] = joined_in[...]
    inside(rows, cols, 2, coords, last, enc, weights, base_in, base, joined, panel)


def rim_kernel(rows, cols, shards, pick, enc, relayed, weights, base, joined_in, out, joined):
    chan, width = out.shape[1], joined.shape[1]
    last_a, b, before, after = neighbours(
        rows, cols, shards, pick, enc, relayed[rows:, :], relayed[0:rows, :]
    )
    joined[...] = joined_in[...]
    add_columns(rows, cols, joined, weights, last_a, 2, b, 3)
    add_rows(rows, cols, pick, joined, weights, 3, before, after)
    group = where_of(2, chan)[0]
    added = silu(joined[0 : rows * cols, :])
    for c, lanes in tiles(chan):
        here = group == c * LANES // width
        out[:, lanes] = (base[:, lanes] + jnp.where(here, added, 0.0)).astype(BF16)


def shape(rows, chan, dtype=BF16):
    return jax.ShapeDtypeStruct((rows, chan), dtype)


def call(kernel, ins, outs, scratch=(), cost=None):
    return pl.pallas_call(
        kernel,
        out_shape=outs,
        in_specs=[VMEM_SPEC] * len(ins),
        out_specs=jax.tree.map(lambda _: VMEM_SPEC, outs),
        scratch_shapes=list(scratch),
        compiler_params=pltpu.CompilerParams(vmem_limit_bytes=32 * 1024 * 1024),
        cost_estimate=cost,
    )(*ins)


def local(src_feat, coords, offsets, weights):
    _, rows, cols, chan = src_feat.shape
    pixels = rows * cols
    width = weights.shape[4]
    own = src_feat.reshape(pixels, chan)

    def across(array, k):
        return lax.ppermute(array, "src", [(i, i ^ k) for i in range(4)])

    far = across(own, 3)
    near = across(own, 1)
    rowpos = offsets[0] + jnp.arange(rows, dtype=jnp.int32)
    enc = encoding(rowpos, chan)

    line = shape(rows, chan)
    col_a, col_b, edge_rows, panel = call(
        functools.partial(columns_kernel, rows, cols),
        [own],
        [line, line, shape(2 * cols, chan), shape(pixels, chan)],
        [pltpu.VMEM((chan // LANES, pixels + cols, LANES), F32)],
    )
    place = jnp.broadcast_to(coords.astype(F32).reshape(2, 1), (2, chan))
    shards, slabs = lax.axis_size("shard"), lax.axis_size("slab")

    def swap(array, first):
        pairs = [(i, i + 1) for i in range(first, shards - 1, 2)]
        return lax.ppermute(array, "shard", pairs + [(j, i) for i, j in pairs])

    got_b, got_a = swap(col_b, 1), swap(col_a, 0)
    pick = "slab" if slabs == 2 else None
    edge = shape(cols + 8, chan)
    edges = call(
        functools.partial(edges_kernel, rows, cols, shards, pick),
        [edge_rows, got_a, got_b, enc],
        [edge] if pick else [edge, edge],
    )
    if pick:
        beyond = [lax.ppermute(edges[0], "slab", [(0, 1), (1, 0)])]
    else:
        up = [(i, i + 1) for i in range(slabs - 1)]
        beyond = [
            lax.ppermute(edges[1], "slab", up),
            lax.ppermute(edges[0], "slab", [(j, i) for i, j in up]),
        ]
    strip = call(
        functools.partial(strip_kernel, rows, shards),
        [got_a, got_b, enc, *beyond],
        [shape(rows + len(beyond) * (cols + 8), chan)],
        cost=pl.CostEstimate(flops=2_000_000_000, bytes_accessed=0, transcendentals=0),
    )[0]
    near_strip, last_strip = across(strip, 1), across(strip, 2)
    far, panel = lax.optimization_barrier((far, panel))
    last = across(far, 1)

    def beside(view):
        out = call(
            functools.partial(inner_kernel, rows, cols),
            [view],
            [line],
            [pltpu.VMEM((chan // LANES, pixels + cols, LANES), F32)],
        )[0]
        return swap(out, 0)


    scratch = [pltpu.VMEM((pixels, chan), BF16)]
    sums = [shape(pixels, chan, F32), shape(pixels + cols, width, F32)]
    cost = pl.CostEstimate(flops=5000000000, bytes_accessed=4_000_000, transcendentals=0)
    base, joined = call(
        functools.partial(own_kernel, rows, cols, shards, pick),
        [place, panel, enc, strip, got_a, weights[0]],
        sums,
        scratch,
        cost=cost,
    )
    near, far, base = lax.optimization_barrier((near, far, base))
    far_a, near_a = beside(far), beside(near)
    near_a, far_a, last_strip = lax.optimization_barrier((near_a, far_a, last_strip))
    near_strip, last_strip = lax.optimization_barrier((near_strip, last_strip))
    relayed = call(
        relay_kernel, [last_strip, far_a], [shape(strip.shape[0] + rows, chan)]
    )[0]
    relayed = across(relayed, 1)
    base, joined = call(
        functools.partial(middle_kernel, rows, cols, shards, pick),
        [place, near, far, enc, near_strip, last_strip, near_a, far_a, weights[0], base, joined],
        sums,
        scratch,
        cost=pl.CostEstimate(flops=0, bytes_accessed=0, transcendentals=0),
    )
    base, joined = call(
        functools.partial(last_kernel, rows, cols),
        [place, last, enc, weights[0], base, joined],
        sums,
        scratch,
        cost=pl.CostEstimate(flops=0, bytes_accessed=0, transcendentals=0),
    )
    out = call(
        functools.partial(rim_kernel, rows, cols, shards, pick),
        [enc, relayed, weights[0], base, joined],
        [shape(pixels, chan)],
        [pltpu.VMEM((pixels + cols, width), F32)],
    )[0]
    return out.reshape(1, rows, cols, chan)


def solution(mesh):
    in_specs = (
        P("src", "slab", "shard", None),
        P("src", None),
        P("slab"),
        P("src", None, None, None, None),
    )
    out_specs = P("src", "slab", "shard", None)
    return jax.shard_map(local, mesh=mesh, in_specs=in_specs, out_specs=out_specs, check_vma=False)
```

```python
import functools
import math

import jax
import jax.numpy as jnp
from jax import lax
from jax.experimental import pallas as pl
from jax.experimental.pallas import tpu as pltpu
from jax.sharding import PartitionSpec as P

BF16, F32 = jnp.bfloat16, jnp.float32
VMEM_SPEC = pl.BlockSpec(memory_space=pltpu.VMEM)
LANES = 128
PARTS = 2
BLOCKS = 4


def encoding(rowpos, chan_count):
    channel_idx = jnp.arange(chan_count, dtype=jnp.int32)
    halves = (channel_idx // 2).astype(F32)
    frequency = jnp.exp(-math.log(1000.0) * halves / (chan_count / 2))
    phases = (channel_idx % 2).astype(F32) * (math.pi / 2)
    return jnp.sin(rowpos.astype(F32)[:, None] * frequency[None, :] + phases[None, :])


def blend_weight(coords, view_index):
    vertical, across = coords[0:1, :] / 6.0, coords[1:2, :] / 6.0
    low, left = lax.div(view_index, 2) == 0, lax.rem(view_index, 2) == 0
    return jnp.where(low, 1.0 - vertical, vertical) * jnp.where(left, 1.0 - across, across)


def tiles(chan):
    return [(c, slice(c * LANES, (c + 1) * LANES)) for c in range(chan // LANES)]


def column(rows, cols, view, wide, pick_last):
    for c, lanes in tiles(view.shape[1]):
        wide[c, 0 : rows * cols, :] = view[:, lanes].astype(F32)
        first = wide[c, pl.ds(0, rows, stride=cols), :]
        last = wide[c, pl.ds(cols - 1, rows, stride=cols), :]
        yield lanes, jnp.where(pick_last, last, first), jnp.where(pick_last, first, last)


def columns_kernel(rows, cols, view, col_a, col_b, edge_rows, panel, wide):
    even = lax.rem(lax.axis_index("shard"), 2) == 0
    for lanes, a, b in column(rows, cols, view, wide, even):
        col_a[:, lanes] = a.astype(BF16)
        col_b[:, lanes] = b.astype(BF16)
    edge_rows[0:cols, :] = view[0:cols, :]
    edge_rows[cols : 2 * cols, :] = view[(rows - 1) * cols :, :]
    panel[...] = view[...]


def inner_kernel(rows, cols, view, out, wide):
    even = lax.rem(lax.axis_index("shard"), 2) == 0
    for lanes, a, _ in column(rows, cols, view, wide, even):
        out[:, lanes] = a.astype(BF16)


def pose(shards, raw, enc, is_a):
    me = lax.axis_index("shard")
    is_left = (lax.rem(me, 2) == 0) != is_a
    inside = jnp.where(is_left, me > 0, me < shards - 1)
    return jnp.where(inside, raw[...].astype(F32) + enc[...], 0.0)


def sides(a, b):
    even = lax.rem(lax.axis_index("shard"), 2) == 0
    return jnp.where(even, b, a), jnp.where(even, a, b)


def corners(left, right, at):
    fill = jnp.zeros((6, left.shape[1]), F32)
    return jnp.concatenate([left[at : at + 1], right[at : at + 1], fill], axis=0)


def edges_kernel(rows, cols, shards, pick, edge_rows, got_a, got_b, enc, *outs):
    left, right = sides(pose(shards, got_a, enc, True), pose(shards, got_b, enc, False))
    lines = []
    for i, h in ((0, 0), (1, rows - 1)):
        row = edge_rows[i * cols : (i + 1) * cols, :].astype(F32) + enc[h : h + 1, :]
        lines.append(jnp.concatenate([row, corners(left, right, h)], axis=0))
    if pick:
        outs[0][...] = jnp.where(lax.axis_index(pick) == 0, lines[1], lines[0]).astype(BF16)
    else:
        outs[0][...] = lines[0].astype(BF16)
        outs[1][...] = lines[1].astype(BF16)


def strip_kernel(rows, shards, got_a, got_b, enc, panel, *refs):
    *beyond, out, longer = refs
    at = rows
    out[0:rows, :] = pose(shards, got_b, enc, False).astype(BF16)
    for ref in beyond:
        out[at : at + ref.shape[0], :] = ref[...]
        at += ref.shape[0]
    size = longer.shape[0] - at
    longer[0:size, :] = panel[0:size, :]
    longer[size:, :] = out[...]


def relay_kernel(strip, far_a, out):
    rows = far_a.shape[0]
    out[0:rows, :] = far_a[...]
    out[rows:, :] = strip[strip.shape[0] - (out.shape[0] - rows) :, :]


def neighbours(rows, cols, shards, pick, enc, strip, raw_a):
    extra = cols + 8
    size = extra if pick else 2 * extra
    lines = strip[rows : rows + size, :].astype(F32)
    if pick:
        first = lax.axis_index(pick) == 0
        zero = jnp.zeros_like(lines)
        both = jnp.where(first, zero, lines), jnp.where(first, lines, zero)
    else:
        both = lines[0:extra], lines[extra:]
    before, after = (
        jnp.concatenate([x[cols : cols + 1], x[0:cols], x[cols + 1 : cols + 2]], axis=0) for x in both
    )
    posed_a = pose(shards, raw_a, enc, True).astype(BF16).astype(F32)
    return posed_a, strip[0:rows, :].astype(F32), before, after


def where_of(k, chan):
    index = jnp.bitwise_xor(lax.axis_index("src"), k)
    return lax.div(index, 2), pl.multiple_of(lax.rem(index, 2) * chan, chan)


def inside(rows, cols, k, coords, view, enc, weights, base_in, base, joined, panel):
    weight = blend_weight(coords, jnp.bitwise_xor(lax.axis_index("src"), k))
    chan, width = panel.shape[1], joined.shape[1]
    pixels = rows * cols
    views = view if isinstance(view, tuple) else (view,)
    lines = [part[i : i + cols, :] for part in views for i in range(0, part.shape[0], cols)]
    for h, line in enumerate(lines):
        here = slice(h * cols, (h + 1) * cols)
        posed = (line.astype(F32) + enc[h : h + 1, :]).astype(BF16)
        part = weight * posed.astype(F32)
        base[here, :] = part if base_in is None else base_in[here, :] + part
        panel[here, :] = posed
    group, at = where_of(k, chan)
    kernel = jnp.concatenate(
        [weights[group, 3 * a + b, pl.ds(at, chan), :] for b in range(3) for a in range(3)], axis=1
    )
    size = pixels // BLOCKS
    taps = jnp.concatenate(
        [
            jnp.dot(panel[i * size : (i + 1) * size, :], kernel, preferred_element_type=F32)
            for i in range(BLOCKS)
        ],
        axis=0,
    )
    column = lax.rem(lax.broadcasted_iota(jnp.int32, (pixels, width), 0), cols)
    zero = jnp.zeros((cols, width), F32)
    total = joined[0:pixels, :]
    for b in (1, 0, 2):
        up, level, down = (taps[:, (3 * b + a) * width : (3 * b + a + 1) * width] for a in range(3))
        part = level + jnp.concatenate([zero, up[: pixels - cols]], axis=0)
        part = part + jnp.concatenate([down[cols:], zero], axis=0)
        if b == 0:
            part = jnp.where(column == 0, 0.0, pltpu.roll(part, 1, 0))
        if b == 2:
            part = jnp.where(column == cols - 1, 0.0, pltpu.roll(part, pixels - 1, 0))
        total = total + part
    joined[0:pixels, :] = total


def add_line(joined, where, line, weights, group, at, taps):
    chan, count = line.shape[1], line.shape[0] - 2
    wide = jnp.concatenate([line[i : i + count] for i in range(3)], axis=1).astype(BF16)
    kernel = jnp.concatenate([weights[group, tap, pl.ds(at, chan), :] for tap in taps], axis=0)
    joined[where, :] += jnp.dot(wide, kernel, preferred_element_type=F32)


def add_columns(rows, cols, joined, weights, a, a_view, b, b_view):
    even = lax.rem(lax.axis_index("shard"), 2) == 0
    chan = a.shape[1]
    group, at_a = where_of(a_view, chan)
    at_b = where_of(b_view, chan)[1]
    zero = jnp.zeros((1, chan), F32)
    left, right = sides(a, b)
    at_left = pl.multiple_of(jnp.where(even, at_b, at_a), chan)
    at_right = pl.multiple_of(jnp.where(even, at_a, at_b), chan)
    for side, tap, start, at in ((left, 0, 0, at_left), (right, 2, cols - 1, at_right)):
        line = jnp.concatenate([zero, side, zero], axis=0)
        where = pl.ds(start, rows, stride=cols)
        add_line(joined, where, line, weights, group, at, [3 * i + tap for i in range(3)])


def add_rows(rows, cols, pick, joined, weights, view, before, after):
    group, at = where_of(view, before.shape[1])
    if pick:
        first = lax.axis_index(pick) == 0
        places = [(before + after, jnp.where(first, rows - 1, 0), jnp.where(first, 6, 0))]
    else:
        places = [(before, 0, 0), (after, rows - 1, 6)]
    for line, h, tap in places:
        where = pl.ds(pl.multiple_of(h * cols, cols), cols)
        add_line(joined, where, line, weights, group, at, [tap + i for i in range(3)])


def silu(x):
    return x / (1.0 + jnp.exp(-x))


def own_kernel(rows, cols, shards, pick, coords, own, enc, strip, got_a, weights, base, joined, panel):
    a, b, before, after = neighbours(rows, cols, shards, pick, enc, strip, got_a)
    joined[...] = jnp.zeros_like(joined)
    inside(rows, cols, 0, coords, own, enc, weights, None, base, joined, panel)
    add_columns(rows, cols, joined, weights, a, 0, b, 0)
    add_rows(rows, cols, pick, joined, weights, 0, before, after)


def middle_kernel(rows, cols, shards, pick, direct, coords, near, far, enc, near_strip, last_strip, near_a,
                  far_a, weights, base_in, joined_in, base, joined, panel):
    me = lax.axis_index("src")
    width = joined.shape[1]
    a, b, before, after = neighbours(rows, cols, shards, pick, enc, near_strip, near_a)
    joined[...] = joined_in[...]
    inside(rows, cols, 1, coords, near, enc, weights, base_in, base, joined, panel)
    add_columns(rows, cols, joined, weights, a, 1, b, 1)
    add_rows(rows, cols, pick, joined, weights, 1, before, after)
    here = pl.ds(pl.multiple_of(lax.div(me, 2) * width, width), width)
    base[:, here] = base[:, here] + silu(joined[0 : rows * cols, :])
    a, b, before, after = neighbours(rows, cols, shards, pick, enc, last_strip[direct:, :], far_a)
    joined[...] = jnp.zeros_like(joined)
    inside(rows, cols, 3, coords, far, enc, weights, base, base, joined, panel)
    add_columns(rows, cols, joined, weights, a, 3, b, 2)
    add_rows(rows, cols, pick, joined, weights, 2, before, after)


def last_kernel(rows, cols, coords, first, last, enc, weights, base_in, joined_in, base, joined, panel):
    joined[...] = joined_in[...]
    first = first[0 : rows * cols - last.shape[0], :]
    inside(rows, cols, 2, coords, (first, last), enc, weights, base_in, base, joined, panel)


def rim_kernel(rows, cols, shards, pick, enc, relayed, weights, base, joined_in, out, joined,
               ready, sems):
    chan, width = out.shape[1], joined.shape[1]
    last_a, b, before, after = neighbours(
        rows, cols, shards, pick, enc, relayed[rows:, :], relayed[0:rows, :]
    )
    joined[...] = joined_in[...]
    add_columns(rows, cols, joined, weights, last_a, 2, b, 3)
    add_rows(rows, cols, pick, joined, weights, 3, before, after)
    group = where_of(2, chan)[0]
    size, copies = rows * cols // PARTS, []
    for i in range(PARTS):
        some = slice(i * size, (i + 1) * size)
        added = silu(joined[some, :])
        for c, lanes in tiles(chan):
            here = group == c * LANES // width
            ready[some, lanes] = (base[some, lanes] + jnp.where(here, added, 0.0)).astype(BF16)
        copies.append(pltpu.make_async_copy(ready.at[some], out.at[some], sems.at[i]))
        copies[-1].start()
    for copy in copies:
        copy.wait()


def shape(rows, chan, dtype=BF16):
    return jax.ShapeDtypeStruct((rows, chan), dtype)


def call(kernel, ins, outs, scratch=(), cost=None, out_spec=VMEM_SPEC):
    return pl.pallas_call(
        kernel,
        out_shape=outs,
        in_specs=[VMEM_SPEC] * len(ins),
        out_specs=jax.tree.map(lambda _: out_spec, outs),
        scratch_shapes=list(scratch),
        compiler_params=pltpu.CompilerParams(vmem_limit_bytes=32 * 1024 * 1024),
        cost_estimate=cost,
    )(*ins)


def local(src_feat, coords, offsets, weights):
    _, rows, cols, chan = src_feat.shape
    pixels = rows * cols
    width = weights.shape[4]
    own = src_feat.reshape(pixels, chan)

    def across(array, k):
        return lax.ppermute(array, "src", [(i, i ^ k) for i in range(4)])

    far = across(own, 3)
    near = across(own, 1)
    rowpos = offsets[0] + jnp.arange(rows, dtype=jnp.int32)
    enc = encoding(rowpos, chan)

    line = shape(rows, chan)
    col_a, col_b, edge_rows, panel = call(
        functools.partial(columns_kernel, rows, cols),
        [own],
        [line, line, shape(2 * cols, chan), shape(pixels, chan)],
        [pltpu.VMEM((chan // LANES, pixels + cols, LANES), F32)],
    )
    place = jnp.broadcast_to(coords.astype(F32).reshape(2, 1), (2, chan))
    shards, slabs = lax.axis_size("shard"), lax.axis_size("slab")

    def swap(array, first):
        pairs = [(i, i + 1) for i in range(first, shards - 1, 2)]
        return lax.ppermute(array, "shard", pairs + [(j, i) for i, j in pairs])

    got_b, got_a = swap(col_b, 1), swap(col_a, 0)
    pick = "slab" if slabs == 2 else None
    edge = shape(cols + 8, chan)
    edges = call(
        functools.partial(edges_kernel, rows, cols, shards, pick),
        [edge_rows, got_a, got_b, enc],
        [edge] if pick else [edge, edge],
    )
    if pick:
        beyond = [lax.ppermute(edges[0], "slab", [(0, 1), (1, 0)])]
    else:
        up = [(i, i + 1) for i in range(slabs - 1)]
        beyond = [
            lax.ppermute(edges[1], "slab", up),
            lax.ppermute(edges[0], "slab", [(j, i) for i, j in up]),
        ]
    direct = rows // 8 * cols
    strip_rows = rows + len(beyond) * (cols + 8)
    strip, longer = call(
        functools.partial(strip_kernel, rows, shards),
        [got_a, got_b, enc, panel, *beyond],
        [shape(strip_rows, chan), shape(strip_rows + direct, chan)],
        cost=pl.CostEstimate(flops=2_000_000_000, bytes_accessed=0, transcendentals=0),
    )
    near_strip, last_strip = across(strip, 1), across(longer, 2)
    far, panel = lax.optimization_barrier((far, panel))
    last = across(far[direct:], 1)

    def beside(view):
        out = call(
            functools.partial(inner_kernel, rows, cols),
            [view],
            [line],
            [pltpu.VMEM((chan // LANES, pixels + cols, LANES), F32)],
        )[0]
        return swap(out, 0)


    scratch = [pltpu.VMEM((pixels, chan), BF16)]
    sums = [shape(pixels, chan, F32), shape(pixels + cols, width, F32)]
    cost = pl.CostEstimate(flops=5000000000, bytes_accessed=4_000_000, transcendentals=0)
    base, joined = call(
        functools.partial(own_kernel, rows, cols, shards, pick),
        [place, panel, enc, strip, got_a, weights[0]],
        sums,
        scratch,
        cost=cost,
    )
    near, far, base = lax.optimization_barrier((near, far, base))
    far_a, near_a = beside(far), beside(near)
    near_a, far_a, last_strip = lax.optimization_barrier((near_a, far_a, last_strip))
    near_strip, last_strip = lax.optimization_barrier((near_strip, last_strip))
    relayed = call(
        relay_kernel, [last_strip, far_a], [shape(strip_rows + rows, chan)]
    )[0]
    relayed = across(relayed, 1)
    base, joined = call(
        functools.partial(middle_kernel, rows, cols, shards, pick, direct),
        [place, near, far, enc, near_strip, last_strip, near_a, far_a, weights[0], base, joined],
        sums,
        scratch,
        cost=pl.CostEstimate(flops=0, bytes_accessed=0, transcendentals=0),
    )
    base, joined = call(
        functools.partial(last_kernel, rows, cols),
        [place, last_strip, last, enc, weights[0], base, joined],
        sums,
        scratch,
        cost=pl.CostEstimate(flops=0, bytes_accessed=0, transcendentals=0),
    )
    out = call(
        functools.partial(rim_kernel, rows, cols, shards, pick),
        [enc, relayed, weights[0], base, joined],
        [shape(pixels, chan)],
        [
            pltpu.VMEM((pixels + cols, width), F32),
            pltpu.VMEM((pixels, chan), BF16),
            pltpu.SemaphoreType.DMA((PARTS,)),
        ],
        out_spec=pl.BlockSpec(memory_space=pl.ANY),
    )[0]
    return out.reshape(1, rows, cols, chan)


def solution(mesh):
    in_specs = (
        P("src", "slab", "shard", None),
        P("src", None),
        P("slab"),
        P("src", None, None, None, None),
    )
    out_specs = P("src", "slab", "shard", None)
    return jax.shard_map(local, mesh=mesh, in_specs=in_specs, out_specs=out_specs, check_vma=False)
```

```python
import functools
import math

import jax
import jax.numpy as jnp
from jax import lax
from jax.experimental import pallas as pl
from jax.experimental.pallas import tpu as pltpu
from jax.sharding import PartitionSpec as P

BF16, F32 = jnp.bfloat16, jnp.float32
VMEM_SPEC = pl.BlockSpec(memory_space=pltpu.VMEM)
LANES = 128
PARTS = 4
BLOCKS = 4


def encoding(rowpos, chan_count):
    channel_idx = jnp.arange(chan_count, dtype=jnp.int32)
    halves = (channel_idx // 2).astype(F32)
    frequency = jnp.exp(-math.log(1000.0) * halves / (chan_count / 2))
    phases = (channel_idx % 2).astype(F32) * (math.pi / 2)
    return jnp.sin(rowpos.astype(F32)[:, None] * frequency[None, :] + phases[None, :])


def blend_weight(coords, view_index):
    vertical, across = coords[0:1, :] / 6.0, coords[1:2, :] / 6.0
    low, left = lax.div(view_index, 2) == 0, lax.rem(view_index, 2) == 0
    return jnp.where(low, 1.0 - vertical, vertical) * jnp.where(left, 1.0 - across, across)


def tiles(chan):
    return [(c, slice(c * LANES, (c + 1) * LANES)) for c in range(chan // LANES)]


def column(rows, cols, view, wide, pick_last):
    for c, lanes in tiles(view.shape[1]):
        wide[c, 0 : rows * cols, :] = view[:, lanes].astype(F32)
        first = wide[c, pl.ds(0, rows, stride=cols), :]
        last = wide[c, pl.ds(cols - 1, rows, stride=cols), :]
        yield lanes, jnp.where(pick_last, last, first), jnp.where(pick_last, first, last)


def columns_kernel(rows, cols, view, col_a, col_b, edge_rows, panel, wide):
    even = lax.rem(lax.axis_index("shard"), 2) == 0
    for lanes, a, b in column(rows, cols, view, wide, even):
        col_a[:, lanes] = a.astype(BF16)
        col_b[:, lanes] = b.astype(BF16)
    edge_rows[0:cols, :] = view[0:cols, :]
    edge_rows[cols : 2 * cols, :] = view[(rows - 1) * cols :, :]
    panel[...] = view[...]


def inner_kernel(rows, cols, view, out, wide):
    even = lax.rem(lax.axis_index("shard"), 2) == 0
    for lanes, a, _ in column(rows, cols, view, wide, even):
        out[:, lanes] = a.astype(BF16)


def pose(shards, raw, enc, is_a):
    me = lax.axis_index("shard")
    is_left = (lax.rem(me, 2) == 0) != is_a
    inside = jnp.where(is_left, me > 0, me < shards - 1)
    return jnp.where(inside, raw[...].astype(F32) + enc[...], 0.0)


def sides(a, b):
    even = lax.rem(lax.axis_index("shard"), 2) == 0
    return jnp.where(even, b, a), jnp.where(even, a, b)


def corners(left, right, at):
    fill = jnp.zeros((6, left.shape[1]), F32)
    return jnp.concatenate([left[at : at + 1], right[at : at + 1], fill], axis=0)


def edges_kernel(rows, cols, shards, pick, edge_rows, got_a, got_b, enc, *outs):
    left, right = sides(pose(shards, got_a, enc, True), pose(shards, got_b, enc, False))
    lines = []
    for i, h in ((0, 0), (1, rows - 1)):
        row = edge_rows[i * cols : (i + 1) * cols, :].astype(F32) + enc[h : h + 1, :]
        lines.append(jnp.concatenate([row, corners(left, right, h)], axis=0))
    if pick:
        outs[0][...] = jnp.where(lax.axis_index(pick) == 0, lines[1], lines[0]).astype(BF16)
    else:
        outs[0][...] = lines[0].astype(BF16)
        outs[1][...] = lines[1].astype(BF16)


def strip_kernel(rows, shards, got_a, got_b, enc, panel, *refs):
    *beyond, out, longer = refs
    at = rows
    out[0:rows, :] = pose(shards, got_b, enc, False).astype(BF16)
    for ref in beyond:
        out[at : at + ref.shape[0], :] = ref[...]
        at += ref.shape[0]
    size = longer.shape[0] - at
    longer[0:size, :] = panel[0:size, :]
    longer[size:, :] = out[...]


def relay_kernel(strip, far_a, out):
    rows = far_a.shape[0]
    out[0:rows, :] = far_a[...]
    out[rows:, :] = strip[strip.shape[0] - (out.shape[0] - rows) :, :]


def neighbours(rows, cols, shards, pick, enc, strip, raw_a):
    extra = cols + 8
    size = extra if pick else 2 * extra
    lines = strip[rows : rows + size, :].astype(F32)
    if pick:
        first = lax.axis_index(pick) == 0
        zero = jnp.zeros_like(lines)
        both = jnp.where(first, zero, lines), jnp.where(first, lines, zero)
    else:
        both = lines[0:extra], lines[extra:]
    before, after = (
        jnp.concatenate([x[cols : cols + 1], x[0:cols], x[cols + 1 : cols + 2]], axis=0) for x in both
    )
    posed_a = pose(shards, raw_a, enc, True).astype(BF16).astype(F32)
    return posed_a, strip[0:rows, :].astype(F32), before, after


def where_of(k, chan):
    index = jnp.bitwise_xor(lax.axis_index("src"), k)
    return lax.div(index, 2), pl.multiple_of(lax.rem(index, 2) * chan, chan)


def inside(rows, cols, k, coords, view, enc, weights, base_in, base, joined, panel):
    weight = blend_weight(coords, jnp.bitwise_xor(lax.axis_index("src"), k))
    chan, width = panel.shape[1], joined.shape[1]
    pixels = rows * cols
    views = view if isinstance(view, tuple) else (view,)
    lines = [part[i : i + cols, :] for part in views for i in range(0, part.shape[0], cols)]
    for h, line in enumerate(lines):
        here = slice(h * cols, (h + 1) * cols)
        posed = (line.astype(F32) + enc[h : h + 1, :]).astype(BF16)
        part = weight * posed.astype(F32)
        base[here, :] = part if base_in is None else base_in[here, :] + part
        panel[here, :] = posed
    group, at = where_of(k, chan)
    kernel = jnp.concatenate(
        [weights[group, 3 * a + b, pl.ds(at, chan), :] for b in range(3) for a in range(3)], axis=1
    )
    size = pixels // BLOCKS
    taps = jnp.concatenate(
        [
            jnp.dot(panel[i * size : (i + 1) * size, :], kernel, preferred_element_type=F32)
            for i in range(BLOCKS)
        ],
        axis=0,
    )
    column = lax.rem(lax.broadcasted_iota(jnp.int32, (pixels, width), 0), cols)
    zero = jnp.zeros((cols, width), F32)
    total = joined[0:pixels, :]
    for b in (1, 0, 2):
        up, level, down = (taps[:, (3 * b + a) * width : (3 * b + a + 1) * width] for a in range(3))
        part = level + jnp.concatenate([zero, up[: pixels - cols]], axis=0)
        part = part + jnp.concatenate([down[cols:], zero], axis=0)
        if b == 0:
            part = jnp.where(column == 0, 0.0, pltpu.roll(part, 1, 0))
        if b == 2:
            part = jnp.where(column == cols - 1, 0.0, pltpu.roll(part, pixels - 1, 0))
        total = total + part
    joined[0:pixels, :] = total


def add_line(joined, where, line, weights, group, at, taps):
    chan, count = line.shape[1], line.shape[0] - 2
    wide = jnp.concatenate([line[i : i + count] for i in range(3)], axis=1).astype(BF16)
    kernel = jnp.concatenate([weights[group, tap, pl.ds(at, chan), :] for tap in taps], axis=0)
    joined[where, :] += jnp.dot(wide, kernel, preferred_element_type=F32)


def add_columns(rows, cols, joined, weights, a, a_view, b, b_view):
    even = lax.rem(lax.axis_index("shard"), 2) == 0
    chan = a.shape[1]
    group, at_a = where_of(a_view, chan)
    at_b = where_of(b_view, chan)[1]
    zero = jnp.zeros((1, chan), F32)
    left, right = sides(a, b)
    at_left = pl.multiple_of(jnp.where(even, at_b, at_a), chan)
    at_right = pl.multiple_of(jnp.where(even, at_a, at_b), chan)
    for side, tap, start, at in ((left, 0, 0, at_left), (right, 2, cols - 1, at_right)):
        line = jnp.concatenate([zero, side, zero], axis=0)
        where = pl.ds(start, rows, stride=cols)
        add_line(joined, where, line, weights, group, at, [3 * i + tap for i in range(3)])


def add_rows(rows, cols, pick, joined, weights, view, before, after):
    group, at = where_of(view, before.shape[1])
    if pick:
        first = lax.axis_index(pick) == 0
        places = [(before + after, jnp.where(first, rows - 1, 0), jnp.where(first, 6, 0))]
    else:
        places = [(before, 0, 0), (after, rows - 1, 6)]
    for line, h, tap in places:
        where = pl.ds(pl.multiple_of(h * cols, cols), cols)
        add_line(joined, where, line, weights, group, at, [tap + i for i in range(3)])


def silu(x):
    return x / (1.0 + jnp.exp(-x))


def own_kernel(rows, cols, shards, pick, coords, own, enc, strip, got_a, weights, base, joined, panel):
    a, b, before, after = neighbours(rows, cols, shards, pick, enc, strip, got_a)
    joined[...] = jnp.zeros_like(joined)
    inside(rows, cols, 0, coords, own, enc, weights, None, base, joined, panel)
    add_columns(rows, cols, joined, weights, a, 0, b, 0)
    add_rows(rows, cols, pick, joined, weights, 0, before, after)


def middle_kernel(rows, cols, shards, pick, direct, coords, near, far, enc, near_strip, last_strip, near_a,
                  far_a, weights, base_in, joined_in, base, joined, panel):
    me = lax.axis_index("src")
    width = joined.shape[1]
    a, b, before, after = neighbours(rows, cols, shards, pick, enc, near_strip, near_a)
    joined[...] = joined_in[...]
    inside(rows, cols, 1, coords, near, enc, weights, base_in, base, joined, panel)
    add_columns(rows, cols, joined, weights, a, 1, b, 1)
    add_rows(rows, cols, pick, joined, weights, 1, before, after)
    here = pl.ds(pl.multiple_of(lax.div(me, 2) * width, width), width)
    base[:, here] = base[:, here] + silu(joined[0 : rows * cols, :])
    a, b, before, after = neighbours(rows, cols, shards, pick, enc, last_strip[direct:, :], far_a)
    joined[...] = jnp.zeros_like(joined)
    inside(rows, cols, 3, coords, far, enc, weights, base, base, joined, panel)
    add_columns(rows, cols, joined, weights, a, 3, b, 2)
    add_rows(rows, cols, pick, joined, weights, 2, before, after)


def last_kernel(rows, cols, coords, first, last, enc, weights, base_in, joined_in, base, joined, panel):
    joined[...] = joined_in[...]
    first = first[0 : rows * cols - last.shape[0], :]
    inside(rows, cols, 2, coords, (first, last), enc, weights, base_in, base, joined, panel)


def rim_kernel(rows, cols, shards, pick, enc, relayed, weights, base, joined_in, out, joined,
               ready, sems):
    chan, width = out.shape[1], joined.shape[1]
    last_a, b, before, after = neighbours(
        rows, cols, shards, pick, enc, relayed[rows:, :], relayed[0:rows, :]
    )
    joined[...] = joined_in[...]
    add_columns(rows, cols, joined, weights, last_a, 2, b, 3)
    add_rows(rows, cols, pick, joined, weights, 3, before, after)
    group = where_of(2, chan)[0]
    size, copies = rows * cols // PARTS, []
    for i in range(PARTS):
        some = slice(i * size, (i + 1) * size)
        added = silu(joined[some, :])
        for c, lanes in tiles(chan):
            here = group == c * LANES // width
            ready[some, lanes] = (base[some, lanes] + jnp.where(here, added, 0.0)).astype(BF16)
        copies.append(pltpu.make_async_copy(ready.at[some], out.at[some], sems.at[i]))
        copies[-1].start()
    for copy in copies:
        copy.wait()


def shape(rows, chan, dtype=BF16):
    return jax.ShapeDtypeStruct((rows, chan), dtype)


def call(kernel, ins, outs, scratch=(), cost=None, out_spec=VMEM_SPEC):
    return pl.pallas_call(
        kernel,
        out_shape=outs,
        in_specs=[VMEM_SPEC] * len(ins),
        out_specs=jax.tree.map(lambda _: out_spec, outs),
        scratch_shapes=list(scratch),
        compiler_params=pltpu.CompilerParams(vmem_limit_bytes=32 * 1024 * 1024),
        cost_estimate=cost,
    )(*ins)


def local(src_feat, coords, offsets, weights):
    _, rows, cols, chan = src_feat.shape
    pixels = rows * cols
    width = weights.shape[4]
    own = src_feat.reshape(pixels, chan)

    def across(array, k):
        return lax.ppermute(array, "src", [(i, i ^ k) for i in range(4)])

    far = across(own, 3)
    near = across(own, 1)
    rowpos = offsets[0] + jnp.arange(rows, dtype=jnp.int32)
    enc = encoding(rowpos, chan)

    line = shape(rows, chan)
    col_a, col_b, edge_rows, panel = call(
        functools.partial(columns_kernel, rows, cols),
        [own],
        [line, line, shape(2 * cols, chan), shape(pixels, chan)],
        [pltpu.VMEM((chan // LANES, pixels + cols, LANES), F32)],
    )
    place = jnp.broadcast_to(coords.astype(F32).reshape(2, 1), (2, chan))
    shards, slabs = lax.axis_size("shard"), lax.axis_size("slab")

    def swap(array, first):
        pairs = [(i, i + 1) for i in range(first, shards - 1, 2)]
        return lax.ppermute(array, "shard", pairs + [(j, i) for i, j in pairs])

    got_b, got_a = swap(col_b, 1), swap(col_a, 0)
    pick = "slab" if slabs == 2 else None
    edge = shape(cols + 8, chan)
    edges = call(
        functools.partial(edges_kernel, rows, cols, shards, pick),
        [edge_rows, got_a, got_b, enc],
        [edge] if pick else [edge, edge],
    )
    if pick:
        beyond = [lax.ppermute(edges[0], "slab", [(0, 1), (1, 0)])]
    else:
        up = [(i, i + 1) for i in range(slabs - 1)]
        beyond = [
            lax.ppermute(edges[1], "slab", up),
            lax.ppermute(edges[0], "slab", [(j, i) for i, j in up]),
        ]
    direct = rows // 8 * cols
    strip_rows = rows + len(beyond) * (cols + 8)
    strip, longer = call(
        functools.partial(strip_kernel, rows, shards),
        [got_a, got_b, enc, panel, *beyond],
        [shape(strip_rows, chan), shape(strip_rows + direct, chan)],
        cost=pl.CostEstimate(flops=2_000_000_000, bytes_accessed=0, transcendentals=0),
    )
    near_strip, last_strip = across(strip, 1), across(longer, 2)
    far, panel = lax.optimization_barrier((far, panel))
    last = across(far[direct:], 1)

    def beside(view):
        out = call(
            functools.partial(inner_kernel, rows, cols),
            [view],
            [line],
            [pltpu.VMEM((chan // LANES, pixels + cols, LANES), F32)],
        )[0]
        return swap(out, 0)


    scratch = [pltpu.VMEM((pixels, chan), BF16)]
    sums = [shape(pixels, chan, F32), shape(pixels + cols, width, F32)]
    cost = pl.CostEstimate(flops=5000000000, bytes_accessed=4_000_000, transcendentals=0)
    base, joined = call(
        functools.partial(own_kernel, rows, cols, shards, pick),
        [place, panel, enc, strip, got_a, weights[0]],
        sums,
        scratch,
        cost=cost,
    )
    near, far, base = lax.optimization_barrier((near, far, base))
    far_a, near_a = beside(far), beside(near)
    near_a, far_a, last_strip = lax.optimization_barrier((near_a, far_a, last_strip))
    near_strip, last_strip = lax.optimization_barrier((near_strip, last_strip))
    relayed = call(
        relay_kernel, [last_strip, far_a], [shape(strip_rows + rows, chan)]
    )[0]
    relayed = across(relayed, 1)
    base, joined = call(
        functools.partial(middle_kernel, rows, cols, shards, pick, direct),
        [place, near, far, enc, near_strip, last_strip, near_a, far_a, weights[0], base, joined],
        sums,
        scratch,
        cost=pl.CostEstimate(flops=0, bytes_accessed=0, transcendentals=0),
    )
    base, joined = call(
        functools.partial(last_kernel, rows, cols),
        [place, last_strip, last, enc, weights[0], base, joined],
        sums,
        scratch,
        cost=pl.CostEstimate(flops=0, bytes_accessed=0, transcendentals=0),
    )
    out = call(
        functools.partial(rim_kernel, rows, cols, shards, pick),
        [enc, relayed, weights[0], base, joined],
        [shape(pixels, chan)],
        [
            pltpu.VMEM((pixels + cols, width), F32),
            pltpu.VMEM((pixels, chan), BF16),
            pltpu.SemaphoreType.DMA((PARTS,)),
        ],
        out_spec=pl.BlockSpec(memory_space=pl.ANY),
    )[0]
    return out.reshape(1, rows, cols, chan)


def solution(mesh):
    in_specs = (
        P("src", "slab", "shard", None),
        P("src", None),
        P("slab"),
        P("src", None, None, None, None),
    )
    out_specs = P("src", "slab", "shard", None)
    return jax.shard_map(local, mesh=mesh, in_specs=in_specs, out_specs=out_specs, check_vma=False)
```

```python
import functools
import math

import jax
import jax.numpy as jnp
from jax import lax
from jax.experimental import pallas as pl
from jax.experimental.pallas import tpu as pltpu
from jax.sharding import PartitionSpec as P

BF16, F32 = jnp.bfloat16, jnp.float32
VMEM_SPEC = pl.BlockSpec(memory_space=pltpu.VMEM)
LANES = 128
PARTS = 2
BLOCKS = 2


def encoding(rowpos, chan_count):
    channel_idx = jnp.arange(chan_count, dtype=jnp.int32)
    halves = (channel_idx // 2).astype(F32)
    frequency = jnp.exp(-math.log(1000.0) * halves / (chan_count / 2))
    phases = (channel_idx % 2).astype(F32) * (math.pi / 2)
    return jnp.sin(rowpos.astype(F32)[:, None] * frequency[None, :] + phases[None, :])


def blend_weight(coords, view_index):
    vertical, across = coords[0:1, :] / 6.0, coords[1:2, :] / 6.0
    low, left = lax.div(view_index, 2) == 0, lax.rem(view_index, 2) == 0
    return jnp.where(low, 1.0 - vertical, vertical) * jnp.where(left, 1.0 - across, across)


def tiles(chan):
    return [(c, slice(c * LANES, (c + 1) * LANES)) for c in range(chan // LANES)]


def column(rows, cols, view, wide, pick_last):
    for c, lanes in tiles(view.shape[1]):
        wide[c, 0 : rows * cols, :] = view[:, lanes].astype(F32)
        first = wide[c, pl.ds(0, rows, stride=cols), :]
        last = wide[c, pl.ds(cols - 1, rows, stride=cols), :]
        yield lanes, jnp.where(pick_last, last, first), jnp.where(pick_last, first, last)


def columns_kernel(rows, cols, view, col_a, col_b, edge_rows, panel, wide):
    even = lax.rem(lax.axis_index("shard"), 2) == 0
    for lanes, a, b in column(rows, cols, view, wide, even):
        col_a[:, lanes] = a.astype(BF16)
        col_b[:, lanes] = b.astype(BF16)
    edge_rows[0:cols, :] = view[0:cols, :]
    edge_rows[cols : 2 * cols, :] = view[(rows - 1) * cols :, :]
    panel[...] = view[...]


def inner_kernel(rows, cols, view, out, wide):
    even = lax.rem(lax.axis_index("shard"), 2) == 0
    for lanes, a, _ in column(rows, cols, view, wide, even):
        out[:, lanes] = a.astype(BF16)


def pose(shards, raw, enc, is_a):
    me = lax.axis_index("shard")
    is_left = (lax.rem(me, 2) == 0) != is_a
    inside = jnp.where(is_left, me > 0, me < shards - 1)
    return jnp.where(inside, raw[...].astype(F32) + enc[...], 0.0)


def sides(a, b):
    even = lax.rem(lax.axis_index("shard"), 2) == 0
    return jnp.where(even, b, a), jnp.where(even, a, b)


def corners(left, right, at):
    fill = jnp.zeros((6, left.shape[1]), F32)
    return jnp.concatenate([left[at : at + 1], right[at : at + 1], fill], axis=0)


def edges_kernel(rows, cols, shards, pick, edge_rows, got_a, got_b, enc, *outs):
    left, right = sides(pose(shards, got_a, enc, True), pose(shards, got_b, enc, False))
    lines = []
    for i, h in ((0, 0), (1, rows - 1)):
        row = edge_rows[i * cols : (i + 1) * cols, :].astype(F32) + enc[h : h + 1, :]
        lines.append(jnp.concatenate([row, corners(left, right, h)], axis=0))
    if pick:
        outs[0][...] = jnp.where(lax.axis_index(pick) == 0, lines[1], lines[0]).astype(BF16)
    else:
        outs[0][...] = lines[0].astype(BF16)
        outs[1][...] = lines[1].astype(BF16)


def strip_kernel(rows, shards, got_a, got_b, enc, panel, *refs):
    *beyond, out, longer = refs
    at = rows
    out[0:rows, :] = pose(shards, got_b, enc, False).astype(BF16)
    for ref in beyond:
        out[at : at + ref.shape[0], :] = ref[...]
        at += ref.shape[0]
    size = longer.shape[0] - at
    longer[0:size, :] = panel[0:size, :]
    longer[size:, :] = out[...]


def relay_kernel(strip, far_a, out):
    rows = far_a.shape[0]
    out[0:rows, :] = far_a[...]
    out[rows:, :] = strip[strip.shape[0] - (out.shape[0] - rows) :, :]


def neighbours(rows, cols, shards, pick, enc, strip, raw_a):
    extra = cols + 8
    size = extra if pick else 2 * extra
    lines = strip[rows : rows + size, :].astype(F32)
    if pick:
        first = lax.axis_index(pick) == 0
        zero = jnp.zeros_like(lines)
        both = jnp.where(first, zero, lines), jnp.where(first, lines, zero)
    else:
        both = lines[0:extra], lines[extra:]
    before, after = (
        jnp.concatenate([x[cols : cols + 1], x[0:cols], x[cols + 1 : cols + 2]], axis=0) for x in both
    )
    posed_a = pose(shards, raw_a, enc, True).astype(BF16).astype(F32)
    return posed_a, strip[0:rows, :].astype(F32), before, after


def where_of(k, chan):
    index = jnp.bitwise_xor(lax.axis_index("src"), k)
    return lax.div(index, 2), pl.multiple_of(lax.rem(index, 2) * chan, chan)


def inside(rows, cols, k, coords, view, enc, weights, base_in, base, joined, panel):
    weight = blend_weight(coords, jnp.bitwise_xor(lax.axis_index("src"), k))
    chan, width = panel.shape[1], joined.shape[1]
    pixels = rows * cols
    views = view if isinstance(view, tuple) else (view,)
    lines = [part[i : i + cols, :] for part in views for i in range(0, part.shape[0], cols)]
    for h, line in enumerate(lines):
        here = slice(h * cols, (h + 1) * cols)
        posed = (line.astype(F32) + enc[h : h + 1, :]).astype(BF16)
        part = weight * posed.astype(F32)
        base[here, :] = part if base_in is None else base_in[here, :] + part
        panel[here, :] = posed
    group, at = where_of(k, chan)
    kernel = jnp.concatenate(
        [weights[group, 3 * a + b, pl.ds(at, chan), :] for b in range(3) for a in range(3)], axis=1
    )
    size = pixels // BLOCKS
    taps = jnp.concatenate(
        [
            jnp.dot(panel[i * size : (i + 1) * size, :], kernel, preferred_element_type=F32)
            for i in range(BLOCKS)
        ],
        axis=0,
    )
    column = lax.rem(lax.broadcasted_iota(jnp.int32, (pixels, width), 0), cols)
    zero = jnp.zeros((cols, width), F32)
    total = joined[0:pixels, :]
    for b in (1, 0, 2):
        up, level, down = (taps[:, (3 * b + a) * width : (3 * b + a + 1) * width] for a in range(3))
        part = level + jnp.concatenate([zero, up[: pixels - cols]], axis=0)
        part = part + jnp.concatenate([down[cols:], zero], axis=0)
        if b == 0:
            part = jnp.where(column == 0, 0.0, pltpu.roll(part, 1, 0))
        if b == 2:
            part = jnp.where(column == cols - 1, 0.0, pltpu.roll(part, pixels - 1, 0))
        total = total + part
    joined[0:pixels, :] = total


def add_line(joined, where, line, weights, group, at, taps):
    chan, count = line.shape[1], line.shape[0] - 2
    wide = jnp.concatenate([line[i : i + count] for i in range(3)], axis=1).astype(BF16)
    kernel = jnp.concatenate([weights[group, tap, pl.ds(at, chan), :] for tap in taps], axis=0)
    joined[where, :] += jnp.dot(wide, kernel, preferred_element_type=F32)


def add_columns(rows, cols, joined, weights, a, a_view, b, b_view):
    even = lax.rem(lax.axis_index("shard"), 2) == 0
    chan = a.shape[1]
    group, at_a = where_of(a_view, chan)
    at_b = where_of(b_view, chan)[1]
    zero = jnp.zeros((1, chan), F32)
    left, right = sides(a, b)
    at_left = pl.multiple_of(jnp.where(even, at_b, at_a), chan)
    at_right = pl.multiple_of(jnp.where(even, at_a, at_b), chan)
    for side, tap, start, at in ((left, 0, 0, at_left), (right, 2, cols - 1, at_right)):
        line = jnp.concatenate([zero, side, zero], axis=0)
        where = pl.ds(start, rows, stride=cols)
        add_line(joined, where, line, weights, group, at, [3 * i + tap for i in range(3)])


def add_rows(rows, cols, pick, joined, weights, view, before, after):
    group, at = where_of(view, before.shape[1])
    if pick:
        first = lax.axis_index(pick) == 0
        places = [(before + after, jnp.where(first, rows - 1, 0), jnp.where(first, 6, 0))]
    else:
        places = [(before, 0, 0), (after, rows - 1, 6)]
    for line, h, tap in places:
        where = pl.ds(pl.multiple_of(h * cols, cols), cols)
        add_line(joined, where, line, weights, group, at, [tap + i for i in range(3)])


def silu(x):
    return x / (1.0 + jnp.exp(-x))


def own_kernel(rows, cols, shards, pick, coords, own, enc, strip, got_a, weights, base, joined, panel):
    a, b, before, after = neighbours(rows, cols, shards, pick, enc, strip, got_a)
    joined[...] = jnp.zeros_like(joined)
    inside(rows, cols, 0, coords, own, enc, weights, None, base, joined, panel)
    add_columns(rows, cols, joined, weights, a, 0, b, 0)
    add_rows(rows, cols, pick, joined, weights, 0, before, after)


def middle_kernel(rows, cols, shards, pick, direct, coords, near, far, enc, near_strip, last_strip, near_a,
                  far_a, weights, base_in, joined_in, base, joined, panel):
    me = lax.axis_index("src")
    width = joined.shape[1]
    a, b, before, after = neighbours(rows, cols, shards, pick, enc, near_strip, near_a)
    joined[...] = joined_in[...]
    inside(rows, cols, 1, coords, near, enc, weights, base_in, base, joined, panel)
    add_columns(rows, cols, joined, weights, a, 1, b, 1)
    add_rows(rows, cols, pick, joined, weights, 1, before, after)
    here = pl.ds(pl.multiple_of(lax.div(me, 2) * width, width), width)
    base[:, here] = base[:, here] + silu(joined[0 : rows * cols, :])
    a, b, before, after = neighbours(rows, cols, shards, pick, enc, last_strip[direct:, :], far_a)
    joined[...] = jnp.zeros_like(joined)
    inside(rows, cols, 3, coords, far, enc, weights, base, base, joined, panel)
    add_columns(rows, cols, joined, weights, a, 3, b, 2)
    add_rows(rows, cols, pick, joined, weights, 2, before, after)


def last_kernel(rows, cols, coords, first, last, enc, weights, base_in, joined_in, base, joined, panel):
    joined[...] = joined_in[...]
    first = first[0 : rows * cols - last.shape[0], :]
    inside(rows, cols, 2, coords, (first, last), enc, weights, base_in, base, joined, panel)


def rim_kernel(rows, cols, shards, pick, enc, relayed, weights, base, joined_in, out, joined,
               ready, sems):
    chan, width = out.shape[1], joined.shape[1]
    last_a, b, before, after = neighbours(
        rows, cols, shards, pick, enc, relayed[rows:, :], relayed[0:rows, :]
    )
    joined[...] = joined_in[...]
    add_columns(rows, cols, joined, weights, last_a, 2, b, 3)
    add_rows(rows, cols, pick, joined, weights, 3, before, after)
    group = where_of(2, chan)[0]
    size, copies = rows * cols // PARTS, []
    for i in range(PARTS):
        some = slice(i * size, (i + 1) * size)
        added = silu(joined[some, :])
        for c, lanes in tiles(chan):
            here = group == c * LANES // width
            ready[some, lanes] = (base[some, lanes] + jnp.where(here, added, 0.0)).astype(BF16)
        copies.append(pltpu.make_async_copy(ready.at[some], out.at[some], sems.at[i]))
        copies[-1].start()
    for copy in copies:
        copy.wait()


def shape(rows, chan, dtype=BF16):
    return jax.ShapeDtypeStruct((rows, chan), dtype)


def call(kernel, ins, outs, scratch=(), cost=None, out_spec=VMEM_SPEC):
    return pl.pallas_call(
        kernel,
        out_shape=outs,
        in_specs=[VMEM_SPEC] * len(ins),
        out_specs=jax.tree.map(lambda _: out_spec, outs),
        scratch_shapes=list(scratch),
        compiler_params=pltpu.CompilerParams(vmem_limit_bytes=32 * 1024 * 1024),
        cost_estimate=cost,
    )(*ins)


def local(src_feat, coords, offsets, weights):
    _, rows, cols, chan = src_feat.shape
    pixels = rows * cols
    width = weights.shape[4]
    own = src_feat.reshape(pixels, chan)

    def across(array, k):
        return lax.ppermute(array, "src", [(i, i ^ k) for i in range(4)])

    far = across(own, 3)
    near = across(own, 1)
    rowpos = offsets[0] + jnp.arange(rows, dtype=jnp.int32)
    enc = encoding(rowpos, chan)

    line = shape(rows, chan)
    col_a, col_b, edge_rows, panel = call(
        functools.partial(columns_kernel, rows, cols),
        [own],
        [line, line, shape(2 * cols, chan), shape(pixels, chan)],
        [pltpu.VMEM((chan // LANES, pixels + cols, LANES), F32)],
    )
    place = jnp.broadcast_to(coords.astype(F32).reshape(2, 1), (2, chan))
    shards, slabs = lax.axis_size("shard"), lax.axis_size("slab")

    def swap(array, first):
        pairs = [(i, i + 1) for i in range(first, shards - 1, 2)]
        return lax.ppermute(array, "shard", pairs + [(j, i) for i, j in pairs])

    got_b, got_a = swap(col_b, 1), swap(col_a, 0)
    pick = "slab" if slabs == 2 else None
    edge = shape(cols + 8, chan)
    edges = call(
        functools.partial(edges_kernel, rows, cols, shards, pick),
        [edge_rows, got_a, got_b, enc],
        [edge] if pick else [edge, edge],
    )
    if pick:
        beyond = [lax.ppermute(edges[0], "slab", [(0, 1), (1, 0)])]
    else:
        up = [(i, i + 1) for i in range(slabs - 1)]
        beyond = [
            lax.ppermute(edges[1], "slab", up),
            lax.ppermute(edges[0], "slab", [(j, i) for i, j in up]),
        ]
    direct = rows // 8 * cols
    strip_rows = rows + len(beyond) * (cols + 8)
    strip, longer = call(
        functools.partial(strip_kernel, rows, shards),
        [got_a, got_b, enc, panel, *beyond],
        [shape(strip_rows, chan), shape(strip_rows + direct, chan)],
        cost=pl.CostEstimate(flops=2_000_000_000, bytes_accessed=0, transcendentals=0),
    )
    near_strip, last_strip = across(strip, 1), across(longer, 2)
    far, panel = lax.optimization_barrier((far, panel))
    last = across(far[direct:], 1)

    def beside(view):
        out = call(
            functools.partial(inner_kernel, rows, cols),
            [view],
            [line],
            [pltpu.VMEM((chan // LANES, pixels + cols, LANES), F32)],
        )[0]
        return swap(out, 0)


    scratch = [pltpu.VMEM((pixels, chan), BF16)]
    sums = [shape(pixels, chan, F32), shape(pixels + cols, width, F32)]
    cost = pl.CostEstimate(flops=5000000000, bytes_accessed=4_000_000, transcendentals=0)
    base, joined = call(
        functools.partial(own_kernel, rows, cols, shards, pick),
        [place, panel, enc, strip, got_a, weights[0]],
        sums,
        scratch,
        cost=cost,
    )
    near, far, base = lax.optimization_barrier((near, far, base))
    far_a, near_a = beside(far), beside(near)
    near_a, far_a, last_strip = lax.optimization_barrier((near_a, far_a, last_strip))
    near_strip, last_strip = lax.optimization_barrier((near_strip, last_strip))
    relayed = call(
        relay_kernel, [last_strip, far_a], [shape(strip_rows + rows, chan)]
    )[0]
    relayed = across(relayed, 1)
    base, joined = call(
        functools.partial(middle_kernel, rows, cols, shards, pick, direct),
        [place, near, far, enc, near_strip, last_strip, near_a, far_a, weights[0], base, joined],
        sums,
        scratch,
        cost=pl.CostEstimate(flops=0, bytes_accessed=0, transcendentals=0),
    )
    base, joined = call(
        functools.partial(last_kernel, rows, cols),
        [place, last_strip, last, enc, weights[0], base, joined],
        sums,
        scratch,
        cost=pl.CostEstimate(flops=0, bytes_accessed=0, transcendentals=0),
    )
    out = call(
        functools.partial(rim_kernel, rows, cols, shards, pick),
        [enc, relayed, weights[0], base, joined],
        [shape(pixels, chan)],
        [
            pltpu.VMEM((pixels + cols, width), F32),
            pltpu.VMEM((pixels, chan), BF16),
            pltpu.SemaphoreType.DMA((PARTS,)),
        ],
        out_spec=pl.BlockSpec(memory_space=pl.ANY),
    )[0]
    return out.reshape(1, rows, cols, chan)


def solution(mesh):
    in_specs = (
        P("src", "slab", "shard", None),
        P("src", None),
        P("slab"),
        P("src", None, None, None, None),
    )
    out_specs = P("src", "slab", "shard", None)
    return jax.shard_map(local, mesh=mesh, in_specs=in_specs, out_specs=out_specs, check_vma=False)
```
